32 devices in a mesh: ctx: 8 (over z, x), fsdp: 4 (over y, core).
Axes of the slice: x: 2, y: 2, z: 4, core: 2. Of those that a mesh axis runs over, the one named last changes fastest.
Arguments:
- inputs: bfloat16 [8, 512, 768], P('fsdp', 'ctx'), may hold values from -6 to 6
- w_qkv: bfloat16 [2, 3, 768, 768], P(None, None, ('ctx', 'fsdp')), may hold values from -0.21650635 to 0.21650635
- w_out: bfloat16 [2, 768, 768], P(None, ('ctx', 'fsdp')), may hold values from -4.8989795 to 4.8989795
- w_up: bfloat16 [2, 768, 3072], P(None, ('ctx', 'fsdp')), may hold values from -0.21875 to 0.21875
- w_down: bfloat16 [2, 3072, 768], P(None, ('ctx', 'fsdp')), may hold values from -0.109375 to 0.109375
- biases: bfloat16 [2, 3, 768], P(None, None, ('ctx', 'fsdp')), may hold values from -1.75 to 1.75
- value_bias: bfloat16 [2, 768], P(None, ('ctx', 'fsdp')), may hold values from -0.078125 to 0.078125
- up_bias: bfloat16 [2, 3072], P(None, ('ctx', 'fsdp')), may hold values from -1.75 to 1.75
- gains: bfloat16 [2, 2, 768], P(None, None, ('ctx', 'fsdp')), may hold values from 0.5 to 1.5
- shifts: bfloat16 [2, 2, 768], P(None, None, ('ctx', 'fsdp')), may hold values from -1.75 to 1.75
- cotangent: bfloat16 [8, 512, 768], P('fsdp', 'ctx'), may hold values from -8 to 8
Outputs:
- output: bfloat16 [8, 512, 768], P('fsdp', 'ctx')
- grad_inputs: bfloat16 [8, 512, 768], P('fsdp', 'ctx')
- grad_w_qkv: float32 [2, 3, 768, 768], P(None, None, ('ctx', 'fsdp'))
- grad_w_out: float32 [2, 768, 768], P(None, ('ctx', 'fsdp'))
- grad_w_up: float32 [2, 768, 3072], P(None, ('ctx', 'fsdp'))
- grad_w_down: float32 [2, 3072, 768], P(None, ('ctx', 'fsdp'))
- grad_biases: float32 [2, 3, 768], P(None, None, ('ctx', 'fsdp'))
- grad_value_bias: float32 [2, 768], P(None, ('ctx', 'fsdp'))
- grad_up_bias: float32 [2, 3072], P(None, ('ctx', 'fsdp'))
- grad_gains: float32 [2, 2, 768], P(None, None, ('ctx', 'fsdp'))
- grad_shifts: float32 [2, 2, 768], P(None, None, ('ctx', 'fsdp'))
The draws below stay inside these ranges and needn't reach their ends.
All inputs are finite; a program needn't handle non-finite values.
Results may differ from the reference program's by a relative error of at most 0.024.
Values may be sent and summed in bfloat16 or wider, within the bound.
A program may use at most 320 MiB of HBM per device.

```python
import jax
import jax.numpy as jnp
from jax import lax

D = 768
HEADS = 12
HEAD_DIM = 64
FF = 3072
LAYERS = 2
TOK_DEV = 64
LENGTH = 512
SEQS = 8
N_CTX = 8


def spread_values(key, shape, deviation):
    return jnp.clip(jax.random.normal(key, shape, jnp.float32), -6.0, 6.0) * deviation


def draw_inputs(key, part):
    key = jax.random.fold_in(key, 11)
    return spread_values(key, (SEQS, LENGTH, D), 1.0).astype(jnp.bfloat16)


def draw_w_qkv(key, part):
    key = jax.random.fold_in(key, 12)
    return spread_values(key, (LAYERS, 3, D, D), D ** (-0.5)).astype(jnp.bfloat16)


def draw_w_out(key, part):
    key = jax.random.fold_in(key, 13)
    return spread_values(key, (LAYERS, D, D), LENGTH ** 0.5 * D ** (-0.5)).astype(jnp.bfloat16)


def raised(result, own_key, source, target, blocks, factor):
    owner, partner = [(jnp.arange(result.shape[position]) // (result.shape[position] // blocks)).reshape([-1 if axis == position else 1 for axis in range(result.ndim)]) for position in (source, target)]
    chosen = jax.random.permutation(own_key, blocks)[partner]
    strong = (owner == chosen) | (owner == (partner + blocks // 2) % blocks)
    return jnp.where(strong, factor * result, result)


def block_levels(stream_key, dims, cuts, least, largest):
    factor_of, own = 1.0, jax.random.fold_in(stream_key, 6)
    for axis_at, blocks in cuts:
        heights = jnp.exp(jax.random.uniform(jax.random.fold_in(own, axis_at), (blocks,), jnp.float32, least / len(cuts), largest / len(cuts)))
        factor_of = factor_of * jnp.repeat(heights, dims[axis_at] // blocks).reshape([-1 if axis == axis_at else 1 for axis in range(len(dims))])
    return factor_of


def bell_draw(stream_key, shape, width, reach, split=(), held_as=jnp.bfloat16):
    drawn = width * jax.random.normal(stream_key, shape, jnp.float32)
    if split:
        drawn = drawn * block_levels(stream_key, shape, split, -0.22, 0.18)
    return jnp.clip(drawn, -reach, reach).astype(held_as)


def heavy_noise(own_key, dims, scale, reach, shards, heavy, dtype=jnp.bfloat16):
    values = scale * jax.random.normal(own_key, dims, jnp.float32)
    if shards:
        values = values * block_levels(own_key, dims, shards, -0.22, 0.18)
    return jnp.clip(raised(values, jax.random.fold_in(own_key, 3), *heavy), -reach, reach).astype(dtype)


def setup_inputs(seed: int = 0) -> dict:
    splits = jax.random.split(jax.random.key(seed), 12)
    inputs = draw_inputs(jax.random.fold_in(splits[11], 71), 0)
    w_qkv = draw_w_qkv(jax.random.fold_in(splits[11], 71), 0)
    w_out = draw_w_out(jax.random.fold_in(splits[11], 71), 0)
    w_up = bell_draw(splits[3], (LAYERS, D, FF), D ** -0.5, 0.21875, ((1, 32),))
    w_down = bell_draw(splits[4], (LAYERS, FF, D), FF ** -0.5, 0.109375, ((1, 32),))
    biases = bell_draw(splits[5], (LAYERS, 3, D), 0.3, 1.75, ((2, 32),))
    value_bias = bell_draw(splits[6], (LAYERS, D), (0.3 * (TOK_DEV * N_CTX) ** -0.5), 0.078125, ((1, 32),))
    up_bias = bell_draw(splits[7], (LAYERS, FF), 0.3, 1.75, ((1, 32),))
    gains = jnp.clip(1.0 + 0.1 * jax.random.normal(splits[8], (LAYERS, 2, D), jnp.float32), 0.5, 1.5).astype(jnp.bfloat16)
    shifts = bell_draw(splits[9], (LAYERS, 2, D), 0.3, 1.75, ((2, 32),))
    cotangent = heavy_noise(splits[10], (SEQS, LENGTH, D), 1.0, 8.0, ((0, 4), (1, 8)), (1, 2, 8, 2.0))
    return {"inputs": inputs, "w_qkv": w_qkv, "w_out": w_out, "w_up": w_up, "w_down": w_down, "biases": biases, "value_bias": value_bias, "up_bias": up_bias, "gains": gains, "shifts": shifts, "cotangent": cotangent}


@jax.custom_vjp
def low(v):
    return lax.optimization_barrier(v.astype(jnp.bfloat16)).astype(jnp.float32)

@jax.custom_vjp
def low_back(v):
    return v

def low_keep(v):
    return (low(v), None)

def low_pass(kept, grad):
    return (grad,)

def back_keep(v):
    return (v, None)

def back_low(kept, grad):
    return (low(grad),)
low.defvjp(low_keep, low_pass)
low_back.defvjp(back_keep, back_low)

def normalize(values, gain, shift):
    centred = values - lax.optimization_barrier(jnp.mean(values, axis=1, keepdims=True))
    spread = lax.optimization_barrier(jnp.mean(centred * centred, axis=1, keepdims=True))
    return centred * lax.rsqrt(spread + 1e-12) * gain + shift

def attend_sequence(parts):
    queries, keys, values = parts
    query_blocks = queries.reshape(LENGTH // TOK_DEV, TOK_DEV, HEADS, HEAD_DIM)
    key_heads = keys.reshape(LENGTH, HEADS, HEAD_DIM)
    value_heads = values.reshape(LENGTH, HEADS, HEAD_DIM)

    @jax.checkpoint
    def attend_block(query_block):
        scores = jnp.einsum('thd,khd->htk', query_block, key_heads, precision=lax.Precision.HIGHEST) * HEAD_DIM ** (-0.5)
        scores = low_back(scores)
        weights = low(jax.nn.softmax(scores, axis=2))
        mixed = jnp.einsum('htk,khd->thd', weights, value_heads, precision=lax.Precision.HIGHEST)
        return mixed.reshape(TOK_DEV, D)
    return lax.map(attend_block, query_blocks).reshape(LENGTH, D)

def forward(inputs, w_qkv, w_out, w_up, w_down, biases, value_bias, up_bias, gains, shifts):
    highest = lax.Precision.HIGHEST
    stream = inputs.reshape(SEQS * LENGTH, D)
    for layer in range(LAYERS):
        rounded = low(stream)
        queries = low_back(low(jnp.dot(rounded, w_qkv[layer, 0], precision=highest) + biases[layer, 0]))
        keys = low_back(low(jnp.dot(rounded, w_qkv[layer, 1], precision=highest)))
        values = low_back(low(jnp.dot(rounded, w_qkv[layer, 2], precision=highest) + value_bias[layer]))
        mixed = lax.map(attend_sequence, (queries.reshape(SEQS, LENGTH, D), keys.reshape(SEQS, LENGTH, D), values.reshape(SEQS, LENGTH, D)))
        mixed = low_back(low(mixed.reshape(SEQS * LENGTH, D)))
        branch = low_back(jnp.dot(mixed, w_out[layer], precision=highest) + biases[layer, 1])
        normed = normalize(stream + branch, gains[layer, 0], shifts[layer, 0])
        upward = low_back(jnp.dot(low(normed), w_up[layer], precision=highest) + up_bias[layer])
        active = low(jax.nn.gelu(upward, approximate=False))
        lowered = low_back(jnp.dot(active, w_down[layer], precision=highest) + biases[layer, 2])
        stream = normalize(normed + lowered, gains[layer, 1], shifts[layer, 1])
    return stream.reshape(SEQS, LENGTH, D)

def reference(inputs, w_qkv, w_out, w_up, w_down, biases, value_bias, up_bias, gains, shifts, cotangent):
    floats = tuple((array.astype(jnp.float32) for array in (inputs, w_qkv, w_out, w_up, w_down, biases, value_bias, up_bias, gains, shifts)))
    output, pullback = jax.vjp(forward, *floats)
    grads = pullback(cotangent.astype(jnp.float32))
    return (output.astype(jnp.bfloat16), grads[0].astype(jnp.bfloat16), grads[1], grads[2], grads[3], grads[4], grads[5], grads[6], grads[7], grads[8], grads[9])
```

```python
import functools
import types

import jax
import jax.numpy as jnp
from jax import lax
from jax.experimental import pallas as pl
from jax.experimental.pallas import tpu as pltpu
from jax.sharding import PartitionSpec as P

D = 768
HEADS = 12
HEAD_DIM = 64
LAYERS = 2
KERNEL_VMEM = 63 * 2**20


BF = jnp.bfloat16
F32 = jnp.float32
MESH = pl.DeviceIdType.MESH
MEMBERS = 4
LOCAL_HEADS = HEADS // MEMBERS
PACK = 640
SLOT = 64
PIECE = 64


def dot_nn(left, right):
    return lax.dot_general(left, right, (((1,), (0,)), ((), ())), preferred_element_type=F32)


def dot_nt(left, right):
    return lax.dot_general(left, right, (((1,), (1,)), ((), ())), preferred_element_type=F32)


def dot_tn(left, right):
    return lax.dot_general(left, right, (((0,), (0,)), ((), ())), preferred_element_type=F32)


def dot_exact(left, right):
    return lax.dot_general(
        left,
        right,
        (((1,), (0,)), ((), ())),
        precision=lax.Precision.HIGHEST,
        preferred_element_type=F32,
    )


def packed_lanes(shape, axis):
    lane = lax.broadcasted_iota(jnp.int32, shape, axis)
    slot = lane >> 6
    head = jnp.where(slot >= 6, 2, slot & 1)
    is_query = (slot < 2) | (slot == 6)
    is_value = (slot == 4) | (slot == 5) | (slot == 8)
    return (head * HEAD_DIM + (lane & 63), is_query, is_value)


def scratch_layout(nz, ny, rows, half, d_rows, f_rows):
    dma = pltpu.SemaphoreType.DMA
    two = 2 * d_rows
    ff = nz * ny * f_rows
    vm = pltpu.VMEM
    return dict(
        wq=vm((LAYERS, nz, 2, ny, two, PACK), BF),
        wu=vm((LAYERS, nz, 2, ny, two, ff), BF),
        wd=vm((LAYERS, nz, ny, f_rows, D), BF),
        wog=vm((nz, ny, two, D), BF),
        wo=vm((LAYERS, 256, D), BF),
        smg=vm((nz, ny, MEMBERS, 32, 128), BF),
        qs=vm((MEMBERS, two, PACK), BF),
        us=vm((MEMBERS, two, ff), BF),
        pb=vm((16, D), F32),
        ub=vm((16, ff), F32),
        bq=vm((LAYERS, 8, PACK), F32),
        xf=vm((LAYERS, rows, D), BF),
        qkv=vm((LAYERS, rows, PACK), BF),
        prob=vm((LAYERS, LOCAL_HEADS, rows, rows), BF),
        mix=vm((LAYERS, rows, 256), F32),
        mixl=vm((LAYERS, rows, 256), BF),
        xh1=vm((LAYERS, half, D), F32),
        iv1=vm((LAYERS, half, 128), F32),
        nl=vm((LAYERS, rows, D), BF),
        gp=vm((LAYERS, rows, ff), F32),
        act=vm((LAYERS, rows, ff), BF),
        xh2=vm((LAYERS, half, D), F32),
        iv2=vm((LAYERS, half, 128), F32),
        stream=vm((half, D), F32),
        normed=vm((half, D), F32),
        ct=vm((half, D), BF),
        ownp=vm((half, D), F32),
        sibs=vm((2, half, D), BF),
        sibr=vm((2, half, D), BF),
        xs=vm((2, half, D), BF),
        xr=vm((2, half, D), BF),
        dl=vm((rows, D), BF),
        db=vm((rows, D), BF),
        du=vm((rows, ff), BF),
        dq=vm((rows, PACK), BF),
        dm=vm((rows, 256), BF),
        ds=vm((rows, rows), BF),
        back=vm((2, half, D), BF),
        land=vm((2, 2, rows // (2 * nz), D), BF),
        gq=vm((LAYERS, nz, 2, ny, two, PACK), BF),
        gu=vm((LAYERS, nz, 2, ny, two, ff), BF),
        gd=vm((LAYERS, nz, ny, f_rows, D), BF),
        go=vm((LAYERS, nz, ny, 32, D), BF),
        ryq=vm((LAYERS, nz, 2, two, PACK), BF),
        ryu=vm((LAYERS, nz, 2, two, ff), BF),
        ryd=vm((LAYERS, nz, f_rows, D), BF),
        ryo=vm((LAYERS, nz, 32, D), BF),
        rzq=vm((LAYERS, 2, nz - 1, 2, two, PACK), BF),
        rzu=vm((LAYERS, 2, nz - 1, 2, two, ff), BF),
        rzd=vm((LAYERS, 2, nz - 1, f_rows, D), BF),
        rzo=vm((LAYERS, 2, nz - 1, 32, D), BF),
        fq=vm((LAYERS, 2, two, PACK), F32),
        fu=vm((LAYERS, 2, two, ff), F32),
        fo=vm((LAYERS, d_rows, D), F32),
        oq=vm((LAYERS, MEMBERS, d_rows, PACK), F32),
        ou=vm((LAYERS, MEMBERS, d_rows, ff), F32),
        oo=vm((LAYERS, d_rows, D), F32),
        sg=vm((LAYERS, 8, D), F32),
        sgy=vm((LAYERS, 8, D), F32),
        sgt=vm((LAYERS, 8, D), F32),
        sgz=vm((LAYERS, nz, 8, D), F32),
        sga=vm((LAYERS, MEMBERS, 8, D), F32),
        stage_s=dma((3, 3)),
        stage_r=dma((3, 3)),
        perm=dma((2,)),
        in_s=dma((4, 2)),
        in_r=dma((4, 2)),
        inx_s=dma((2, 2)),
        inx_r=dma((2, 2)),
        ins_s=dma((1,)),
        ins_r=dma((1,)),
        gz_s=dma((8, 2, nz)),
        gz_r=dma((8, 2, nz)),
        gy_s=dma((8, nz)),
        gy_r=dma((8, nz)),
        sib_s=dma((2, half // PIECE)),
        sib_r=dma((2, half // PIECE)),
        x_s=dma((2, half // PIECE)),
        x_r=dma((2, half // PIECE)),
        ag_s=dma((2, half // PIECE)),
        ag_r=dma((2, half // PIECE)),
        ry_s=dma((8,)),
        ry_r=dma((8,)),
        rz_s=dma((8, 2, nz)),
        rz_r=dma((8, 2, nz)),
        fin_s=dma((LAYERS, 2, 3)),
        fin_r=dma((LAYERS, 2, 3)),
        fino=dma((LAYERS, 2)),
        sgy_s=dma((LAYERS,)),
        sgy_r=dma((LAYERS,)),
        sgz_s=dma((LAYERS, nz)),
        sgz_r=dma((LAYERS, nz)),
        sga_s=dma((LAYERS, 3)),
        sga_r=dma((LAYERS, 3)),
    )


def group_kernel(layout, nz, *refs):
    inp, q_in, u_in, o_in, d_in, s_in, cot = refs[:7]
    out, gin, q_out, u_out, o_out, d_out, s_out = refs[7:14]
    S = types.SimpleNamespace(**dict(zip(layout.keys(), refs[14:])))
    rows = S.dl.shape[0]
    half = rows // 2
    block = inp.shape[1]
    d_rows = d_in.shape[1] // 4
    f_rows = d_in.shape[1]
    two = 2 * d_rows
    ff = S.du.shape[1]
    pieces = half // PIECE
    place = lax.axis_index("ctx")
    lane_f = lax.axis_index("fsdp")
    z, x = lax.div(place, 2), lax.rem(place, 2)
    y, c = lax.div(lane_f, 2), lax.rem(lane_f, 2)
    m = 2 * x + c
    d = 4 * place + lane_f
    devices = 8 * nz

    def dev(z_at, x_at, y_at, c_at):
        return (2 * z_at + x_at, 2 * y_at + c_at)

    def rcopy(source, target, send, recv, to):
        return pltpu.make_async_remote_copy(
            src_ref=source,
            dst_ref=target,
            send_sem=send,
            recv_sem=recv,
            device_id=to,
            device_id_type=MESH,
        )

    barrier = pltpu.get_barrier_semaphore()

    def hail(step, carry):
        other = lax.rem(d + step, devices)
        pl.semaphore_signal(
            barrier, inc=1, device_id=(lax.div(other, 4), lax.rem(other, 4)), device_id_type=MESH
        )
        return carry

    lax.fori_loop(1, devices, hail, 0)
    pl.semaphore_wait(barrier, devices - 1)

    relation = ((x, 1 - c), (1 - x, c), (1 - x, 1 - c))
    sibling = dev(z, x, y, 1 - c)
    peer = dev(z, 1 - x, y, c)
    across = dev(z, x, 1 - y, c)

    def stage_copy(kind, r):
        x_r, c_r = relation[r]
        m_r = 2 * x_r + c_r
        source = (s_in, q_in.at[m_r], u_in.at[m_r])[kind]
        target = (S.smg.at[z, y, m], S.qs.at[m], S.us.at[m])[kind]
        return rcopy(source, target, S.stage_s.at[kind, r], S.stage_r.at[kind, r], dev(z, x_r, y, c_r))

    def stage_wait(kind, r):
        x_r, c_r = relation[r]
        m_r = 2 * x_r + c_r
        target = (S.smg.at[z, y, m_r], S.qs.at[m_r], S.us.at[m_r])[kind]
        rcopy(
            target, target, S.stage_s.at[kind, r], S.stage_r.at[kind, r], dev(z, x_r, y, c_r)
        ).wait_recv()

    for kind in (1, 0):
        for r in (1, 2, 0):
            stage_copy(kind, r).start()

    def own_block(j):
        return (2 * c + j == z) & (lax.div(z, 2) == c)

    def scatter_in(which, source, target, position):
        for j in range(2):
            copy = rcopy(
                source.at[j],
                target.at[pl.ds(position, block)],
                S.in_s.at[which, j],
                S.in_r.at[which, lax.rem(z, 2)],
                dev(2 * c + j, x, y, lax.div(z, 2)),
            )

            @pl.when(own_block(j))
            def _():
                target[pl.ds(position, block), :] = source[j]

            @pl.when(jnp.logical_not(own_block(j)))
            def _():
                copy.start()

    def scatter_in_wait(which, source, target, base):
        for k in range(2):

            @pl.when(2 * c + k != z)
            def _():
                spot = target.at[pl.ds(base + 2 * block * k, block)]
                rcopy(
                    spot, spot, S.in_s.at[which, 0], S.in_r.at[which, k], peer
                ).wait_recv()

    def scatter_in_drain(which, source, target):
        for j in range(2):

            @pl.when(jnp.logical_not(own_block(j)))
            def _():
                rcopy(
                    source.at[j], source.at[j], S.in_s.at[which, j], S.in_r.at[which, 0], peer
                ).wait_send()

    first = S.xf.at[0]
    scatter_in(0, inp, first, block * place)

    perm_to = dev(2 * x + y, lax.div(z, 2), c, lax.rem(z, 2))
    perm_stays = (2 * x + y == z) & (lax.div(z, 2) == x) & (c == y) & (lax.rem(z, 2) == c)
    perm_copy = rcopy(o_in, S.wog.at[2 * x + y, c], S.perm.at[0], S.perm.at[1], perm_to)

    @pl.when(perm_stays)
    def _():
        S.wog[z, y] = o_in[...]

    @pl.when(jnp.logical_not(perm_stays))
    def _():
        perm_copy.start()

    for r in (1, 2, 0):
        stage_copy(2, r).start()
    S.smg[z, y, m] = s_in[...]
    S.qs[m] = q_in[m]
    S.us[m] = u_in[m]
    for layer in range(LAYERS):
        S.wd[layer, z, y] = d_in[layer]

    def join(staged, target):
        for xx in range(2):
            first_part = staged[2 * xx].astype(F32)
            second_part = staged[2 * xx + 1].astype(F32)
            for layer in range(LAYERS):
                cut = slice(layer * d_rows, (layer + 1) * d_rows)
                target[layer, z, xx, y] = jnp.concatenate(
                    [first_part[cut], second_part[cut]], axis=0
                ).astype(BF)

    def slab(cls, z_at, y_at):
        return (
            lambda: S.smg.at[z_at, y_at],
            lambda: S.wq.at[0, z_at, :, y_at],
            lambda: S.wog.at[z_at, y_at],
            lambda: S.wu.at[0, z_at, :, y_at],
            lambda: S.wd.at[0, z_at, y_at],
            lambda: S.wq.at[1, z_at, :, y_at],
            lambda: S.wu.at[1, z_at, :, y_at],
            lambda: S.wd.at[1, z_at, y_at],
        )[cls]()

    def z_copy(cls, way, step, z_at):
        spot = slab(cls, z_at, y)
        to = dev(z + 1 - 2 * way, x, y, c)
        return rcopy(spot, spot, S.gz_s.at[cls, way, step], S.gz_r.at[cls, way, step], to)

    def y_copy(cls, z_at):
        spot = slab(cls, z_at, y)
        return rcopy(spot, spot, S.gy_s.at[cls, z_at], S.gy_r.at[cls, z_at], across)

    def gather_step(cls, step):
        @pl.when(z >= step)
        def _():
            if step > 0:
                z_copy(cls, 0, step - 1, z - step).wait_recv()
            if step < nz - 1:

                @pl.when(z < nz - 1)
                def _():
                    z_copy(cls, 0, step, z - step).start()

            y_copy(cls, z - step).start()

        @pl.when(z + step <= nz - 1)
        def _():
            if step > 0:
                z_copy(cls, 1, step - 1, z + step).wait_recv()
            if step < nz - 1:

                @pl.when(z > 0)
                def _():
                    z_copy(cls, 1, step, z + step).start()

            if step > 0:
                y_copy(cls, z + step).start()

    def gather_wait(cls):
        def one(t, carry):
            spot = slab(cls, t, 1 - y)
            rcopy(spot, spot, S.gy_s.at[cls, t], S.gy_r.at[cls, t], across).wait_recv()
            return carry

        lax.fori_loop(0, nz, one, 0)

    def gather_drain(cls):
        for step in range(nz - 1):

            @pl.when((z >= step) & (z < nz - 1))
            def _():
                z_copy(cls, 0, step, z - step).wait_send()

            @pl.when((z + step <= nz - 1) & (z > 0))
            def _():
                z_copy(cls, 1, step, z + step).wait_send()

        def one(t, carry):
            y_copy(cls, t).wait_send()
            return carry

        lax.fori_loop(0, nz, one, 0)

    for r in range(3):
        stage_wait(1, r)
    join(S.qs, S.wq)
    gather_step(1, 0)
    for r in range(3):
        stage_wait(0, r)
    gather_step(0, 0)

    def x_spots(target, base, mine):
        return [target.at[pl.ds(base + block * (2 * k + mine), block)] for k in range(2)]

    def swap_start(which, target, base):
        for k, spot in enumerate(x_spots(target, base, x)):
            rcopy(spot, spot, S.inx_s.at[which, k], S.inx_r.at[which, k], peer).start()

    def swap_wait(which, target, base):
        for k, spot in enumerate(x_spots(target, base, 1 - x)):
            rcopy(spot, spot, S.inx_s.at[which, k], S.inx_r.at[which, k], peer).wait_recv()
        for k, spot in enumerate(x_spots(target, base, x)):
            rcopy(spot, spot, S.inx_s.at[which, k], S.inx_r.at[which, k], peer).wait_send()

    mine = half * c
    theirs = half * (1 - c)
    scatter_in_wait(0, inp, first, mine + block * x)
    swap_start(0, first, mine)
    gather_step(1, 1)
    gather_step(0, 1)
    for r in range(3):
        stage_wait(2, r)
    join(S.us, S.wu)
    swap_wait(0, first, mine)
    spot = first.at[pl.ds(mine, half)]
    rcopy(spot, spot, S.ins_s.at[0], S.ins_r.at[0], sibling).start()
    S.stream[...] = S.xf[0, pl.ds(mine, half), :].astype(F32)
    gather_step(1, 2)
    gather_step(0, 2)
    gather_step(1, 3)
    gather_step(0, 3)

    @pl.when(jnp.logical_not(perm_stays))
    def _():
        spot = S.wog.at[z, y]
        rcopy(spot, spot, S.perm.at[0], S.perm.at[1], peer).wait_recv()

    gather_step(2, 0)
    gather_step(3, 0)
    gather_step(4, 0)
    gather_wait(0)

    def small_params():
        row_shape = (devices * 16, D)
        lane = lax.broadcasted_iota(jnp.int32, (128, D), 0)
        col = lax.broadcasted_iota(jnp.int32, (128, D), 1)
        tile = jnp.where(lax.rem(col, d_rows) == lane, 1.0, 0.0).astype(BF)
        packs = S.smg[:, :, :, 0:16, :].reshape(devices * 16, 128)
        spread = dot_nn(packs, tile)
        owner_row = lax.broadcasted_iota(jnp.int32, row_shape, 0) >> 4
        zz = owner_row >> 3
        yy = (owner_row >> 2) & 1
        xx = (owner_row >> 1) & 1
        cc = owner_row & 1
        owner = zz * 8 + xx * 4 + yy * 2 + cc
        at = lax.div(lax.broadcasted_iota(jnp.int32, row_shape, 1), d_rows)
        spread = jnp.where(owner == at, spread, 0.0)
        S.pb[...] = jnp.sum(spread.reshape(devices, 16, D), axis=0)
        lane = lax.broadcasted_iota(jnp.int32, (128, ff), 0)
        col = lax.broadcasted_iota(jnp.int32, (128, ff), 1)
        tile = jnp.where(lax.rem(col, f_rows) == lane, 1.0, 0.0).astype(BF)
        packs = S.smg[:, :, m, 16:32, :].reshape(2 * nz * 16, 128)
        spread = dot_nn(packs, tile)
        row_shape = (2 * nz * 16, ff)
        owner = lax.broadcasted_iota(jnp.int32, row_shape, 0) >> 4
        at = lax.div(lax.broadcasted_iota(jnp.int32, row_shape, 1), f_rows)
        spread = jnp.where(owner == at, spread, 0.0)
        S.ub[...] = jnp.sum(spread.reshape(2 * nz, 16, ff), axis=0)
        source = lax.broadcasted_iota(jnp.int32, (D, PACK), 0)
        target, unused_q, unused_v = packed_lanes((D, PACK), 1)
        pick = jnp.where(source == target + m * (LOCAL_HEADS * HEAD_DIM), 1.0, 0.0).astype(BF)
        picked = dot_nn(S.pb[...].astype(BF), pick)
        unused, is_query, is_value = packed_lanes((1, PACK), 1)
        for layer in range(LAYERS):
            base = 8 * layer
            row = jnp.where(is_query, picked[base : base + 1], 0.0)
            row = jnp.where(is_value, picked[base + 3 : base + 4], row)
            S.bq[layer, 0:1, :] = row

    small_params()
    scatter_in(1, cot, S.ct, block * (2 * lax.rem(z, 2) + x))

    def param(layer, kind):
        return S.pb[8 * layer + kind : 8 * layer + kind + 1, :]

    def piece_rows(i):
        return pl.ds(i * PIECE if isinstance(i, int) else pl.multiple_of(i * PIECE, PIECE), PIECE)

    def spread_start(par, i, ref, value):
        spot_rows = pl.ds(pl.multiple_of(mine + i * PIECE, PIECE), PIECE)
        ref[spot_rows, :] = value
        spot = ref.at[spot_rows]
        rcopy(spot, spot, S.ag_s.at[par, i], S.ag_r.at[par, i], sibling).start()

    def spread_wait(par, ref):
        def one(i, carry):
            got = ref.at[pl.ds(pl.multiple_of(theirs + i * PIECE, PIECE), PIECE)]
            sent = ref.at[pl.ds(pl.multiple_of(mine + i * PIECE, PIECE), PIECE)]
            rcopy(got, got, S.ag_s.at[par, i], S.ag_r.at[par, i], sibling).wait_recv()
            rcopy(sent, sent, S.ag_s.at[par, i], S.ag_r.at[par, i], sibling).wait_send()
            return carry

        lax.fori_loop(0, pieces, one, 0)

    def sib_copy(par, i):
        at = piece_rows(i)
        return rcopy(
            S.sibs.at[par, at], S.sibr.at[par, at], S.sib_s.at[par, i], S.sib_r.at[par, i], sibling
        )

    def peer_copy(par, i):
        at = piece_rows(i)
        return rcopy(S.xs.at[par, at], S.xr.at[par, at], S.x_s.at[par, i], S.x_r.at[par, i], peer)

    def member_sum(par, part, use, filler):
        S.sibs[par] = part(pl.multiple_of(theirs, half)).astype(BF)
        for i in range(pieces):
            sib_copy(par, i).start()
        S.ownp[...] = part(pl.multiple_of(mine, half))

        def send(i, carry):
            at = piece_rows(i)
            sib_copy(par, i).wait_recv()
            S.xs[par, at, :] = (S.ownp[at, :] + S.sibr[par, at, :].astype(F32)).astype(BF)
            peer_copy(par, i).start()
            return carry

        lax.fori_loop(0, pieces, send, 0)
        filler()

        def take(i, carry):
            at = piece_rows(i)
            peer_copy(par, i).wait_recv()
            use(i, S.xs[par, at, :].astype(F32) + S.xr[par, at, :].astype(F32))
            return carry

        lax.fori_loop(0, pieces, take, 0)

        def drain(i, carry):
            sib_copy(par, i).wait_send()
            peer_copy(par, i).wait_send()
            return carry

        lax.fori_loop(0, pieces, drain, 0)

    def norm_piece(total, at, layer, gain, shift, scaled_ref, inv_ref):
        centred = total - jnp.mean(total, axis=1, keepdims=True)
        inv = lax.rsqrt(jnp.mean(centred * centred, axis=1, keepdims=True) + 1e-12)
        scaled = centred * inv
        scaled_ref[layer, at, :] = scaled
        inv_ref[layer, at, :] = jnp.broadcast_to(inv, (PIECE, 128))
        return scaled * gain + shift

    def flat(value):
        return value.reshape(-1, value.shape[-1])

    lane_low = lax.broadcasted_iota(jnp.int32, (1, 128), 1) < HEAD_DIM

    def swap_lanes(value):
        return pltpu.roll(value.astype(F32), HEAD_DIM, 1).astype(BF)

    def head_parts(layer, h, at):
        zero = jnp.zeros((), BF)
        if h < 2:
            keep = lane_low if h == 0 else jnp.logical_not(lane_low)
            queries = S.qkv[layer, at, 0:128]
        else:
            keep = lane_low
            queries = S.qkv[layer, at, 384:512]
        return jnp.where(keep, queries * jnp.asarray(HEAD_DIM**-0.5, BF), zero)

    def head_keys(layer, h):
        if h < 2:
            return S.qkv[layer, :, 128:256]
        return swap_lanes(S.qkv[layer, :, 384:512])

    def head_values(layer, h):
        return S.qkv[layer, :, 256:384] if h < 2 else S.qkv[layer, :, 512:640]

    def forward(layer, fill_one, fill_two, last):
        weight = flat(S.wq[layer])
        for i in range(2):
            at = slice(i * half, (i + 1) * half)
            S.qkv[layer, at, :] = (
                dot_nn(S.xf[layer, at, :], weight) + S.bq[layer, 0:1, :]
            ).astype(BF)

        def attend(i, carry):
            at = pl.ds(pl.multiple_of(i * 128, 128), 128)
            mixes = []
            for h in range(LOCAL_HEADS):
                scores = dot_nt(head_parts(layer, h, at), head_keys(layer, h))
                weights = jnp.exp(scores - jnp.max(scores, axis=1, keepdims=True))
                weights = (weights * (1.0 / jnp.sum(weights, axis=1, keepdims=True))).astype(BF)
                S.prob[layer, h, at, :] = weights
                mixes.append(dot_nn(weights, head_values(layer, h)))
            left = jnp.where(lane_low, mixes[0], mixes[1])
            right = jnp.where(lane_low, mixes[2], 0.0)
            S.mix[layer, at, 0:128] = left
            S.mix[layer, at, 128:256] = right
            S.mixl[layer, at, 0:128] = left.astype(BF)
            S.mixl[layer, at, 128:256] = right.astype(BF)
            return carry

        lax.fori_loop(0, rows // 128, attend, 0)

    def mixed_part(layer):
        return lambda start: dot_nn(S.mixl[layer, pl.ds(start, half), :], S.wo[layer])

    def after_attention(layer):
        def use(i, total):
            at = piece_rows(i)
            total = S.stream[at, :] + total + param(layer, 1)
            normed = norm_piece(
                total, at, layer, param(layer, 4), param(layer, 6), S.xh1, S.iv1
            )
            S.normed[at, :] = normed
            spread_start(0, i, S.nl.at[layer], normed.astype(BF))

        return use

    def raise_part(layer):
        def one(i, carry):
            at = pl.ds(pl.multiple_of(i * 128, 128), 128)
            upward = dot_nn(S.nl[layer, at, :], flat(S.wu[layer])) + S.ub[layer : layer + 1, :]
            cdf = 0.5 * (1.0 + lax.erf(upward * (0.5**0.5)))
            density = jnp.exp(-0.5 * upward * upward) * ((2.0 * jnp.pi) ** -0.5)
            S.act[layer, at, :] = (upward * cdf).astype(BF)
            S.gp[layer, at, :] = cdf + upward * density
            return carry

        lax.fori_loop(0, rows // 128, one, 0)

    def lower_part(layer):
        return lambda start: dot_nn(S.act[layer, pl.ds(start, half), :], flat(S.wd[layer]))

    def after_lower(layer):
        def use(i, total):
            at = piece_rows(i)
            total = S.normed[at, :] + total + param(layer, 2)
            result = norm_piece(
                total, at, layer, param(layer, 5), param(layer, 7), S.xh2, S.iv2
            )
            if layer < LAYERS - 1:
                S.stream[at, :] = result
                spread_start(1, i, S.xf.at[layer + 1], result.astype(BF))
            else:
                S.back[0, at, :] = result.astype(BF)

        return use

    def scatter_out(which, source):
        for k in range(2):
            stays = (2 * c + k == z) & (lax.div(z, 2) == c)
            spot = source.at[pl.ds(pl.multiple_of(block * (2 * k + x), block), block)]
            slot = lax.rem(z, 2)

            @pl.when(stays)
            def _():
                S.land[which, slot] = spot[...]

            @pl.when(jnp.logical_not(stays))
            def _():
                rcopy(
                    spot,
                    S.land.at[which, slot],
                    S.in_s.at[2 + which, k],
                    S.in_r.at[2 + which, slot],
                    dev(2 * c + k, x, y, lax.div(z, 2)),
                ).start()

    def scatter_out_wait(which, source, result):
        for k in range(2):
            spot = source.at[pl.ds(pl.multiple_of(block * (2 * k + x), block), block)]

            @pl.when(jnp.logical_not((2 * c + k == z) & (lax.div(z, 2) == c)))
            def _():
                rcopy(
                    spot, spot, S.in_s.at[2 + which, k], S.in_r.at[2 + which, 0], peer
                ).wait_send()

            @pl.when(jnp.logical_not(own_block(k)))
            def _():
                landed = S.land.at[which, k]
                rcopy(
                    landed, landed, S.in_s.at[2 + which, 0], S.in_r.at[2 + which, k], peer
                ).wait_recv()

        result[...] = S.land[which]

    def out_weights():
        gather_wait(2)
        for layer in range(LAYERS):
            cut = slice(layer * d_rows, (layer + 1) * d_rows)
            parts = [S.wog[t, yy].astype(F32)[cut] for t in range(nz) for yy in range(2)]
            parts.append(jnp.zeros((256 - 2 * nz * d_rows, D), F32))
            S.wo[layer] = jnp.concatenate(parts, axis=0).astype(BF)

    nothing = lambda: None

    spot = first.at[pl.ds(theirs, half)]
    rcopy(spot, spot, S.ins_s.at[0], S.ins_r.at[0], sibling).wait_recv()
    gather_wait(1)
    gather_step(2, 1)
    forward(0, nothing, nothing, False)
    gather_step(2, 2)
    gather_step(3, 1)
    gather_step(2, 3)
    out_weights()

    def fill_a():
        gather_step(3, 2)
        gather_step(4, 1)
        gather_step(5, 0)
        gather_step(6, 0)
        gather_step(7, 0)
        gather_step(3, 3)
        gather_step(4, 2)
        scatter_in_wait(1, cot, S.ct, block * x)
        swap_start(1, S.ct, 0)
        gather_wait(3)

    member_sum(0, mixed_part(0), after_attention(0), fill_a)
    spread_wait(0, S.nl.at[0])
    raise_part(0)
    gather_step(4, 3)
    gather_step(5, 1)
    gather_wait(4)

    def fill_b():
        gather_step(5, 2)
        gather_step(6, 1)
        gather_step(5, 3)
        gather_step(7, 1)

    member_sum(1, lower_part(0), after_lower(0), fill_b)
    spread_wait(1, S.xf.at[1])
    gather_wait(5)
    forward(1, nothing, nothing, False)
    gather_step(6, 2)

    def fill_c():
        gather_step(7, 2)
        gather_step(6, 3)
        gather_step(7, 3)
        gather_wait(6)

    member_sum(0, mixed_part(1), after_attention(1), fill_c)
    spread_wait(0, S.nl.at[1])
    raise_part(1)
    gather_wait(7)
    swap_wait(1, S.ct, 0)
    member_sum(1, lower_part(1), after_lower(1), nothing)
    scatter_out(0, S.back.at[0])

    S.sg[...] = jnp.zeros_like(S.sg)

    def add_row(layer, kind, value):
        S.sg[layer, kind : kind + 1, :] += jnp.sum(value, axis=0, keepdims=True)

    def norm_back_piece(grad, at, layer, which):
        scaled = (S.xh1 if which == 0 else S.xh2)[layer, at, :]
        inv = (S.iv1 if which == 0 else S.iv2)[layer, at, 0:1]
        add_row(layer, 2 + which, grad * scaled)
        add_row(layer, 4 + which, grad)
        weighted = grad * param(layer, 4 + which)
        back = (
            weighted
            - jnp.mean(weighted, axis=1, keepdims=True)
            - scaled * jnp.mean(weighted * scaled, axis=1, keepdims=True)
        ) * inv
        return back

    def lower_back(layer, i, grad):
        at = piece_rows(i)
        back = norm_back_piece(grad, at, layer, 1)
        S.normed[at, :] = back
        rounded = back.astype(BF)
        add_row(layer, 1, rounded.astype(F32))
        spread_start(0, i, S.dl, rounded)

    def first_back(i, carry):
        lower_back(LAYERS - 1, i, S.ct[piece_rows(i), :].astype(F32))
        return carry

    lax.fori_loop(0, pieces, first_back, 0)

    def raise_back(layer):
        def one(i, carry):
            at = pl.ds(pl.multiple_of(i * 128, 128), 128)
            back = dot_nt(S.dl[at, :], flat(S.wd[layer])) * S.gp[layer, at, :]
            rounded = back.astype(BF)
            S.du[at, :] = rounded
            add_row(layer, 6, rounded.astype(F32))
            return carry

        lax.fori_loop(0, rows // 128, one, 0)

    grads = (S.gq, S.gu, S.gd, S.go)
    from_y = (S.ryq, S.ryu, S.ryd, S.ryo)
    from_z = (S.rzq, S.rzu, S.rzd, S.rzo)

    def grad_slab(layer, kind, t, y_at):
        ref = grads[kind]
        return ref.at[layer, t, :, y_at] if kind < 2 else ref.at[layer, t, y_at]

    def reduce_y_copy(layer, kind):
        ref = grads[kind]
        source = ref.at[layer, :, :, 1 - y] if kind < 2 else ref.at[layer, :, 1 - y]
        target = from_y[kind].at[layer]
        n = 4 * layer + kind
        return rcopy(source, target, S.ry_s.at[n], S.ry_r.at[n], across)

    def reduce_z_copy(layer, kind, way, t):
        source = grad_slab(layer, kind, t, y)
        target = from_z[kind].at[layer, way, t - way]
        n = 4 * layer + kind
        to = dev(z - 1 + 2 * way, x, y, c)
        return rcopy(source, target, S.rz_s.at[n, way, t], S.rz_r.at[n, way, t], to)

    def slab_add(target, other):
        if len(target.shape) == 3:
            for xx in range(2):
                target[xx] = (target[xx].astype(F32) + other[xx].astype(F32)).astype(BF)
        else:
            target[...] = (target[...].astype(F32) + other[...].astype(F32)).astype(BF)

    def reduce_start(layer, kind):
        reduce_y_copy(layer, kind).start()

    def reduce_wave(layer, kind, wave):
        if wave == 0:
            reduce_y_copy(layer, kind).wait_recv()

            def one(t, carry):
                slab_add(grad_slab(layer, kind, t, y), from_y[kind].at[layer, t])
                return carry

            lax.fori_loop(0, nz, one, 0)

        @pl.when(z == nz - 1 - wave)
        def _():
            for t in range(nz - 1 - wave):
                if wave > 0:
                    copy = reduce_z_copy(layer, kind, 0, t)
                    copy.wait_recv()
                    slab_add(grad_slab(layer, kind, t, y), from_z[kind].at[layer, 0, t])
                reduce_z_copy(layer, kind, 0, t).start()

        @pl.when(z == wave)
        def _():
            for t in range(nz - 1, wave, -1):
                if wave > 0:
                    copy = reduce_z_copy(layer, kind, 1, t)
                    copy.wait_recv()
                    slab_add(grad_slab(layer, kind, t, y), from_z[kind].at[layer, 1, t - 1])
                reduce_z_copy(layer, kind, 1, t).start()

    final = (S.fq, S.fu, d_out, S.fo)

    def reduce_last(layer, kind):
        if kind == 3:
            target = S.fo.at[layer]
            cut = lambda value: value[0:d_rows]
        else:
            target = final[kind].at[layer]
            cut = lambda value: value
        target[...] = cut(grad_slab(layer, kind, z, y)[...].astype(F32))

        @pl.when(z < nz - 1)
        def _():
            reduce_z_copy(layer, kind, 0, z).wait_recv()
            target[...] += cut(from_z[kind][layer, 0, z].astype(F32))

        @pl.when(z > 0)
        def _():
            reduce_z_copy(layer, kind, 1, z).wait_recv()
            target[...] += cut(from_z[kind][layer, 1, z - 1].astype(F32))

        if kind < 2:
            result = (S.oq, S.ou)[kind]
            for r in (1, 2, 0):
                hand_copy(layer, kind, r).start()
            for xx in range(2):
                for cc in range(2):

                    @pl.when((x == xx) & (c == cc))
                    def _():
                        result[layer, 2 * xx + cc] = target[xx, cc * d_rows : (cc + 1) * d_rows, :]

        if kind == 3:
            @pl.when(owner_stays)
            def _():
                S.oo[layer] = target[...]

            @pl.when(jnp.logical_not(owner_stays))
            def _():
                owner_copy(layer).start()

    def hand_copy(layer, kind, r):
        x_r, c_r = relation[r]
        source = (S.fq, S.fu)[kind].at[
            layer, x_r, pl.ds(pl.multiple_of(c_r * d_rows, 8), d_rows)
        ]
        target = (S.oq, S.ou)[kind].at[layer, m]
        return rcopy(
            source,
            target,
            S.fin_s.at[layer, kind, r],
            S.fin_r.at[layer, kind, r],
            dev(z, x_r, y, c_r),
        )

    owner_to = dev(2 * x + c, lax.div(z, 2), lax.rem(z, 2), y)
    owner_stays = (2 * x + c == z) & (lax.div(z, 2) == x) & (lax.rem(z, 2) == y) & (y == c)

    def owner_copy(layer):
        return rcopy(
            S.fo.at[layer], S.oo.at[layer], S.fino.at[layer, 0], S.fino.at[layer, 1], owner_to
        )

    def reduce_drain(layer, kind):
        reduce_y_copy(layer, kind).wait_send()
        for t in range(nz):

            @pl.when(z > t)
            def _():
                reduce_z_copy(layer, kind, 0, t).wait_send()

            @pl.when(z < t)
            def _():
                reduce_z_copy(layer, kind, 1, t).wait_send()

        if kind < 2:
            for r in range(3):
                copy = hand_copy(layer, kind, r)
                copy.wait_send()
                copy.wait_recv()
        if kind == 3:
            @pl.when(jnp.logical_not(owner_stays))
            def _():
                owner_copy(layer).wait_send()
                owner_copy(layer).wait_recv()

    def lower_grad(layer):
        for i in range(2):
            value = dot_tn(S.act[layer, :, i * (ff // 2) : (i + 1) * (ff // 2)], S.dl[...])
            S.gd[layer, i * (nz // 2) : (i + 1) * (nz // 2)] = value.astype(BF).reshape(
                nz // 2, 2, f_rows, D
            )
        reduce_start(layer, 2)

    def raise_grad(layer):
        for i in range(2):
            value = dot_tn(S.nl[layer, :, i * (D // 2) : (i + 1) * (D // 2)], S.du[...])
            S.gu[layer, i * (nz // 2) : (i + 1) * (nz // 2)] = value.astype(BF).reshape(
                nz // 2, 2, 2, two, ff
            )
        reduce_start(layer, 1)

    def out_grad(layer):
        value = dot_tn(S.mixl[layer], S.db[...])
        empty = jnp.zeros((32 - d_rows, D), F32)
        for t in range(nz):
            for yy in range(2):
                at = (2 * t + yy) * d_rows
                S.go[layer, t, yy] = jnp.concatenate(
                    [value[at : at + d_rows], empty], axis=0
                ).astype(BF)
        reduce_start(layer, 3)

    def project_grad(layer):
        for i in range(2):
            value = dot_tn(S.xf[layer, :, i * (D // 2) : (i + 1) * (D // 2)], S.dq[...])
            S.gq[layer, i * (nz // 2) : (i + 1) * (nz // 2)] = value.astype(BF).reshape(
                nz // 2, 2, 2, two, PACK
            )
        reduce_start(layer, 0)

    def branch_back(layer):
        def use(i, total):
            at = piece_rows(i)
            back = norm_back_piece(total + S.normed[at, :], at, layer, 0)
            S.stream[at, :] = back
            rounded = back.astype(BF)
            add_row(layer, 0, rounded.astype(F32))
            spread_start(1, i, S.db, rounded)

        return use

    def attend_back(layer):
        for i in range(2):
            at = slice(i * half, (i + 1) * half)
            S.dm[at, :] = dot_nt(S.db[at, :], S.wo[layer]).astype(BF)
        scale = HEAD_DIM**-0.5
        halves = []
        for h in range(LOCAL_HEADS):
            keep = jnp.logical_not(lane_low) if h == 1 else lane_low
            cols = slice(0, 128) if h < 2 else slice(128, 256)

            def one(i, carry):
                at = pl.ds(pl.multiple_of(i * 128, 128), 128)
                grad = S.dm[at, cols]
                grad = jnp.where(keep, grad, jnp.zeros((), BF))
                delta = jnp.sum(grad.astype(F32) * S.mix[layer, at, cols], axis=1, keepdims=True)
                grad_weights = dot_nt(grad, head_values(layer, h))
                grad_scores = S.prob[layer, h, at, :].astype(F32) * (grad_weights - delta)
                rounded = grad_scores.astype(BF)
                S.ds[at, :] = rounded
                result = dot_nn(rounded, head_keys(layer, h)) * scale
                if h == 0:
                    S.dq[at, 0:128] = result.astype(BF)
                elif h == 1:
                    old = S.dq[at, 0:128]
                    S.dq[at, 0:128] = jnp.where(lane_low, old, result.astype(BF))
                else:
                    S.dq[at, 384:512] = result.astype(BF)
                return carry

            lax.fori_loop(0, rows // 128, one, 0)
            every = slice(0, rows)
            keys_back = dot_tn(S.ds[...], head_parts(layer, h, every)).astype(BF)
            values_back = dot_tn(S.prob[layer, h], S.dm[:, cols]).astype(BF)
            if h == 0:
                S.dq[:, 128:256] = keys_back
                S.dq[:, 256:384] = values_back
            elif h == 1:
                S.dq[:, 128:256] = jnp.where(lane_low, S.dq[:, 128:256], keys_back)
                S.dq[:, 256:384] = jnp.where(lane_low, S.dq[:, 256:384], values_back)
            else:
                old = S.dq[:, 384:512]
                S.dq[:, 384:512] = jnp.where(lane_low, old, swap_lanes(keys_back))
                S.dq[:, 512:640] = jnp.where(lane_low, values_back, jnp.zeros((), BF))
        S.sg[layer, 7:8, 0:PACK] = jnp.sum(S.dq[...].astype(F32), axis=0, keepdims=True)

    def raise_sum(layer):
        return lambda start: dot_nt(S.du[pl.ds(start, half), :], flat(S.wu[layer]))

    def project_sum(layer):
        return lambda start: dot_nt(S.dq[pl.ds(start, half), :], flat(S.wq[layer]))

    def next_back(layer):
        def use(i, total):
            at = piece_rows(i)
            grad = total + S.stream[at, :]
            if layer > 0:
                lower_back(layer - 1, i, grad)
            else:
                S.back[1, at, :] = grad.astype(BF)

        return use

    def small_y(layer):
        return rcopy(S.sg.at[layer], S.sgy.at[layer], S.sgy_s.at[layer], S.sgy_r.at[layer], across)

    def small_z(layer, k):
        to = dev(lax.rem(z + k, nz), x, y, c)
        return rcopy(
            S.sgt.at[layer], S.sgz.at[layer, k], S.sgz_s.at[layer, k], S.sgz_r.at[layer, k], to
        )

    def small_member(layer, r):
        x_r, c_r = relation[r]
        return rcopy(
            S.sgt.at[layer],
            S.sga.at[layer, m],
            S.sga_s.at[layer, r],
            S.sga_r.at[layer, r],
            dev(z, x_r, y, c_r),
        )

    def small_one(layer):
        small_y(layer).start()

    def small_two(layer):
        small_y(layer).wait_recv()
        S.sgt[layer] = S.sg[layer] + S.sgy[layer]
        for k in range(1, nz):
            small_z(layer, k).start()

    def small_three(layer):
        for k in range(1, nz):
            small_z(layer, k).wait_recv()
        for k in range(1, nz):
            small_z(layer, k).wait_send()
        total = S.sgt[layer]
        for k in range(1, nz):
            total = total + S.sgz[layer, k]
        S.sgt[layer] = total
        for r in range(3):
            small_member(layer, r).start()
        S.sga[layer, m] = total

    def small_four(layer):
        for r in range(3):
            small_member(layer, r).wait_send()
            small_member(layer, r).wait_recv()
        small_y(layer).wait_send()
        lane = lax.broadcasted_iota(jnp.int32, (D, 128), 1)
        col = lax.broadcasted_iota(jnp.int32, (D, 128), 0)
        narrow = lane < d_rows
        pick = jnp.where((col == d_rows * d + lane) & narrow, 1.0, 0.0)
        both = S.sga[layer, 2 * x] + S.sga[layer, 2 * x + 1]
        s_out[layer, 0:8, :] = dot_exact(both, pick)
        dim, is_query, is_value = packed_lanes((D, 128), 0)
        hit = (dim == d_rows * (d - 8 * z) + lane) & narrow
        attn = S.sga[layer, z]
        s_out[layer, 8:16, :] = dot_exact(attn, jnp.where(hit & is_query, 1.0, 0.0))
        s_out[layer, 16:24, :] = dot_exact(attn, jnp.where(hit & is_value, 1.0, 0.0))
        pick = jnp.where((col == f_rows * (2 * z + y) + lane) & (lane < f_rows), 1.0, 0.0)
        s_out[layer, 24:32, :] = dot_exact(S.sga[layer, m], pick)

    spread_wait(0, S.dl)
    raise_back(1)

    def fill_d():
        lower_grad(1)
        raise_grad(1)

    member_sum(0, raise_sum(1), branch_back(1), fill_d)
    spread_wait(1, S.db)
    reduce_wave(1, 2, 0)
    attend_back(1)
    reduce_wave(1, 1, 0)

    def fill_e():
        project_grad(1)
        out_grad(1)
        reduce_wave(1, 2, 1)
        reduce_wave(1, 1, 1)
        reduce_wave(1, 2, 2)

    member_sum(1, project_sum(1), next_back(1), fill_e)
    spread_wait(0, S.dl)
    small_one(1)
    reduce_wave(1, 0, 0)
    reduce_wave(1, 1, 2)
    raise_back(0)

    def fill_f():
        lower_grad(0)
        raise_grad(0)
        reduce_last(1, 2)
        reduce_wave(1, 3, 0)
        reduce_wave(1, 0, 1)
        small_two(1)
        reduce_last(1, 1)

    member_sum(0, raise_sum(0), branch_back(0), fill_f)
    spread_wait(1, S.db)
    reduce_wave(1, 3, 1)
    reduce_wave(1, 0, 2)
    reduce_wave(0, 2, 0)
    small_three(1)
    attend_back(0)
    reduce_wave(1, 3, 2)
    reduce_wave(0, 1, 0)
    reduce_wave(0, 2, 1)
    project_grad(0)

    def fill_g():
        out_grad(0)
        reduce_last(1, 0)
        reduce_wave(0, 1, 1)
        small_one(0)
        reduce_wave(0, 2, 2)
        reduce_last(1, 3)

    member_sum(1, project_sum(0), next_back(0), fill_g)
    scatter_out(1, S.back.at[1])
    reduce_wave(0, 0, 0)
    reduce_wave(0, 3, 0)
    reduce_wave(0, 1, 2)
    small_two(0)
    reduce_last(0, 2)
    small_four(1)
    reduce_wave(0, 0, 1)
    reduce_wave(0, 3, 1)
    reduce_last(0, 1)
    small_three(0)
    reduce_wave(0, 0, 2)
    reduce_wave(0, 3, 2)
    reduce_last(0, 0)
    reduce_last(0, 3)
    small_four(0)

    for kind in range(3):
        for r in range(3):
            stage_copy(kind, r).wait_send()
    scatter_in_drain(0, inp, first)
    scatter_in_drain(1, cot, S.ct)

    @pl.when(jnp.logical_not(perm_stays))
    def _():
        perm_copy.wait_send()

    spot = first.at[pl.ds(mine, half)]
    rcopy(spot, spot, S.ins_s.at[0], S.ins_r.at[0], sibling).wait_send()
    for cls in range(8):
        gather_drain(cls)
    scatter_out_wait(0, S.back.at[0], out)
    scatter_out_wait(1, S.back.at[1], gin)
    for layer in range(LAYERS):
        for kind in range(4):
            reduce_drain(layer, kind)
    q_out[...] = S.oq[...]
    u_out[...] = S.ou[...]
    o_out[...] = S.oo[...]


def grouped(nz, ny):
    def run(inputs, w_qkv, w_out, w_up, w_down, biases, value_bias, up_bias, gains, shifts, cotangent):
        seqs, block, unused = inputs.shape
        d_rows = w_out.shape[1]
        f_rows = w_down.shape[1]
        ff = nz * ny * f_rows
        rows = 2 * nz * block
        half = rows // 2
        heads = w_qkv.reshape(LAYERS, 3, d_rows, MEMBERS, LOCAL_HEADS, HEAD_DIM)
        order = ((0, 0), (0, 1), (1, 0), (1, 1), (2, 0), (2, 1), (0, 2), (1, 2), (2, 2))
        columns = [heads[:, kind, :, :, head] for kind, head in order]
        columns.append(jnp.zeros_like(columns[0]))
        q_in = jnp.concatenate(columns, axis=3).transpose(2, 0, 1, 3)
        q_in = q_in.reshape(MEMBERS, LAYERS * d_rows, PACK)
        u_in = w_up.reshape(LAYERS, d_rows, nz, 2, ny, 2, f_rows).transpose(3, 5, 0, 1, 2, 4, 6)
        u_in = u_in.reshape(MEMBERS, LAYERS * d_rows, ff)
        o_in = w_out.reshape(LAYERS * d_rows, D)
        small = jnp.concatenate([biases, value_bias[:, None], gains, shifts], axis=1)
        small = jnp.pad(small.reshape(LAYERS * 8, d_rows), ((0, 0), (0, 128 - d_rows)))
        s_in = jnp.concatenate(
            [small, jnp.pad(up_bias, ((0, 16 - LAYERS), (0, 128 - f_rows)))], axis=0
        )
        layout = scratch_layout(nz, ny, rows, half, d_rows, f_rows)
        vmem = pl.BlockSpec(memory_space=pltpu.VMEM)
        shapes = (
            jax.ShapeDtypeStruct(inputs.shape, BF),
            jax.ShapeDtypeStruct(inputs.shape, BF),
            jax.ShapeDtypeStruct((LAYERS, MEMBERS, d_rows, PACK), F32),
            jax.ShapeDtypeStruct((LAYERS, MEMBERS, d_rows, ff), F32),
            jax.ShapeDtypeStruct((LAYERS, d_rows, D), F32),
            jax.ShapeDtypeStruct((LAYERS, f_rows, D), F32),
            jax.ShapeDtypeStruct((LAYERS, 32, 128), F32),
        )
        output, grad_inputs, q_out, u_out, o_out, d_out, s_out = pl.pallas_call(
            functools.partial(group_kernel, layout, nz),
            out_shape=shapes,
            in_specs=[vmem] * 7,
            out_specs=[vmem] * 7,
            scratch_shapes=list(layout.values()),
            compiler_params=pltpu.CompilerParams(
                collective_id=0, has_side_effects=True, vmem_limit_bytes=KERNEL_VMEM
            ),
        )(inputs, q_in, u_in, o_in, w_down, s_in, cotangent)
        parts = q_out.reshape(LAYERS, MEMBERS, d_rows, PACK // HEAD_DIM, HEAD_DIM)
        picks = [
            jnp.stack([parts[:, :, :, order.index((kind, head))] for head in range(LOCAL_HEADS)], axis=3)
            for kind in range(3)
        ]
        grad_qkv = jnp.stack(picks, axis=1).transpose(0, 1, 3, 2, 4, 5).reshape(w_qkv.shape)
        grad_up = u_out.reshape(LAYERS, 2, 2, d_rows, nz, ny, f_rows).transpose(0, 3, 4, 1, 5, 2, 6)
        narrow = s_out[:, :, :d_rows]
        grad_biases = jnp.stack([narrow[:, 15], narrow[:, 0], narrow[:, 1]], axis=1)
        return (
            output,
            grad_inputs,
            grad_qkv,
            o_out,
            grad_up.reshape(w_up.shape),
            d_out,
            grad_biases,
            narrow[:, 23],
            s_out[:, 30, :f_rows],
            narrow[:, 2:4],
            narrow[:, 4:6],
        )

    return run


def part_count(row_count):
    count = 1
    while row_count % count != 0 or row_count // count > 2048:
        count = count + 1
    return count


def exact_gelu(values):
    return jax.nn.gelu(values, approximate=False)


def normalize(values, gain, shift):
    centred = values - jnp.mean(values, axis=1, keepdims=True)
    inv_std = lax.rsqrt(jnp.mean(centred * centred, axis=1, keepdims=True) + 1e-12)
    scaled = centred * inv_std
    return (scaled * gain + shift, scaled, inv_std)


def norm_back(grad, scaled, inv_std, gain):
    weighted = grad * gain
    return (
        weighted
        - jnp.mean(weighted, axis=1, keepdims=True)
        - scaled * jnp.mean(weighted * scaled, axis=1, keepdims=True)
    ) * inv_std


def split_heads(seq_array, count):
    seq_count, width, unused = seq_array.shape
    return seq_array.reshape(seq_count, count, width // count, HEADS, HEAD_DIM).transpose(
        1, 0, 2, 3, 4
    )


def merge_heads(head_array):
    seq_count, unused, row_count, unused_dim = head_array.shape
    return head_array.transpose(0, 2, 1, 3).reshape(seq_count * row_count, HEADS * HEAD_DIM)


def attend_forward(queries, keys, values):
    seq_count, row_count, unused = queries.shape
    factor = HEAD_DIM ** (-0.5)
    query_heads = queries.reshape(seq_count, row_count, HEADS, HEAD_DIM)
    start_state = (
        jnp.full((seq_count, HEADS, row_count), -1e30, jnp.float32),
        jnp.zeros((seq_count, HEADS, row_count), jnp.float32),
        jnp.zeros((seq_count, HEADS, row_count, HEAD_DIM), jnp.float32),
    )
    piece = (
        lax.all_gather(keys, "ctx", axis=1, tiled=True),
        lax.all_gather(values, "ctx", axis=1, tiled=True),
    )
    count = part_count(piece[0].shape[1])

    def attend_advance(inner, parts):
        peak, totals, accum = inner
        key_part, value_part = parts
        scores = (
            jnp.einsum("sthd,skhd->shtk", query_heads, key_part, preferred_element_type=jnp.float32)
            * factor
        )
        new_peak = jnp.maximum(peak, jnp.max(scores, axis=3))
        decay = jnp.exp(peak - new_peak)
        weights = jnp.exp(scores - new_peak[..., None])
        totals = totals * decay + jnp.sum(weights, axis=3)
        accum = accum * decay[..., None] + jnp.einsum(
            "shtk,skhd->shtd",
            weights.astype(jnp.bfloat16),
            value_part,
            preferred_element_type=jnp.float32,
        )
        return ((new_peak, totals, accum), None)

    result, _ = lax.scan(
        attend_advance, start_state, (split_heads(piece[0], count), split_heads(piece[1], count))
    )
    peak, totals, accum = result
    mixed = merge_heads(accum / totals[..., None])
    return (mixed, peak + jnp.log(totals))


def query_fold(queries, grad_mixed, logsum, row_delta, keys, values):
    seq_count, row_count, unused = queries.shape
    factor = HEAD_DIM ** (-0.5)
    query_heads = queries.reshape(seq_count, row_count, HEADS, HEAD_DIM)
    grad_heads = grad_mixed.reshape(seq_count, row_count, HEADS, HEAD_DIM)
    start_state = jnp.zeros((seq_count, HEADS, row_count, HEAD_DIM), jnp.float32)
    piece = (
        lax.all_gather(keys, "ctx", axis=1, tiled=True),
        lax.all_gather(values, "ctx", axis=1, tiled=True),
    )
    count = part_count(piece[0].shape[1])

    def query_advance(totals, parts):
        key_part, value_part = parts
        scores = (
            jnp.einsum("sthd,skhd->shtk", query_heads, key_part, preferred_element_type=jnp.float32)
            * factor
        )
        weights = jnp.exp(scores - logsum[..., None])
        grad_weights = jnp.einsum(
            "sthd,skhd->shtk", grad_heads, value_part, preferred_element_type=jnp.float32
        )
        grad_scores = (weights * (grad_weights - row_delta[..., None])).astype(jnp.bfloat16)
        return (
            totals
            + jnp.einsum(
                "shtk,skhd->shtd", grad_scores, key_part, preferred_element_type=jnp.float32
            )
            * factor,
            None,
        )

    result, _ = lax.scan(
        query_advance, start_state, (split_heads(piece[0], count), split_heads(piece[1], count))
    )
    return result


def key_fold(queries, grad_mixed, keys, values, all_logsum, all_delta):
    seq_count, row_count, unused = keys.shape
    factor = HEAD_DIM ** (-0.5)
    key_heads = keys.reshape(seq_count, row_count, HEADS, HEAD_DIM)
    value_heads = values.reshape(seq_count, row_count, HEADS, HEAD_DIM)
    start_state = (
        jnp.zeros((seq_count, HEADS, row_count, HEAD_DIM), jnp.float32),
        jnp.zeros((seq_count, HEADS, row_count, HEAD_DIM), jnp.float32),
    )
    piece = (
        lax.all_gather(queries, "ctx", axis=1, tiled=True),
        lax.all_gather(grad_mixed, "ctx", axis=1, tiled=True),
    )
    width = piece[0].shape[1]
    count = part_count(width)
    block = width // count
    log_parts = all_logsum.reshape(seq_count, HEADS, count, block).transpose(2, 0, 1, 3)
    delta_parts = all_delta.reshape(seq_count, HEADS, count, block).transpose(2, 0, 1, 3)

    def key_advance(inner, parts):
        grad_keys, grad_values = inner
        query_part, grad_part, log_part, delta_part = parts
        scores = (
            jnp.einsum("sqhd,skhd->shqk", query_part, key_heads, preferred_element_type=jnp.float32)
            * factor
        )
        weights = jnp.exp(scores - log_part[..., None])
        grad_values = grad_values + jnp.einsum(
            "shqk,sqhd->shkd",
            weights.astype(jnp.bfloat16),
            grad_part,
            preferred_element_type=jnp.float32,
        )
        grad_weights = jnp.einsum(
            "sqhd,skhd->shqk", grad_part, value_heads, preferred_element_type=jnp.float32
        )
        grad_scores = (weights * (grad_weights - delta_part[..., None])).astype(jnp.bfloat16)
        grad_keys = (
            grad_keys
            + jnp.einsum(
                "shqk,sqhd->shkd", grad_scores, query_part, preferred_element_type=jnp.float32
            )
            * factor
        )
        return ((grad_keys, grad_values), None)

    result, _ = lax.scan(
        key_advance,
        start_state,
        (split_heads(piece[0], count), split_heads(piece[1], count), log_parts, delta_parts),
    )
    return result


def forward_layer(stream, full, seq_count):
    w_attn, w_mix, w_raise, w_lower, bias_rows, bias_value, bias_raise, gain_rows, shift_rows = full
    total_rows = stream.shape[0]
    rounded = stream.astype(jnp.bfloat16)
    projected = jnp.einsum("td,cde->cte", rounded, w_attn, preferred_element_type=jnp.float32)
    queries = (projected[0] + bias_rows[0].astype(jnp.float32)).astype(jnp.bfloat16)
    keys = projected[1].astype(jnp.bfloat16)
    values = (projected[2] + bias_value.astype(jnp.float32)).astype(jnp.bfloat16)
    seq_shape = (seq_count, total_rows // seq_count, D)
    mixed, logsum = attend_forward(
        queries.reshape(seq_shape), keys.reshape(seq_shape), values.reshape(seq_shape)
    )
    mixed_low = mixed.astype(jnp.bfloat16)
    branch = jnp.dot(mixed_low, w_mix, preferred_element_type=jnp.float32) + bias_rows[1].astype(
        jnp.float32
    )
    normed, scaled_one, inv_one = normalize(
        stream + branch, gain_rows[0].astype(jnp.float32), shift_rows[0].astype(jnp.float32)
    )
    normed_low = normed.astype(jnp.bfloat16)
    upward = jnp.dot(normed_low, w_raise, preferred_element_type=jnp.float32) + bias_raise.astype(
        jnp.float32
    )
    active = exact_gelu(upward).astype(jnp.bfloat16)
    lowered = jnp.dot(active, w_lower, preferred_element_type=jnp.float32) + bias_rows[2].astype(
        jnp.float32
    )
    result, scaled_two, inv_two = normalize(
        normed + lowered, gain_rows[1].astype(jnp.float32), shift_rows[1].astype(jnp.float32)
    )
    states = (
        rounded,
        queries,
        keys,
        values,
        mixed,
        mixed_low,
        logsum,
        scaled_one,
        inv_one,
        normed_low,
        upward,
        active,
        scaled_two,
        inv_two,
    )
    return (result, states)


def backward_layer(grad, full, states, seq_count):
    w_attn, w_mix, w_raise, w_lower, bias_rows, bias_value, bias_raise, gain_rows, shift_rows = full
    (
        rounded,
        queries,
        keys,
        values,
        mixed,
        mixed_low,
        logsum,
        scaled_one,
        inv_one,
        normed_low,
        upward,
        active,
        scaled_two,
        inv_two,
    ) = states
    total_rows = grad.shape[0]
    row_count = total_rows // seq_count
    seq_shape = (seq_count, row_count, D)
    grad_gain_two = jnp.sum(grad * scaled_two, axis=0)
    grad_shift_two = jnp.sum(grad, axis=0)
    grad_resid = norm_back(grad, scaled_two, inv_two, gain_rows[1].astype(jnp.float32))
    grad_lowered = grad_resid.astype(jnp.bfloat16)
    grad_w_lower = jnp.einsum("tf,td->fd", active, grad_lowered, preferred_element_type=jnp.float32)
    grad_active = jnp.einsum("td,fd->tf", grad_lowered, w_lower, preferred_element_type=jnp.float32)
    unused, gelu_back = jax.vjp(exact_gelu, upward)
    grad_upward = gelu_back(grad_active)[0].astype(jnp.bfloat16)
    grad_w_raise = jnp.einsum(
        "td,tf->df", normed_low, grad_upward, preferred_element_type=jnp.float32
    )
    grad_normed = (
        jnp.einsum("tf,df->td", grad_upward, w_raise, preferred_element_type=jnp.float32)
        + grad_resid
    )
    grad_gain_one = jnp.sum(grad_normed * scaled_one, axis=0)
    grad_shift_one = jnp.sum(grad_normed, axis=0)
    grad_inner = norm_back(grad_normed, scaled_one, inv_one, gain_rows[0].astype(jnp.float32))
    grad_branch = grad_inner.astype(jnp.bfloat16)
    grad_w_mix = jnp.einsum("td,te->de", mixed_low, grad_branch, preferred_element_type=jnp.float32)
    grad_mixed = jnp.einsum(
        "te,de->td", grad_branch, w_mix, preferred_element_type=jnp.float32
    ).astype(jnp.bfloat16)
    row_delta = jnp.sum(
        (grad_mixed.astype(jnp.float32) * mixed).reshape(seq_count, row_count, HEADS, HEAD_DIM),
        axis=3,
    ).transpose(0, 2, 1)
    seq_queries = queries.reshape(seq_shape)
    seq_keys = keys.reshape(seq_shape)
    seq_values = values.reshape(seq_shape)
    seq_grad_mixed = grad_mixed.reshape(seq_shape)
    grad_queries = query_fold(seq_queries, seq_grad_mixed, logsum, row_delta, seq_keys, seq_values)
    grad_queries = merge_heads(grad_queries).astype(jnp.bfloat16)
    all_logsum, all_delta = (
        lax.all_gather(logsum, "ctx", axis=2, tiled=True),
        lax.all_gather(row_delta, "ctx", axis=2, tiled=True),
    )
    grad_keys, grad_values = key_fold(
        seq_queries, seq_grad_mixed, seq_keys, seq_values, all_logsum, all_delta
    )
    grad_keys = merge_heads(grad_keys).astype(jnp.bfloat16)
    grad_values = merge_heads(grad_values).astype(jnp.bfloat16)
    grad_project = jnp.stack([grad_queries, grad_keys, grad_values])
    grad_w_attn = jnp.einsum(
        "td,cte->dce", rounded, grad_project, preferred_element_type=jnp.float32
    )
    grad_stream = (
        jnp.einsum("cte,cde->td", grad_project, w_attn, preferred_element_type=jnp.float32)
        + grad_inner
    )
    grad_bias_rows = jnp.stack(
        [
            jnp.sum(grad_queries.astype(jnp.float32), axis=0),
            jnp.sum(grad_branch.astype(jnp.float32), axis=0),
            jnp.sum(grad_lowered.astype(jnp.float32), axis=0),
        ],
        axis=1,
    )
    grad_bias_value = jnp.sum(grad_values.astype(jnp.float32), axis=0)
    grad_bias_raise = jnp.sum(grad_upward.astype(jnp.float32), axis=0)
    local_sums = (
        grad_w_attn,
        grad_w_mix,
        grad_w_raise,
        grad_w_lower,
        grad_bias_rows,
        grad_bias_value,
        grad_bias_raise,
        jnp.stack([grad_gain_one, grad_gain_two], axis=1),
        jnp.stack([grad_shift_one, grad_shift_two], axis=1),
    )
    return (grad_stream, local_sums)


def body(inputs, w_qkv, w_out, w_up, w_down, biases, value_bias, up_bias, gains, shifts, cotangent):
    stacked = (w_qkv, w_out, w_up, w_down, biases, value_bias, up_bias, gains, shifts)
    seq_count = inputs.shape[0]
    stream = inputs.reshape(-1, D).astype(jnp.float32)
    kept_states = []
    for layer in range(LAYERS):
        shards = tuple((array[layer] for array in stacked))
        full = (
            lax.all_gather(shards[0], ("ctx", "fsdp"), axis=1, tiled=True),
            lax.all_gather(shards[1], ("ctx", "fsdp"), axis=0, tiled=True),
            lax.all_gather(shards[2], ("ctx", "fsdp"), axis=0, tiled=True),
            lax.all_gather(shards[3], ("ctx", "fsdp"), axis=0, tiled=True),
            lax.all_gather(shards[4], ("ctx", "fsdp"), axis=1, tiled=True),
            lax.all_gather(shards[5], ("ctx", "fsdp"), axis=0, tiled=True),
            lax.all_gather(shards[6], ("ctx", "fsdp"), axis=0, tiled=True),
            lax.all_gather(shards[7], ("ctx", "fsdp"), axis=1, tiled=True),
            lax.all_gather(shards[8], ("ctx", "fsdp"), axis=1, tiled=True),
        )
        stream, states = forward_layer(stream, full, seq_count)
        kept_states.append(states)
    output = stream.astype(jnp.bfloat16).reshape(inputs.shape)
    grad = cotangent.reshape(-1, D).astype(jnp.float32)
    layer_grads = [None] * LAYERS
    for layer in reversed(range(LAYERS)):
        shards = tuple((array[layer] for array in stacked))
        full = (
            lax.all_gather(shards[0], ("ctx", "fsdp"), axis=1, tiled=True),
            lax.all_gather(shards[1], ("ctx", "fsdp"), axis=0, tiled=True),
            lax.all_gather(shards[2], ("ctx", "fsdp"), axis=0, tiled=True),
            lax.all_gather(shards[3], ("ctx", "fsdp"), axis=0, tiled=True),
            lax.all_gather(shards[4], ("ctx", "fsdp"), axis=1, tiled=True),
            lax.all_gather(shards[5], ("ctx", "fsdp"), axis=0, tiled=True),
            lax.all_gather(shards[6], ("ctx", "fsdp"), axis=0, tiled=True),
            lax.all_gather(shards[7], ("ctx", "fsdp"), axis=1, tiled=True),
            lax.all_gather(shards[8], ("ctx", "fsdp"), axis=1, tiled=True),
        )
        grad, local_sums = backward_layer(grad, full, kept_states[layer], seq_count)
        partial_sums = (
            lax.psum_scatter(local_sums[0], "ctx", scatter_dimension=0, tiled=True),
            lax.psum_scatter(local_sums[1], "ctx", scatter_dimension=0, tiled=True),
            lax.psum_scatter(local_sums[2], "ctx", scatter_dimension=0, tiled=True),
            lax.psum_scatter(local_sums[3], "ctx", scatter_dimension=0, tiled=True),
            lax.psum_scatter(local_sums[4], "ctx", scatter_dimension=0, tiled=True),
            lax.psum_scatter(local_sums[5], "ctx", scatter_dimension=0, tiled=True),
            lax.psum_scatter(local_sums[6], "ctx", scatter_dimension=0, tiled=True),
            lax.psum_scatter(local_sums[7], "ctx", scatter_dimension=0, tiled=True),
            lax.psum_scatter(local_sums[8], "ctx", scatter_dimension=0, tiled=True),
        )
        reduced = (
            lax.psum_scatter(
                partial_sums[0].astype(jnp.bfloat16), "fsdp", scatter_dimension=0, tiled=True
            ).astype(jnp.float32),
            lax.psum_scatter(
                partial_sums[1].astype(jnp.bfloat16), "fsdp", scatter_dimension=0, tiled=True
            ).astype(jnp.float32),
            lax.psum_scatter(
                partial_sums[2].astype(jnp.bfloat16), "fsdp", scatter_dimension=0, tiled=True
            ).astype(jnp.float32),
            lax.psum_scatter(
                partial_sums[3].astype(jnp.bfloat16), "fsdp", scatter_dimension=0, tiled=True
            ).astype(jnp.float32),
            lax.psum_scatter(
                partial_sums[4].astype(jnp.bfloat16), "fsdp", scatter_dimension=0, tiled=True
            ).astype(jnp.float32),
            lax.psum_scatter(
                partial_sums[5].astype(jnp.bfloat16), "fsdp", scatter_dimension=0, tiled=True
            ).astype(jnp.float32),
            lax.psum_scatter(
                partial_sums[6].astype(jnp.bfloat16), "fsdp", scatter_dimension=0, tiled=True
            ).astype(jnp.float32),
            lax.psum_scatter(
                partial_sums[7].astype(jnp.bfloat16), "fsdp", scatter_dimension=0, tiled=True
            ).astype(jnp.float32),
            lax.psum_scatter(
                partial_sums[8].astype(jnp.bfloat16), "fsdp", scatter_dimension=0, tiled=True
            ).astype(jnp.float32),
        )
        layer_grads[layer] = (
            reduced[0].transpose(1, 0, 2),
            reduced[1],
            reduced[2],
            reduced[3],
            reduced[4].T,
            reduced[5],
            reduced[6],
            reduced[7].T,
            reduced[8].T,
        )
    grad_inputs = grad.astype(jnp.bfloat16).reshape(inputs.shape)
    return (
        output,
        grad_inputs,
        jnp.stack([member[0] for member in layer_grads]),
        jnp.stack([member[1] for member in layer_grads]),
        jnp.stack([member[2] for member in layer_grads]),
        jnp.stack([member[3] for member in layer_grads]),
        jnp.stack([member[4] for member in layer_grads]),
        jnp.stack([member[5] for member in layer_grads]),
        jnp.stack([member[6] for member in layer_grads]),
        jnp.stack([member[7] for member in layer_grads]),
        jnp.stack([member[8] for member in layer_grads]),
    )


def one_group_per_sequence(mesh, seqs):
    return mesh.shape["fsdp"] == 4 and mesh.shape["ctx"] == seqs


def solution(mesh):
    def run(*arrays):
        seqs = arrays[0].shape[0]
        chosen = grouped(mesh.shape["ctx"] // 2, 2) if one_group_per_sequence(mesh, seqs) else body
        return on_devices(mesh, chosen)(*arrays)

    return run


def on_devices(mesh, chosen):
    return jax.shard_map(
        chosen,
        mesh=mesh,
        in_specs=(
            P("fsdp", "ctx", None),
            P(None, None, ("ctx", "fsdp"), None),
            P(None, ("ctx", "fsdp"), None),
            P(None, ("ctx", "fsdp"), None),
            P(None, ("ctx", "fsdp"), None),
            P(None, None, ("ctx", "fsdp")),
            P(None, ("ctx", "fsdp")),
            P(None, ("ctx", "fsdp")),
            P(None, None, ("ctx", "fsdp")),
            P(None, None, ("ctx", "fsdp")),
            P("fsdp", "ctx", None),
        ),
        out_specs=(
            P("fsdp", "ctx", None),
            P("fsdp", "ctx", None),
            P(None, None, ("ctx", "fsdp"), None),
            P(None, ("ctx", "fsdp"), None),
            P(None, ("ctx", "fsdp"), None),
            P(None, ("ctx", "fsdp"), None),
            P(None, None, ("ctx", "fsdp")),
            P(None, ("ctx", "fsdp")),
            P(None, ("ctx", "fsdp")),
            P(None, None, ("ctx", "fsdp")),
            P(None, None, ("ctx", "fsdp")),
        ),
        check_vma=False,
    )
```

```python
import functools
import types

import jax
import jax.numpy as jnp
from jax import lax
from jax.experimental import pallas as pl
from jax.experimental.pallas import tpu as pltpu
from jax.sharding import PartitionSpec as P

D = 768
HEADS = 12
HEAD_DIM = 64
LAYERS = 2
KERNEL_VMEM = 63 * 2**20


BF = jnp.bfloat16
F32 = jnp.float32
MESH = pl.DeviceIdType.MESH
MEMBERS = 4
LOCAL_HEADS = HEADS // MEMBERS
PACK = 640
SLOT = 64
PIECE = 64


def dot_nn(left, right):
    return lax.dot_general(left, right, (((1,), (0,)), ((), ())), preferred_element_type=F32)


def dot_nt(left, right):
    return lax.dot_general(left, right, (((1,), (1,)), ((), ())), preferred_element_type=F32)


def dot_tn(left, right):
    return lax.dot_general(left, right, (((0,), (0,)), ((), ())), preferred_element_type=F32)


def dot_exact(left, right):
    return lax.dot_general(
        left,
        right,
        (((1,), (0,)), ((), ())),
        precision=lax.Precision.HIGHEST,
        preferred_element_type=F32,
    )


def packed_lanes(shape, axis):
    lane = lax.broadcasted_iota(jnp.int32, shape, axis)
    slot = lane >> 6
    head = jnp.where(slot >= 6, 2, slot & 1)
    is_query = (slot < 2) | (slot == 6)
    is_value = (slot == 4) | (slot == 5) | (slot == 8)
    return (head * HEAD_DIM + (lane & 63), is_query, is_value)


def scratch_layout(nz, ny, rows, half, d_rows, f_rows):
    dma = pltpu.SemaphoreType.DMA
    two = 2 * d_rows
    ff = nz * ny * f_rows
    vm = pltpu.VMEM
    return dict(
        wq=vm((LAYERS, nz, 2, ny, two, PACK), BF),
        wu=vm((LAYERS, nz, 2, ny, two, ff), BF),
        wd=vm((LAYERS, nz, ny, f_rows, D), BF),
        wog=vm((nz, ny, two, D), BF),
        wo=vm((LAYERS, 256, D), BF),
        smg=vm((nz, ny, MEMBERS, 32, 128), BF),
        qi=vm((MEMBERS, two, PACK), BF),
        ui=vm((MEMBERS, two, ff), BF),
        oi=vm((two, D), BF),
        sf=vm((32, 128), F32),
        si=vm((32, 128), BF),
        qs=vm((MEMBERS, two, PACK), BF),
        us=vm((MEMBERS, two, ff), BF),
        pb=vm((16, D), F32),
        ub=vm((16, ff), F32),
        bq=vm((LAYERS, 8, PACK), F32),
        xf=vm((LAYERS, rows, D), BF),
        qkv=vm((LAYERS, rows, PACK), BF),
        prob=vm((LAYERS, LOCAL_HEADS, rows, rows), BF),
        mix=vm((LAYERS, rows, 256), F32),
        mixl=vm((LAYERS, rows, 256), BF),
        xh1=vm((LAYERS, half, D), F32),
        iv1=vm((LAYERS, half, 128), F32),
        nl=vm((LAYERS, rows, D), BF),
        gp=vm((LAYERS, rows, ff), F32),
        act=vm((LAYERS, rows, ff), BF),
        xh2=vm((LAYERS, half, D), F32),
        iv2=vm((LAYERS, half, 128), F32),
        stream=vm((half, D), F32),
        normed=vm((half, D), F32),
        ct=vm((half, D), BF),
        ownp=vm((half, D), F32),
        sibs=vm((2, half, D), BF),
        sibr=vm((2, half, D), BF),
        xs=vm((2, half, D), BF),
        xr=vm((2, half, D), BF),
        dl=vm((rows, D), BF),
        db=vm((rows, D), BF),
        du=vm((rows, ff), BF),
        dq=vm((rows, PACK), BF),
        dm=vm((rows, 256), BF),
        ds=vm((LOCAL_HEADS, rows, rows), BF),
        back=vm((2, half, D), BF),
        land=vm((2, 2, rows // (2 * nz), D), BF),
        gq=vm((LAYERS, nz, 2, ny, two, PACK), BF),
        gu=vm((LAYERS, nz, 2, ny, two, ff), BF),
        gd=vm((LAYERS, nz, ny, f_rows, D), BF),
        go=vm((LAYERS, nz, ny, 32, D), BF),
        ryq=vm((LAYERS, nz, 2, two, PACK), BF),
        ryu=vm((LAYERS, nz, 2, two, ff), BF),
        ryd=vm((nz, f_rows, D), BF),
        ryl=vm((f_rows, D), BF),
        syl=vm((f_rows, D), BF),
        ryo=vm((LAYERS, nz, 32, D), BF),
        rzq=vm((LAYERS, 4, 2, two, PACK), BF),
        rzu=vm((LAYERS, 4, 2, two, ff), BF),
        rzd=vm((4, f_rows, D), BF),
        rzl=vm((4, 2, f_rows, D), BF),
        rzo=vm((LAYERS, 4, 32, D), BF),
        fq=vm((LAYERS, 2, two, PACK), F32),
        fu=vm((LAYERS, 2, two, ff), F32),
        fo=vm((LAYERS, d_rows, D), F32),
        oq=vm((LAYERS, MEMBERS, d_rows, PACK), F32),
        ou=vm((LAYERS, MEMBERS, d_rows, ff), F32),
        oo=vm((LAYERS, d_rows, D), F32),
        sg=vm((LAYERS, 8, D), F32),
        sgy=vm((LAYERS, 8, D), F32),
        sgt=vm((LAYERS, 8, D), F32),
        sgz=vm((LAYERS, nz, 8, D), F32),
        sga=vm((LAYERS, MEMBERS, 8, D), F32),
        stage_s=dma((3, 3)),
        stage_r=dma((3, 3)),
        perm=dma((2,)),
        in_s=dma((4, 2)),
        in_r=dma((4, 2)),
        inx_s=dma((2, 2)),
        inx_r=dma((2, 2)),
        ins_s=dma((1,)),
        ins_r=dma((1,)),
        gz_s=dma((8, nz)),
        gz_r=dma((8, nz)),
        gy_s=dma((8, nz)),
        gy_r=dma((8, nz)),
        sib_s=dma((2, half // PIECE)),
        sib_r=dma((2, half // PIECE)),
        x_s=dma((2, half // PIECE)),
        x_r=dma((2, half // PIECE)),
        ag_s=dma((2, half // PIECE)),
        ag_r=dma((2, half // PIECE)),
        ry_s=dma((8,)),
        ry_r=dma((8,)),
        rz_s=dma((8, nz)),
        rz_r=dma((8, nz)),
        fin_s=dma((LAYERS, 2, 3)),
        fin_r=dma((LAYERS, 2, 3)),
        fino=dma((LAYERS, 2)),
        sgy_s=dma((LAYERS,)),
        sgy_r=dma((LAYERS,)),
        sgz_s=dma((LAYERS, nz)),
        sgz_r=dma((LAYERS, nz)),
        sga_s=dma((LAYERS, 3)),
        sga_r=dma((LAYERS, 3)),
    )


def group_kernel(layout, nz, *refs):
    inp, w_qkv, w_out, w_up, d_in, biases, value_bias, up_bias, gains, shifts, cot = refs[:11]
    out, gin, g_qkv, o_out, g_up, d_out, g_biases, g_value, g_raise, g_gains, g_shifts = refs[11:22]
    S = types.SimpleNamespace(**dict(zip(layout.keys(), refs[22:])))
    q_in, u_in, o_in, s_in = S.qi, S.ui, S.oi, S.si
    rows = S.dl.shape[0]
    half = rows // 2
    block = inp.shape[1]
    d_rows = w_out.shape[1]
    f_rows = d_in.shape[1]
    two = 2 * d_rows
    ff = S.du.shape[1]
    pieces = half // PIECE
    place = lax.axis_index("ctx")
    lane_f = lax.axis_index("fsdp")
    z, x = lax.div(place, 2), lax.rem(place, 2)
    y, c = lax.div(lane_f, 2), lax.rem(lane_f, 2)
    m = 2 * x + c
    d = 4 * place + lane_f
    devices = 8 * nz

    def dev(z_at, x_at, y_at, c_at):
        return (2 * z_at + x_at, 2 * y_at + c_at)

    def rcopy(source, target, send, recv, to):
        return pltpu.make_async_remote_copy(
            src_ref=source,
            dst_ref=target,
            send_sem=send,
            recv_sem=recv,
            device_id=to,
            device_id_type=MESH,
        )

    barrier = pltpu.get_barrier_semaphore()

    def hail(step, carry):
        other = lax.rem(d + step, devices)
        pl.semaphore_signal(
            barrier, inc=1, device_id=(lax.div(other, 4), lax.rem(other, 4)), device_id_type=MESH
        )
        return carry

    lax.fori_loop(1, devices, hail, 0)

    lane_low = lax.broadcasted_iota(jnp.int32, (1, 128), 1) < HEAD_DIM

    def turn(value):
        return pltpu.roll(value, HEAD_DIM, 1)

    def pack_heads(layer, pair):
        tiles = []
        for kind in range(3):
            base = 2 * pair * LOCAL_HEADS * HEAD_DIM
            whole = w_qkv[layer, kind, :, base : base + 384].astype(F32)
            tiles.append([whole[:, 0:128], whole[:, 128:256], whole[:, 256:384]])
        (q0, q1, q2), (k0, k1, k2), (v0, v1, v2) = tiles
        even = (q0, k0, v0, jnp.where(lane_low, q1, turn(k1)), jnp.where(lane_low, v1, 0.0))
        odd = (
            jnp.where(lane_low, turn(q1), turn(q2)),
            jnp.where(lane_low, turn(k1), turn(k2)),
            jnp.where(lane_low, turn(v1), turn(v2)),
            jnp.where(lane_low, turn(q2), k2),
            jnp.where(lane_low, turn(v2), 0.0),
        )
        return [jnp.concatenate(part, axis=1) for part in (even, odd)]

    for pair in range(2):
        packed = [pack_heads(layer, pair) for layer in range(LAYERS)]
        for odd in range(2):
            both = jnp.concatenate([part[odd] for part in packed], axis=0)
            q_in[2 * pair + odd] = both.astype(BF)

    def owner_block(z_at, x_at, y_at, c_at):
        at = (8 * z_at + 4 * x_at + 2 * y_at + c_at) * f_rows
        return slice(at, at + f_rows)

    grid_places = [(z_at, y_at) for z_at in range(nz) for y_at in range(2)]

    def pack_raise():
        wide = [w_up[layer].astype(F32) for layer in range(LAYERS)]
        for x_at in range(2):
            for c_at in range(2):
                both = [
                    jnp.concatenate(
                        [part[:, owner_block(z_at, x_at, y_at, c_at)] for z_at, y_at in grid_places], axis=1
                    )
                    for part in wide
                ]
                u_in[2 * x_at + c_at] = jnp.concatenate(both, axis=0).astype(BF)

    def pack_small():
        S.sf[...] = jnp.zeros_like(S.sf)
        for layer in range(LAYERS):
            base = 8 * layer
            S.sf[base : base + 3, 0:d_rows] = biases[layer].astype(F32)
            S.sf[base + 3 : base + 4, 0:d_rows] = value_bias[layer : layer + 1].astype(F32)
            S.sf[base + 4 : base + 6, 0:d_rows] = gains[layer].astype(F32)
            S.sf[base + 6 : base + 8, 0:d_rows] = shifts[layer].astype(F32)
            S.sf[16 + layer : 17 + layer, 0:f_rows] = up_bias[layer : layer + 1].astype(F32)
        s_in[...] = S.sf[...].astype(BF)

    pack_small()
    pack_raise()
    o_in[...] = jnp.concatenate([w_out[layer].astype(F32) for layer in range(LAYERS)], axis=0).astype(BF)
    pl.semaphore_wait(barrier, devices - 1)

    relation = ((x, 1 - c), (1 - x, c), (1 - x, 1 - c))
    sibling = dev(z, x, y, 1 - c)
    peer = dev(z, 1 - x, y, c)
    across = dev(z, x, 1 - y, c)

    def stage_copy(kind, r):
        x_r, c_r = relation[r]
        m_r = 2 * x_r + c_r
        source = (s_in, q_in.at[m_r], u_in.at[m_r])[kind]
        target = (S.smg.at[z, y, m], S.qs.at[m], S.us.at[m])[kind]
        return rcopy(source, target, S.stage_s.at[kind, r], S.stage_r.at[kind, r], dev(z, x_r, y, c_r))

    def stage_wait(kind, r):
        x_r, c_r = relation[r]
        m_r = 2 * x_r + c_r
        target = (S.smg.at[z, y, m_r], S.qs.at[m_r], S.us.at[m_r])[kind]
        rcopy(
            target, target, S.stage_s.at[kind, r], S.stage_r.at[kind, r], dev(z, x_r, y, c_r)
        ).wait_recv()

    for kind in (1, 0):
        for r in (1, 2, 0):
            stage_copy(kind, r).start()

    def own_block(j):
        return (2 * c + j == z) & (lax.div(z, 2) == c)

    def scatter_in(which, source, target, position):
        for j in range(2):
            copy = rcopy(
                source.at[j],
                target.at[pl.ds(position, block)],
                S.in_s.at[which, j],
                S.in_r.at[which, lax.rem(z, 2)],
                dev(2 * c + j, x, y, lax.div(z, 2)),
            )

            @pl.when(own_block(j))
            def _():
                target[pl.ds(position, block), :] = source[j]

            @pl.when(jnp.logical_not(own_block(j)))
            def _():
                copy.start()

    def scatter_in_wait(which, source, target, base):
        for k in range(2):

            @pl.when(2 * c + k != z)
            def _():
                spot = target.at[pl.ds(base + 2 * block * k, block)]
                rcopy(
                    spot, spot, S.in_s.at[which, 0], S.in_r.at[which, k], peer
                ).wait_recv()

    def scatter_in_drain(which, source, target):
        for j in range(2):

            @pl.when(jnp.logical_not(own_block(j)))
            def _():
                rcopy(
                    source.at[j], source.at[j], S.in_s.at[which, j], S.in_r.at[which, 0], peer
                ).wait_send()

    first = S.xf.at[0]
    scatter_in(0, inp, first, block * place)

    perm_to = dev(2 * x + y, lax.div(z, 2), c, lax.rem(z, 2))
    perm_stays = (2 * x + y == z) & (lax.div(z, 2) == x) & (c == y) & (lax.rem(z, 2) == c)
    perm_copy = rcopy(o_in, S.wog.at[2 * x + y, c], S.perm.at[0], S.perm.at[1], perm_to)

    @pl.when(perm_stays)
    def _():
        S.wog[z, y] = o_in[...]

    def start_perm():
        @pl.when(jnp.logical_not(perm_stays))
        def _():
            perm_copy.start()

    for r in (1, 2, 0):
        stage_copy(2, r).start()
    S.smg[z, y, m] = s_in[...]
    S.qs[m] = q_in[m]
    S.us[m] = u_in[m]
    for layer in range(LAYERS):
        S.wd[layer, z, y] = d_in[layer]

    def join(staged, target):
        for xx in range(2):
            first_part = staged[2 * xx].astype(F32)
            second_part = staged[2 * xx + 1].astype(F32)
            for layer in range(LAYERS):
                cut = slice(layer * d_rows, (layer + 1) * d_rows)
                target[layer, z, xx, y] = jnp.concatenate(
                    [first_part[cut], second_part[cut]], axis=0
                ).astype(BF)

    side = lax.div(z, 2)
    inner = (z == 1) | (z == 2)
    outer = jnp.logical_not(inner)
    near_in, near_out = 1 + side, 3 * side
    far_in, far_out = 2 - side, 3 * (1 - side)
    buddy = near_in + near_out - z

    def at_z(z_at):
        return dev(z_at, x, y, c)

    LAST = 7

    def slab(cls, z_at, y_at):
        return (
            lambda: S.smg.at[z_at, y_at],
            lambda: S.wq.at[0, z_at, :, y_at],
            lambda: S.wog.at[z_at, y_at],
            lambda: S.wu.at[0, z_at, :, y_at],
            lambda: S.wd.at[0, z_at, y_at],
            lambda: S.wq.at[1, z_at, :, y_at],
            lambda: S.wu.at[1, z_at, :, y_at],
            lambda: S.wd.at[1, z_at, y_at],
        )[cls]()

    def z_copy(cls, n, z_at, to):
        spot = S.wd.at[1, z_at] if cls == LAST else slab(cls, z_at, y)
        return rcopy(spot, spot, S.gz_s.at[cls, n], S.gz_r.at[cls, z_at], at_z(to))

    def y_copy(cls, z_at):
        spot = slab(cls, z_at, y)
        return rcopy(spot, spot, S.gy_s.at[cls, z_at], S.gy_r.at[cls, z_at], across)

    def gather_direct(cls):
        z_copy(cls, 0, z, buddy).start()
        z_copy(cls, 1, z, far_in).start()

    def gather_start(cls):
        if cls != LAST:
            gather_direct(cls)
        y_copy(cls, z).start()

    def gather_cross(cls):
        spot = slab(cls, z, 1 - y)
        rcopy(spot, spot, S.gy_s.at[cls, z], S.gy_r.at[cls, z], across).wait_recv()
        gather_direct(cls)

    def gather_take(cls, z_at, relay):
        z_copy(cls, 0, z_at, buddy).wait_recv()
        if relay is not None:
            z_copy(cls, relay, z_at, near_out).start()
        if cls != LAST:
            y_copy(cls, z_at).start()

    def gather_relay(cls):
        gather_take(cls, buddy, None)

        @pl.when(inner)
        def _():
            gather_take(cls, far_in, 2)
            gather_take(cls, far_out, 3)

    def gather_end(cls):
        @pl.when(outer)
        def _():
            gather_take(cls, far_in, None)
            gather_take(cls, far_out, None)

    def gather_wait(cls):
        if cls == LAST:
            return

        def one(t):
            spot = slab(cls, t, 1 - y)
            rcopy(spot, spot, S.gy_s.at[cls, t], S.gy_r.at[cls, t], across).wait_recv()

        for t in (z, buddy, far_in, far_out):
            one(t)

    def gather_drain(cls):
        z_copy(cls, 0, z, buddy).wait_send()
        z_copy(cls, 1, z, far_in).wait_send()

        @pl.when(inner)
        def _():
            z_copy(cls, 2, far_in, near_out).wait_send()
            z_copy(cls, 3, far_out, near_out).wait_send()

        def one(t, carry):
            y_copy(cls, t).wait_send()
            return carry

        if cls == LAST:
            one(z, 0)
        else:
            lax.fori_loop(0, nz, one, 0)

    for r in range(3):
        stage_wait(1, r)
    join(S.qs, S.wq)
    gather_start(1)
    for r in range(3):
        stage_wait(0, r)
    gather_start(0)

    def x_spots(target, base, mine):
        return [target.at[pl.ds(base + block * (2 * k + mine), block)] for k in range(2)]

    def swap_start(which, target, base):
        for k, spot in enumerate(x_spots(target, base, x)):
            rcopy(spot, spot, S.inx_s.at[which, k], S.inx_r.at[which, k], peer).start()

    def swap_wait(which, target, base):
        for k, spot in enumerate(x_spots(target, base, 1 - x)):
            rcopy(spot, spot, S.inx_s.at[which, k], S.inx_r.at[which, k], peer).wait_recv()
        for k, spot in enumerate(x_spots(target, base, x)):
            rcopy(spot, spot, S.inx_s.at[which, k], S.inx_r.at[which, k], peer).wait_send()

    mine = half * c
    theirs = half * (1 - c)
    scatter_in_wait(0, inp, first, mine + block * x)
    swap_start(0, first, mine)
    start_perm()
    for r in range(3):
        stage_wait(2, r)
    join(S.us, S.wu)
    gather_relay(1)
    gather_relay(0)
    swap_wait(0, first, mine)
    spot = first.at[pl.ds(mine, half)]
    rcopy(spot, spot, S.ins_s.at[0], S.ins_r.at[0], sibling).start()
    S.stream[...] = S.xf[0, pl.ds(mine, half), :].astype(F32)

    @pl.when(jnp.logical_not(perm_stays))
    def _():
        spot = S.wog.at[z, y]
        rcopy(spot, spot, S.perm.at[0], S.perm.at[1], peer).wait_recv()

    gather_start(2)
    gather_start(3)
    gather_end(1)
    gather_end(0)
    gather_relay(2)
    gather_wait(0)

    def small_params():
        row_shape = (devices * 16, D)
        lane = lax.broadcasted_iota(jnp.int32, (128, D), 0)
        col = lax.broadcasted_iota(jnp.int32, (128, D), 1)
        tile = jnp.where(lax.rem(col, d_rows) == lane, 1.0, 0.0).astype(BF)
        packs = S.smg[:, :, :, 0:16, :].reshape(devices * 16, 128)
        spread = dot_nn(packs, tile)
        owner_row = lax.broadcasted_iota(jnp.int32, row_shape, 0) >> 4
        zz = owner_row >> 3
        yy = (owner_row >> 2) & 1
        xx = (owner_row >> 1) & 1
        cc = owner_row & 1
        owner = zz * 8 + xx * 4 + yy * 2 + cc
        at = lax.div(lax.broadcasted_iota(jnp.int32, row_shape, 1), d_rows)
        spread = jnp.where(owner == at, spread, 0.0)
        S.pb[...] = jnp.sum(spread.reshape(devices, 16, D), axis=0)
        lane = lax.broadcasted_iota(jnp.int32, (128, ff), 0)
        col = lax.broadcasted_iota(jnp.int32, (128, ff), 1)
        tile = jnp.where(lax.rem(col, f_rows) == lane, 1.0, 0.0).astype(BF)
        packs = S.smg[:, :, m, 16:32, :].reshape(2 * nz * 16, 128)
        spread = dot_nn(packs, tile)
        row_shape = (2 * nz * 16, ff)
        owner = lax.broadcasted_iota(jnp.int32, row_shape, 0) >> 4
        at = lax.div(lax.broadcasted_iota(jnp.int32, row_shape, 1), f_rows)
        spread = jnp.where(owner == at, spread, 0.0)
        S.ub[...] = jnp.sum(spread.reshape(2 * nz, 16, ff), axis=0)
        source = lax.broadcasted_iota(jnp.int32, (D, PACK), 0)
        target, unused_q, unused_v = packed_lanes((D, PACK), 1)
        pick = jnp.where(source == target + m * (LOCAL_HEADS * HEAD_DIM), 1.0, 0.0).astype(BF)
        picked = dot_nn(S.pb[...].astype(BF), pick)
        unused, is_query, is_value = packed_lanes((1, PACK), 1)
        for layer in range(LAYERS):
            base = 8 * layer
            row = jnp.where(is_query, picked[base : base + 1], 0.0)
            row = jnp.where(is_value, picked[base + 3 : base + 4], row)
            S.bq[layer, 0:1, :] = row

    small_params()
    scatter_in(1, cot, S.ct, block * (2 * lax.rem(z, 2) + x))

    def param(layer, kind):
        return S.pb[8 * layer + kind : 8 * layer + kind + 1, :]

    def piece_rows(i):
        return pl.ds(i * PIECE if isinstance(i, int) else pl.multiple_of(i * PIECE, PIECE), PIECE)

    def own_rows(i):
        return pl.ds(pl.multiple_of(mine + i * PIECE, PIECE), PIECE)

    def other_rows(i):
        return pl.ds(pl.multiple_of(theirs + i * PIECE, PIECE), PIECE)

    every = slice(None)

    def load_both(ref, i, cols=every):
        return jnp.concatenate([ref[other_rows(i), cols], ref[own_rows(i), cols]], axis=0)

    def store_both(ref, i, value, cols=every):
        ref[other_rows(i), cols] = value[:PIECE]
        ref[own_rows(i), cols] = value[PIECE:]

    def spread_start(par, i, ref, value):
        ref[own_rows(i), :] = value
        spot = ref.at[own_rows(i)]
        rcopy(spot, spot, S.ag_s.at[par, i], S.ag_r.at[par, i], sibling).start()

    def spread_wait(par, i, ref):
        got = ref.at[other_rows(i)]
        sent = ref.at[own_rows(i)]
        rcopy(got, got, S.ag_s.at[par, i], S.ag_r.at[par, i], sibling).wait_recv()
        rcopy(sent, sent, S.ag_s.at[par, i], S.ag_r.at[par, i], sibling).wait_send()

    def sib_copy(par, i):
        at = piece_rows(i)
        return rcopy(
            S.sibs.at[par, at], S.sibr.at[par, at], S.sib_s.at[par, i], S.sib_r.at[par, i], sibling
        )

    def peer_copy(par, i):
        at = piece_rows(i)
        return rcopy(S.xs.at[par, at], S.xr.at[par, at], S.x_s.at[par, i], S.x_r.at[par, i], peer)

    def part_send(par, i, value):
        at = piece_rows(i)
        S.sibs[par, at, :] = value[:PIECE].astype(BF)
        sib_copy(par, i).start()
        S.ownp[at, :] = value[PIECE:]

    def part_pass(par, i):
        at = piece_rows(i)
        sib_copy(par, i).wait_recv()
        S.xs[par, at, :] = (S.ownp[at, :] + S.sibr[par, at, :].astype(F32)).astype(BF)
        peer_copy(par, i).start()

    def part_take(par, i):
        at = piece_rows(i)
        peer_copy(par, i).wait_recv()
        return S.xs[par, at, :].astype(F32) + S.xr[par, at, :].astype(F32)

    def part_drain(par):
        for i in range(pieces):
            sib_copy(par, i).wait_send()
            peer_copy(par, i).wait_send()

    def pipeline(stages, between=None):
        for step in range(pieces + len(stages) - 1):
            for lag, stage in enumerate(stages):
                if 0 <= step - lag < pieces:
                    stage(step - lag)
            for call in (between or {}).get(step, ()):
                call()

    def norm_piece(total, at, layer, gain, shift, scaled_ref, inv_ref):
        centred = total - jnp.mean(total, axis=1, keepdims=True)
        inv = lax.rsqrt(jnp.mean(centred * centred, axis=1, keepdims=True) + 1e-12)
        scaled = centred * inv
        scaled_ref[layer, at, :] = scaled
        inv_ref[layer, at, :] = jnp.broadcast_to(inv, (PIECE, 128))
        return scaled * gain + shift

    def flat(value):
        return value.reshape(-1, value.shape[-1])

    def swap_lanes(value):
        return pltpu.roll(value.astype(F32), HEAD_DIM, 1).astype(BF)

    def mask_queries(queries, h):
        keep = jnp.logical_not(lane_low) if h == 1 else lane_low
        return jnp.where(keep, queries * jnp.asarray(HEAD_DIM**-0.5, BF), jnp.zeros((), BF))

    def query_cols(h):
        return slice(0, 128) if h < 2 else slice(384, 512)

    def head_keys(layer, h):
        if h < 2:
            return S.qkv[layer, :, 128:256]
        return swap_lanes(S.qkv[layer, :, 384:512])

    def head_values(layer, h):
        return S.qkv[layer, :, 256:384] if h < 2 else S.qkv[layer, :, 512:640]

    def project(layer, i):
        value = dot_nn(load_both(S.xf.at[layer], i), flat(S.wq[layer])) + S.bq[layer, 0:1, :]
        store_both(S.qkv.at[layer], i, value.astype(BF))

    def attend(layer, i):
        mixes = []
        for h in range(LOCAL_HEADS):
            queries = mask_queries(load_both(S.qkv.at[layer], i, query_cols(h)), h)
            scores = dot_nt(queries, head_keys(layer, h))
            weights = jnp.exp(scores - jnp.max(scores, axis=1, keepdims=True))
            weights = (weights * (1.0 / jnp.sum(weights, axis=1, keepdims=True))).astype(BF)
            store_both(S.prob.at[layer, h], i, weights)
            mixes.append(dot_nn(weights, head_values(layer, h)))
        mix = jnp.concatenate(
            [jnp.where(lane_low, mixes[0], mixes[1]), jnp.where(lane_low, mixes[2], 0.0)], axis=1
        )
        store_both(S.mix.at[layer], i, mix)
        store_both(S.mixl.at[layer], i, mix.astype(BF))
        part_send(0, i, dot_nn(mix.astype(BF), S.wo[layer]))

    def after_attention(layer, i):
        at = piece_rows(i)
        total = S.stream[at, :] + part_take(0, i) + param(layer, 1)
        normed = norm_piece(total, at, layer, param(layer, 4), param(layer, 6), S.xh1, S.iv1)
        S.normed[at, :] = normed
        spread_start(0, i, S.nl.at[layer], normed.astype(BF))

    def raise_part(layer, i):
        spread_wait(0, i, S.nl.at[layer])
        rounded = load_both(S.nl.at[layer], i)
        upward = dot_nn(rounded, flat(S.wu[layer])) + S.ub[layer : layer + 1, :]
        cdf = 0.5 * (1.0 + lax.erf(upward * (0.5**0.5)))
        density = jnp.exp(-0.5 * upward * upward) * ((2.0 * jnp.pi) ** -0.5)
        store_both(S.act.at[layer], i, (upward * cdf).astype(BF))
        store_both(S.gp.at[layer], i, cdf + upward * density)

    def lower_part(layer, i):
        part_send(1, i, dot_nn(load_both(S.act.at[layer], i), flat(S.wd[layer])))

    def after_lower(layer, i):
        at = piece_rows(i)
        total = S.normed[at, :] + part_take(1, i) + param(layer, 2)
        result = norm_piece(total, at, layer, param(layer, 5), param(layer, 7), S.xh2, S.iv2)
        if layer < LAYERS - 1:
            S.stream[at, :] = result
            spread_start(1, i, S.xf.at[layer + 1], result.astype(BF))
        else:
            S.back[0, at, :] = result.astype(BF)

    def next_project(layer, i):
        spread_wait(1, i, S.xf.at[layer])
        project(layer, i)

    def scatter_out(which, source):
        for k in range(2):
            stays = (2 * c + k == z) & (lax.div(z, 2) == c)
            spot = source.at[pl.ds(pl.multiple_of(block * (2 * k + x), block), block)]
            slot = lax.rem(z, 2)

            @pl.when(stays)
            def _():
                S.land[which, slot] = spot[...]

            @pl.when(jnp.logical_not(stays))
            def _():
                rcopy(
                    spot,
                    S.land.at[which, slot],
                    S.in_s.at[2 + which, k],
                    S.in_r.at[2 + which, slot],
                    dev(2 * c + k, x, y, lax.div(z, 2)),
                ).start()

    def scatter_out_wait(which, source, result):
        for k in range(2):
            spot = source.at[pl.ds(pl.multiple_of(block * (2 * k + x), block), block)]

            @pl.when(jnp.logical_not((2 * c + k == z) & (lax.div(z, 2) == c)))
            def _():
                rcopy(
                    spot, spot, S.in_s.at[2 + which, k], S.in_r.at[2 + which, 0], peer
                ).wait_send()

            @pl.when(jnp.logical_not(own_block(k)))
            def _():
                landed = S.land.at[which, k]
                rcopy(
                    landed, landed, S.in_s.at[2 + which, 0], S.in_r.at[2 + which, k], peer
                ).wait_recv()

        result[...] = S.land[which]

    def out_weights():
        gather_wait(2)
        for layer in range(LAYERS):
            cut = slice(layer * d_rows, (layer + 1) * d_rows)
            parts = [S.wog[t, yy].astype(F32)[cut] for t in range(nz) for yy in range(2)]
            parts.append(jnp.zeros((256 - 2 * nz * d_rows, D), F32))
            S.wo[layer] = jnp.concatenate(parts, axis=0).astype(BF)

    spot = first.at[pl.ds(theirs, half)]
    rcopy(spot, spot, S.ins_s.at[0], S.ins_r.at[0], sibling).wait_recv()
    gather_wait(1)
    for i in range(pieces):
        project(0, i)
    gather_end(2)
    gather_start(4)
    out_weights()
    pipeline(
        (lambda i: attend(0, i), lambda i: part_pass(0, i)),
        {1: [lambda: gather_relay(3)], 3: [lambda: gather_start(5)]},
    )
    gather_end(3)
    pipeline((lambda i: after_attention(0, i),))
    part_drain(0)
    gather_relay(4)
    gather_start(6)
    gather_wait(3)
    pipeline((lambda i: raise_part(0, i),))
    scatter_in_wait(1, cot, S.ct, block * x)
    gather_end(4)
    gather_relay(5)
    gather_start(7)
    gather_wait(4)
    pipeline((lambda i: lower_part(0, i), lambda i: part_pass(1, i)))
    swap_start(1, S.ct, 0)
    gather_end(5)
    gather_relay(6)
    gather_cross(7)
    gather_wait(5)
    pipeline(
        (lambda i: after_lower(0, i), lambda i: next_project(1, i)),
        {3: [lambda: gather_end(6)]},
    )
    part_drain(1)
    pipeline(
        (lambda i: attend(1, i), lambda i: part_pass(0, i)),
        {2: [lambda: gather_relay(7)]},
    )
    gather_wait(6)
    pipeline(
        (lambda i: after_attention(1, i), lambda i: raise_part(1, i)),
    )
    gather_end(7)
    pipeline((lambda i: lower_part(1, i), lambda i: part_pass(1, i)))
    part_drain(0)
    swap_wait(1, S.ct, 0)
    pipeline((lambda i: after_lower(1, i),))
    part_drain(1)
    scatter_out(0, S.back.at[0])

    S.sg[...] = jnp.zeros_like(S.sg)

    def add_row(layer, kind, value):
        S.sg[layer, kind : kind + 1, :] += jnp.sum(value, axis=0, keepdims=True)

    def norm_back_piece(grad, at, layer, which):
        scaled = (S.xh1 if which == 0 else S.xh2)[layer, at, :]
        inv = (S.iv1 if which == 0 else S.iv2)[layer, at, 0:1]
        add_row(layer, 2 + which, grad * scaled)
        add_row(layer, 4 + which, grad)
        weighted = grad * param(layer, 4 + which)
        back = (
            weighted
            - jnp.mean(weighted, axis=1, keepdims=True)
            - scaled * jnp.mean(weighted * scaled, axis=1, keepdims=True)
        ) * inv
        return back

    def lower_back(layer, i, grad):
        at = piece_rows(i)
        back = norm_back_piece(grad, at, layer, 1)
        S.normed[at, :] = back
        rounded = back.astype(BF)
        add_row(layer, 1, rounded.astype(F32))
        spread_start(0, i, S.dl, rounded)

    def raise_back(layer, i):
        spread_wait(0, i, S.dl)
        back = dot_nt(load_both(S.dl, i), flat(S.wd[layer])) * load_both(S.gp.at[layer], i)
        rounded = back.astype(BF)
        store_both(S.du, i, rounded)
        add_row(layer, 6, rounded.astype(F32))
        part_send(0, i, dot_nt(rounded, flat(S.wu[layer])))

    grads = (S.gq, S.gu, S.gd, S.go)
    from_y = (S.ryq, S.ryu, None, S.ryo)
    from_z = (S.rzq, S.rzu, None, S.rzo)

    def grad_slab(layer, kind, t, y_at):
        ref = grads[kind]
        return ref.at[layer, t, :, y_at] if kind < 2 else ref.at[layer, t, y_at]

    def z_first(layer, kind):
        return kind == 2 and layer == LAYERS - 1

    def z_slab(layer, kind, t):
        return S.gd.at[layer, t] if z_first(layer, kind) else grad_slab(layer, kind, t, y)

    def y_landing(layer, kind):
        if kind == 2:
            return S.ryl if z_first(layer, kind) else S.ryd
        return from_y[kind].at[layer]

    def z_landing(layer, kind, slot):
        if kind == 2:
            return (S.rzl if z_first(layer, kind) else S.rzd).at[slot]
        return from_z[kind].at[layer, slot]

    def reduce_y_copy(layer, kind):
        ref = grads[kind]
        if z_first(layer, kind):
            source = S.syl
        else:
            source = ref.at[layer, :, :, 1 - y] if kind < 2 else ref.at[layer, :, 1 - y]
        n = 4 * layer + kind
        return rcopy(source, y_landing(layer, kind), S.ry_s.at[n], S.ry_r.at[n], across)

    def reduce_z_copy(layer, kind, t, slot, to):
        n = 4 * layer + kind
        return rcopy(
            z_slab(layer, kind, t),
            z_landing(layer, kind, slot),
            S.rz_s.at[n, t],
            S.rz_r.at[n, slot],
            at_z(to),
        )

    def slab_add(target, other):
        if len(target.shape) == 3:
            for xx in range(2):
                target[xx] = (target[xx].astype(F32) + other[xx].astype(F32)).astype(BF)
        else:
            target[...] = (target[...].astype(F32) + other[...].astype(F32)).astype(BF)

    def reduce_direct(layer, kind):
        @pl.when(outer)
        def _():
            reduce_z_copy(layer, kind, far_in, 2, buddy).start()
            reduce_z_copy(layer, kind, far_out, 3, buddy).start()

        reduce_z_copy(layer, kind, buddy, 0, buddy).start()

    def reduce_start(layer, kind):
        if z_first(layer, kind):
            reduce_direct(layer, kind)
        else:
            reduce_y_copy(layer, kind).start()

    def reduce_first(layer, kind):
        reduce_y_copy(layer, kind).wait_recv()

        def one(t, carry):
            slab_add(grad_slab(layer, kind, t, y), y_landing(layer, kind).at[t])
            return carry

        lax.fori_loop(0, nz, one, 0)
        reduce_direct(layer, kind)

    def reduce_relay(layer, kind):
        @pl.when(inner)
        def _():
            for slot, t in ((2, far_in), (3, far_out)):
                reduce_z_copy(layer, kind, t, slot, buddy).wait_recv()
                slab_add(z_slab(layer, kind, t), z_landing(layer, kind, slot))
                reduce_z_copy(layer, kind, t, 1, t).start()

    def reduce_cross(layer):
        d_out[layer] = S.gd[layer, z, y].astype(F32)
        other = S.gd[layer, z, 1 - y].astype(F32)
        for slot in (0, 1):
            reduce_z_copy(layer, 2, z, slot, buddy).wait_recv()
            d_out[layer] += S.rzl[slot, y].astype(F32)
            other = other + S.rzl[slot, 1 - y].astype(F32)
        S.syl[...] = other.astype(BF)
        reduce_y_copy(layer, 2).start()

    def reduce_last_d(layer):
        reduce_y_copy(layer, 2).wait_recv()
        d_out[layer] += S.ryl[...].astype(F32)

    final = (S.fq, S.fu, d_out, S.fo)

    def reduce_last(layer, kind):
        if kind == 3:
            target = S.fo.at[layer]
            cut = lambda value: value[0:d_rows]
        else:
            target = final[kind].at[layer]
            cut = lambda value: value
        target[...] = cut(grad_slab(layer, kind, z, y)[...].astype(F32))

        for slot in (0, 1):
            reduce_z_copy(layer, kind, z, slot, buddy).wait_recv()
            target[...] += cut(z_landing(layer, kind, slot)[...].astype(F32))

        if kind < 2:
            result = (S.oq, S.ou)[kind]
            for r in (1, 2, 0):
                hand_copy(layer, kind, r).start()
            for xx in range(2):
                for cc in range(2):

                    @pl.when((x == xx) & (c == cc))
                    def _():
                        result[layer, 2 * xx + cc] = target[xx, cc * d_rows : (cc + 1) * d_rows, :]

        if kind == 3:
            @pl.when(owner_stays)
            def _():
                S.oo[layer] = target[...]

            @pl.when(jnp.logical_not(owner_stays))
            def _():
                owner_copy(layer).start()

    def hand_copy(layer, kind, r):
        x_r, c_r = relation[r]
        source = (S.fq, S.fu)[kind].at[
            layer, x_r, pl.ds(pl.multiple_of(c_r * d_rows, 8), d_rows)
        ]
        target = (S.oq, S.ou)[kind].at[layer, m]
        return rcopy(
            source,
            target,
            S.fin_s.at[layer, kind, r],
            S.fin_r.at[layer, kind, r],
            dev(z, x_r, y, c_r),
        )

    owner_to = dev(2 * x + c, lax.div(z, 2), lax.rem(z, 2), y)
    owner_stays = (2 * x + c == z) & (lax.div(z, 2) == x) & (lax.rem(z, 2) == y) & (y == c)

    def owner_copy(layer):
        return rcopy(
            S.fo.at[layer], S.oo.at[layer], S.fino.at[layer, 0], S.fino.at[layer, 1], owner_to
        )

    def reduce_drain(layer, kind):
        reduce_y_copy(layer, kind).wait_send()
        for t in range(nz):

            @pl.when(z != t)
            def _():
                reduce_z_copy(layer, kind, t, 0, buddy).wait_send()

        if kind < 2:
            for r in range(3):
                hand_copy(layer, kind, r).wait_send()
        if kind == 3:
            @pl.when(jnp.logical_not(owner_stays))
            def _():
                owner_copy(layer).wait_send()
                owner_copy(layer).wait_recv()

    def lower_grad(layer):
        for i in range(2):
            value = dot_tn(S.act[layer, :, i * (ff // 2) : (i + 1) * (ff // 2)], S.dl[...])
            S.gd[layer, i * (nz // 2) : (i + 1) * (nz // 2)] = value.astype(BF).reshape(
                nz // 2, 2, f_rows, D
            )
        reduce_start(layer, 2)

    def raise_grad(layer):
        for i in range(2):
            value = dot_tn(S.nl[layer, :, i * (D // 2) : (i + 1) * (D // 2)], S.du[...])
            S.gu[layer, i * (nz // 2) : (i + 1) * (nz // 2)] = value.astype(BF).reshape(
                nz // 2, 2, 2, two, ff
            )
        reduce_start(layer, 1)

    def out_grad(layer):
        value = dot_tn(S.mixl[layer], S.db[...])
        empty = jnp.zeros((32 - d_rows, D), F32)
        for t in range(nz):
            for yy in range(2):
                at = (2 * t + yy) * d_rows
                S.go[layer, t, yy] = jnp.concatenate(
                    [value[at : at + d_rows], empty], axis=0
                ).astype(BF)
        reduce_start(layer, 3)

    def project_grad(layer):
        for i in range(2):
            value = dot_tn(S.xf[layer, :, i * (D // 2) : (i + 1) * (D // 2)], S.dq[...])
            S.gq[layer, i * (nz // 2) : (i + 1) * (nz // 2)] = value.astype(BF).reshape(
                nz // 2, 2, 2, two, PACK
            )
        reduce_start(layer, 0)

    def branch_back(layer, i):
        at = piece_rows(i)
        back = norm_back_piece(part_take(0, i) + S.normed[at, :], at, layer, 0)
        S.stream[at, :] = back
        rounded = back.astype(BF)
        add_row(layer, 0, rounded.astype(F32))
        spread_start(1, i, S.db, rounded)

    scale = HEAD_DIM**-0.5

    def attend_back(layer, i):
        spread_wait(1, i, S.db)
        grad_mix = dot_nt(load_both(S.db, i), S.wo[layer]).astype(BF)
        store_both(S.dm, i, grad_mix)
        mix = load_both(S.mix.at[layer], i)
        results = []
        for h in range(LOCAL_HEADS):
            keep = jnp.logical_not(lane_low) if h == 1 else lane_low
            cols = slice(0, 128) if h < 2 else slice(128, 256)
            grad = jnp.where(keep, grad_mix[:, cols], jnp.zeros((), BF))
            delta = jnp.sum(grad.astype(F32) * mix[:, cols], axis=1, keepdims=True)
            grad_weights = dot_nt(grad, head_values(layer, h))
            weights = load_both(S.prob.at[layer, h], i).astype(F32)
            rounded = (weights * (grad_weights - delta)).astype(BF)
            store_both(S.ds.at[h], i, rounded)
            results.append((dot_nn(rounded, head_keys(layer, h)) * scale).astype(BF))
        store_both(S.dq, i, jnp.where(lane_low, results[0], results[1]), slice(0, 128))
        store_both(S.dq, i, results[2], slice(384, 512))

    def attend_back_end(layer):
        keys_back, values_back = [], []
        for h in range(LOCAL_HEADS):
            cols = slice(0, 128) if h < 2 else slice(128, 256)
            queries = mask_queries(S.qkv[layer, :, query_cols(h)], h)
            keys_back.append(dot_tn(S.ds[h], queries).astype(BF))
            values_back.append(dot_tn(S.prob[layer, h], S.dm[:, cols]).astype(BF))
        S.dq[:, 128:256] = jnp.where(lane_low, keys_back[0], keys_back[1])
        S.dq[:, 256:384] = jnp.where(lane_low, values_back[0], values_back[1])
        S.dq[:, 384:512] = jnp.where(lane_low, S.dq[:, 384:512], swap_lanes(keys_back[2]))
        S.dq[:, 512:640] = jnp.where(lane_low, values_back[2], jnp.zeros((), BF))
        S.sg[layer, 7:8, 0:PACK] = jnp.sum(S.dq[...].astype(F32), axis=0, keepdims=True)

    def project_back(layer, i):
        part_send(1, i, dot_nt(load_both(S.dq, i), flat(S.wq[layer])))

    def next_back(layer, i):
        at = piece_rows(i)
        grad = part_take(1, i) + S.stream[at, :]
        if layer > 0:
            lower_back(layer - 1, i, grad)
        else:
            S.back[1, at, :] = grad.astype(BF)

    def small_y(layer):
        return rcopy(S.sg.at[layer], S.sgy.at[layer], S.sgy_s.at[layer], S.sgy_r.at[layer], across)

    def small_z(layer, k):
        to = dev(lax.rem(z + k, nz), x, y, c)
        return rcopy(
            S.sgt.at[layer], S.sgz.at[layer, k], S.sgz_s.at[layer, k], S.sgz_r.at[layer, k], to
        )

    def small_member(layer, r):
        x_r, c_r = relation[r]
        return rcopy(
            S.sgt.at[layer],
            S.sga.at[layer, m],
            S.sga_s.at[layer, r],
            S.sga_r.at[layer, r],
            dev(z, x_r, y, c_r),
        )

    def small_one(layer):
        small_y(layer).start()

    def small_two(layer):
        small_y(layer).wait_recv()
        S.sgt[layer] = S.sg[layer] + S.sgy[layer]
        for k in range(1, nz):
            small_z(layer, k).start()

    def small_three(layer):
        for k in range(1, nz):
            small_z(layer, k).wait_recv()
        for k in range(1, nz):
            small_z(layer, k).wait_send()
        total = S.sgt[layer]
        for k in range(1, nz):
            total = total + S.sgz[layer, k]
        S.sgt[layer] = total
        for r in range(3):
            small_member(layer, r).start()
        S.sga[layer, m] = total

    def small_four(layer):
        for r in range(3):
            small_member(layer, r).wait_send()
            small_member(layer, r).wait_recv()
        small_y(layer).wait_send()
        lane = lax.broadcasted_iota(jnp.int32, (D, 128), 1)
        col = lax.broadcasted_iota(jnp.int32, (D, 128), 0)
        narrow = lane < d_rows
        pick = jnp.where((col == d_rows * d + lane) & narrow, 1.0, 0.0)
        both = S.sga[layer, 2 * x] + S.sga[layer, 2 * x + 1]
        found = dot_exact(both, pick)[:, 0:d_rows]
        g_biases[layer, 1:3, :] = found[0:2]
        g_gains[layer] = found[2:4]
        g_shifts[layer] = found[4:6]
        dim, is_query, is_value = packed_lanes((D, 128), 0)
        hit = (dim == d_rows * (d - 8 * z) + lane) & narrow
        attn = S.sga[layer, z]
        found = dot_exact(attn, jnp.where(hit & is_query, 1.0, 0.0))
        g_biases[layer, 0:1, :] = found[7:8, 0:d_rows]
        found = dot_exact(attn, jnp.where(hit & is_value, 1.0, 0.0))
        g_value[layer : layer + 1, :] = found[7:8, 0:d_rows]
        pick = jnp.where((col == f_rows * (2 * z + y) + lane) & (lane < f_rows), 1.0, 0.0)
        found = dot_exact(S.sga[layer, m], pick)
        g_raise[layer : layer + 1, :] = found[6:7, 0:f_rows]

    def hand_wait(layer, kind):
        for r in range(3):
            hand_copy(layer, kind, r).wait_recv()

    def unpack_heads(layer):
        hand_wait(layer, 0)
        for pair in range(2):
            even = [S.oq[layer, 2 * pair, :, 128 * t : 128 * t + 128] for t in range(5)]
            odd = [S.oq[layer, 2 * pair + 1, :, 128 * t : 128 * t + 128] for t in range(5)]
            thirds = (
                (even[3], turn(odd[3])),
                (turn(even[3]), odd[3]),
                (even[4], turn(odd[4])),
            )
            for kind in range(3):
                turned = turn(odd[kind])
                tiles = [
                    even[kind],
                    jnp.where(lane_low, thirds[kind][0], turned),
                    jnp.where(lane_low, turned, thirds[kind][1]),
                ]
                base = 384 * pair
                g_qkv[layer, kind, :, base : base + 384] = jnp.concatenate(tiles, axis=1)

    def unpack_raise(layer):
        hand_wait(layer, 1)
        wide = [S.ou[layer, member] for member in range(MEMBERS)]
        parts = []
        for z_at in range(nz):
            for x_at in range(2):
                for y_at in range(2):
                    for c_at in range(2):
                        at = (2 * z_at + y_at) * f_rows
                        parts.append(wide[2 * x_at + c_at][:, at : at + f_rows])
        g_up[layer] = jnp.concatenate(parts, axis=1)

    pipeline(
        (
            lambda i: lower_back(1, i, S.ct[piece_rows(i), :].astype(F32)),
            lambda i: raise_back(1, i),
            lambda i: part_pass(0, i),
        ),
        {4: [lambda: lower_grad(1)]},
    )
    raise_grad(1)
    pipeline((lambda i: branch_back(1, i), lambda i: attend_back(1, i)))
    part_drain(0)
    attend_back_end(1)
    pipeline((lambda i: project_back(1, i), lambda i: part_pass(1, i)))
    small_one(1)
    project_grad(1)
    out_grad(1)
    reduce_first(1, 1)
    pipeline(
        (
            lambda i: next_back(1, i),
            lambda i: raise_back(0, i),
            lambda i: part_pass(0, i),
        ),
        {1: [lambda: reduce_relay(1, 2)], 4: [lambda: lower_grad(0)]},
    )
    part_drain(1)
    reduce_first(1, 0)
    raise_grad(0)
    pipeline(
        (lambda i: branch_back(0, i), lambda i: attend_back(0, i)),
        {1: [lambda: reduce_relay(1, 1)], 3: [lambda: reduce_first(1, 3)]},
    )
    part_drain(0)
    attend_back_end(0)
    reduce_cross(1)
    small_one(0)
    pipeline((lambda i: project_back(0, i), lambda i: part_pass(1, i)))
    project_grad(0)
    out_grad(0)
    reduce_relay(1, 0)
    small_two(1)
    pipeline((lambda i: next_back(0, i),), {1: [lambda: reduce_relay(1, 3)]})
    part_drain(1)
    scatter_out(1, S.back.at[1])
    reduce_first(0, 2)
    small_three(1)
    reduce_last(1, 1)
    reduce_last(1, 0)
    reduce_first(0, 1)
    reduce_relay(0, 2)
    reduce_last(1, 3)
    small_two(0)
    reduce_last_d(1)
    small_four(1)
    reduce_first(0, 0)
    reduce_relay(0, 1)
    small_three(0)
    reduce_first(0, 3)
    reduce_last(0, 2)
    reduce_relay(0, 0)
    reduce_last(0, 1)
    reduce_relay(0, 3)
    small_four(0)
    unpack_heads(1)
    unpack_raise(1)
    reduce_last(0, 0)
    reduce_last(0, 3)

    for kind in range(3):
        for r in range(3):
            stage_copy(kind, r).wait_send()
    scatter_in_drain(0, inp, first)
    scatter_in_drain(1, cot, S.ct)

    @pl.when(jnp.logical_not(perm_stays))
    def _():
        perm_copy.wait_send()

    spot = first.at[pl.ds(mine, half)]
    rcopy(spot, spot, S.ins_s.at[0], S.ins_r.at[0], sibling).wait_send()
    for cls in range(8):
        gather_drain(cls)
    scatter_out_wait(0, S.back.at[0], out)
    scatter_out_wait(1, S.back.at[1], gin)
    for layer in range(LAYERS):
        for kind in range(4):
            reduce_drain(layer, kind)
    unpack_raise(0)
    unpack_heads(0)
    o_out[...] = S.oo[...]


def hand_over(*refs):
    for n in range(11):
        refs[n + 11][...] = refs[n][...]


def grouped(nz, ny):
    def run(inputs, w_qkv, w_out, w_up, w_down, biases, value_bias, up_bias, gains, shifts, cotangent):
        block = inputs.shape[1]
        d_rows = w_out.shape[1]
        f_rows = w_down.shape[1]
        rows = 2 * nz * block
        half = rows // 2
        layout = scratch_layout(nz, ny, rows, half, d_rows, f_rows)
        vmem = pl.BlockSpec(memory_space=pltpu.VMEM)
        weights = (w_qkv, w_out, w_up, w_down, biases, value_bias, up_bias, gains, shifts)
        shapes = [jax.ShapeDtypeStruct(inputs.shape, BF)] * 2
        shapes += [jax.ShapeDtypeStruct(array.shape, F32) for array in weights]
        results = pl.pallas_call(
            functools.partial(group_kernel, layout, nz),
            out_shape=tuple(shapes),
            in_specs=[vmem] * 11,
            out_specs=[vmem] * 11,
            scratch_shapes=list(layout.values()),
            compiler_params=pltpu.CompilerParams(
                collective_id=0, has_side_effects=True, vmem_limit_bytes=KERNEL_VMEM
            ),
        )(inputs, *weights, cotangent)
        return pl.pallas_call(
            hand_over,
            out_shape=tuple(shapes),
            in_specs=[vmem] * 11,
            out_specs=[vmem] * 11,
        )(*results)

    return run


def part_count(row_count):
    count = 1
    while row_count % count != 0 or row_count // count > 2048:
        count = count + 1
    return count


def exact_gelu(values):
    return jax.nn.gelu(values, approximate=False)


def normalize(values, gain, shift):
    centred = values - jnp.mean(values, axis=1, keepdims=True)
    inv_std = lax.rsqrt(jnp.mean(centred * centred, axis=1, keepdims=True) + 1e-12)
    scaled = centred * inv_std
    return (scaled * gain + shift, scaled, inv_std)


def norm_back(grad, scaled, inv_std, gain):
    weighted = grad * gain
    return (
        weighted
        - jnp.mean(weighted, axis=1, keepdims=True)
        - scaled * jnp.mean(weighted * scaled, axis=1, keepdims=True)
    ) * inv_std


def split_heads(seq_array, count):
    seq_count, width, unused = seq_array.shape
    return seq_array.reshape(seq_count, count, width // count, HEADS, HEAD_DIM).transpose(
        1, 0, 2, 3, 4
    )


def merge_heads(head_array):
    seq_count, unused, row_count, unused_dim = head_array.shape
    return head_array.transpose(0, 2, 1, 3).reshape(seq_count * row_count, HEADS * HEAD_DIM)


def attend_forward(queries, keys, values):
    seq_count, row_count, unused = queries.shape
    factor = HEAD_DIM ** (-0.5)
    query_heads = queries.reshape(seq_count, row_count, HEADS, HEAD_DIM)
    start_state = (
        jnp.full((seq_count, HEADS, row_count), -1e30, jnp.float32),
        jnp.zeros((seq_count, HEADS, row_count), jnp.float32),
        jnp.zeros((seq_count, HEADS, row_count, HEAD_DIM), jnp.float32),
    )
    piece = (
        lax.all_gather(keys, "ctx", axis=1, tiled=True),
        lax.all_gather(values, "ctx", axis=1, tiled=True),
    )
    count = part_count(piece[0].shape[1])

    def attend_advance(inner, parts):
        peak, totals, accum = inner
        key_part, value_part = parts
        scores = (
            jnp.einsum("sthd,skhd->shtk", query_heads, key_part, preferred_element_type=jnp.float32)
            * factor
        )
        new_peak = jnp.maximum(peak, jnp.max(scores, axis=3))
        decay = jnp.exp(peak - new_peak)
        weights = jnp.exp(scores - new_peak[..., None])
        totals = totals * decay + jnp.sum(weights, axis=3)
        accum = accum * decay[..., None] + jnp.einsum(
            "shtk,skhd->shtd",
            weights.astype(jnp.bfloat16),
            value_part,
            preferred_element_type=jnp.float32,
        )
        return ((new_peak, totals, accum), None)

    result, _ = lax.scan(
        attend_advance, start_state, (split_heads(piece[0], count), split_heads(piece[1], count))
    )
    peak, totals, accum = result
    mixed = merge_heads(accum / totals[..., None])
    return (mixed, peak + jnp.log(totals))


def query_fold(queries, grad_mixed, logsum, row_delta, keys, values):
    seq_count, row_count, unused = queries.shape
    factor = HEAD_DIM ** (-0.5)
    query_heads = queries.reshape(seq_count, row_count, HEADS, HEAD_DIM)
    grad_heads = grad_mixed.reshape(seq_count, row_count, HEADS, HEAD_DIM)
    start_state = jnp.zeros((seq_count, HEADS, row_count, HEAD_DIM), jnp.float32)
    piece = (
        lax.all_gather(keys, "ctx", axis=1, tiled=True),
        lax.all_gather(values, "ctx", axis=1, tiled=True),
    )
    count = part_count(piece[0].shape[1])

    def query_advance(totals, parts):
        key_part, value_part = parts
        scores = (
            jnp.einsum("sthd,skhd->shtk", query_heads, key_part, preferred_element_type=jnp.float32)
            * factor
        )
        weights = jnp.exp(scores - logsum[..., None])
        grad_weights = jnp.einsum(
            "sthd,skhd->shtk", grad_heads, value_part, preferred_element_type=jnp.float32
        )
        grad_scores = (weights * (grad_weights - row_delta[..., None])).astype(jnp.bfloat16)
        return (
            totals
            + jnp.einsum(
                "shtk,skhd->shtd", grad_scores, key_part, preferred_element_type=jnp.float32
            )
            * factor,
            None,
        )

    result, _ = lax.scan(
        query_advance, start_state, (split_heads(piece[0], count), split_heads(piece[1], count))
    )
    return result


def key_fold(queries, grad_mixed, keys, values, all_logsum, all_delta):
    seq_count, row_count, unused = keys.shape
    factor = HEAD_DIM ** (-0.5)
    key_heads = keys.reshape(seq_count, row_count, HEADS, HEAD_DIM)
    value_heads = values.reshape(seq_count, row_count, HEADS, HEAD_DIM)
    start_state = (
        jnp.zeros((seq_count, HEADS, row_count, HEAD_DIM), jnp.float32),
        jnp.zeros((seq_count, HEADS, row_count, HEAD_DIM), jnp.float32),
    )
    piece = (
        lax.all_gather(queries, "ctx", axis=1, tiled=True),
        lax.all_gather(grad_mixed, "ctx", axis=1, tiled=True),
    )
    width = piece[0].shape[1]
    count = part_count(width)
    block = width // count
    log_parts = all_logsum.reshape(seq_count, HEADS, count, block).transpose(2, 0, 1, 3)
    delta_parts = all_delta.reshape(seq_count, HEADS, count, block).transpose(2, 0, 1, 3)

    def key_advance(inner, parts):
        grad_keys, grad_values = inner
        query_part, grad_part, log_part, delta_part = parts
        scores = (
            jnp.einsum("sqhd,skhd->shqk", query_part, key_heads, preferred_element_type=jnp.float32)
            * factor
        )
        weights = jnp.exp(scores - log_part[..., None])
        grad_values = grad_values + jnp.einsum(
            "shqk,sqhd->shkd",
            weights.astype(jnp.bfloat16),
            grad_part,
            preferred_element_type=jnp.float32,
        )
        grad_weights = jnp.einsum(
            "sqhd,skhd->shqk", grad_part, value_heads, preferred_element_type=jnp.float32
        )
        grad_scores = (weights * (grad_weights - delta_part[..., None])).astype(jnp.bfloat16)
        grad_keys = (
            grad_keys
            + jnp.einsum(
                "shqk,sqhd->shkd", grad_scores, query_part, preferred_element_type=jnp.float32
            )
            * factor
        )
        return ((grad_keys, grad_values), None)

    result, _ = lax.scan(
        key_advance,
        start_state,
        (split_heads(piece[0], count), split_heads(piece[1], count), log_parts, delta_parts),
    )
    return result


def forward_layer(stream, full, seq_count):
    w_attn, w_mix, w_raise, w_lower, bias_rows, bias_value, bias_raise, gain_rows, shift_rows = full
    total_rows = stream.shape[0]
    rounded = stream.astype(jnp.bfloat16)
    projected = jnp.einsum("td,cde->cte", rounded, w_attn, preferred_element_type=jnp.float32)
    queries = (projected[0] + bias_rows[0].astype(jnp.float32)).astype(jnp.bfloat16)
    keys = projected[1].astype(jnp.bfloat16)
    values = (projected[2] + bias_value.astype(jnp.float32)).astype(jnp.bfloat16)
    seq_shape = (seq_count, total_rows // seq_count, D)
    mixed, logsum = attend_forward(
        queries.reshape(seq_shape), keys.reshape(seq_shape), values.reshape(seq_shape)
    )
    mixed_low = mixed.astype(jnp.bfloat16)
    branch = jnp.dot(mixed_low, w_mix, preferred_element_type=jnp.float32) + bias_rows[1].astype(
        jnp.float32
    )
    normed, scaled_one, inv_one = normalize(
        stream + branch, gain_rows[0].astype(jnp.float32), shift_rows[0].astype(jnp.float32)
    )
    normed_low = normed.astype(jnp.bfloat16)
    upward = jnp.dot(normed_low, w_raise, preferred_element_type=jnp.float32) + bias_raise.astype(
        jnp.float32
    )
    active = exact_gelu(upward).astype(jnp.bfloat16)
    lowered = jnp.dot(active, w_lower, preferred_element_type=jnp.float32) + bias_rows[2].astype(
        jnp.float32
    )
    result, scaled_two, inv_two = normalize(
        normed + lowered, gain_rows[1].astype(jnp.float32), shift_rows[1].astype(jnp.float32)
    )
    states = (
        rounded,
        queries,
        keys,
        values,
        mixed,
        mixed_low,
        logsum,
        scaled_one,
        inv_one,
        normed_low,
        upward,
        active,
        scaled_two,
        inv_two,
    )
    return (result, states)


def backward_layer(grad, full, states, seq_count):
    w_attn, w_mix, w_raise, w_lower, bias_rows, bias_value, bias_raise, gain_rows, shift_rows = full
    (
        rounded,
        queries,
        keys,
        values,
        mixed,
        mixed_low,
        logsum,
        scaled_one,
        inv_one,
        normed_low,
        upward,
        active,
        scaled_two,
        inv_two,
    ) = states
    total_rows = grad.shape[0]
    row_count = total_rows // seq_count
    seq_shape = (seq_count, row_count, D)
    grad_gain_two = jnp.sum(grad * scaled_two, axis=0)
    grad_shift_two = jnp.sum(grad, axis=0)
    grad_resid = norm_back(grad, scaled_two, inv_two, gain_rows[1].astype(jnp.float32))
    grad_lowered = grad_resid.astype(jnp.bfloat16)
    grad_w_lower = jnp.einsum("tf,td->fd", active, grad_lowered, preferred_element_type=jnp.float32)
    grad_active = jnp.einsum("td,fd->tf", grad_lowered, w_lower, preferred_element_type=jnp.float32)
    unused, gelu_back = jax.vjp(exact_gelu, upward)
    grad_upward = gelu_back(grad_active)[0].astype(jnp.bfloat16)
    grad_w_raise = jnp.einsum(
        "td,tf->df", normed_low, grad_upward, preferred_element_type=jnp.float32
    )
    grad_normed = (
        jnp.einsum("tf,df->td", grad_upward, w_raise, preferred_element_type=jnp.float32)
        + grad_resid
    )
    grad_gain_one = jnp.sum(grad_normed * scaled_one, axis=0)
    grad_shift_one = jnp.sum(grad_normed, axis=0)
    grad_inner = norm_back(grad_normed, scaled_one, inv_one, gain_rows[0].astype(jnp.float32))
    grad_branch = grad_inner.astype(jnp.bfloat16)
    grad_w_mix = jnp.einsum("td,te->de", mixed_low, grad_branch, preferred_element_type=jnp.float32)
    grad_mixed = jnp.einsum(
        "te,de->td", grad_branch, w_mix, preferred_element_type=jnp.float32
    ).astype(jnp.bfloat16)
    row_delta = jnp.sum(
        (grad_mixed.astype(jnp.float32) * mixed).reshape(seq_count, row_count, HEADS, HEAD_DIM),
        axis=3,
    ).transpose(0, 2, 1)
    seq_queries = queries.reshape(seq_shape)
    seq_keys = keys.reshape(seq_shape)
    seq_values = values.reshape(seq_shape)
    seq_grad_mixed = grad_mixed.reshape(seq_shape)
    grad_queries = query_fold(seq_queries, seq_grad_mixed, logsum, row_delta, seq_keys, seq_values)
    grad_queries = merge_heads(grad_queries).astype(jnp.bfloat16)
    all_logsum, all_delta = (
        lax.all_gather(logsum, "ctx", axis=2, tiled=True),
        lax.all_gather(row_delta, "ctx", axis=2, tiled=True),
    )
    grad_keys, grad_values = key_fold(
        seq_queries, seq_grad_mixed, seq_keys, seq_values, all_logsum, all_delta
    )
    grad_keys = merge_heads(grad_keys).astype(jnp.bfloat16)
    grad_values = merge_heads(grad_values).astype(jnp.bfloat16)
    grad_project = jnp.stack([grad_queries, grad_keys, grad_values])
    grad_w_attn = jnp.einsum(
        "td,cte->dce", rounded, grad_project, preferred_element_type=jnp.float32
    )
    grad_stream = (
        jnp.einsum("cte,cde->td", grad_project, w_attn, preferred_element_type=jnp.float32)
        + grad_inner
    )
    grad_bias_rows = jnp.stack(
        [
            jnp.sum(grad_queries.astype(jnp.float32), axis=0),
            jnp.sum(grad_branch.astype(jnp.float32), axis=0),
            jnp.sum(grad_lowered.astype(jnp.float32), axis=0),
        ],
        axis=1,
    )
    grad_bias_value = jnp.sum(grad_values.astype(jnp.float32), axis=0)
    grad_bias_raise = jnp.sum(grad_upward.astype(jnp.float32), axis=0)
    local_sums = (
        grad_w_attn,
        grad_w_mix,
        grad_w_raise,
        grad_w_lower,
        grad_bias_rows,
        grad_bias_value,
        grad_bias_raise,
        jnp.stack([grad_gain_one, grad_gain_two], axis=1),
        jnp.stack([grad_shift_one, grad_shift_two], axis=1),
    )
    return (grad_stream, local_sums)


def body(inputs, w_qkv, w_out, w_up, w_down, biases, value_bias, up_bias, gains, shifts, cotangent):
    stacked = (w_qkv, w_out, w_up, w_down, biases, value_bias, up_bias, gains, shifts)
    seq_count = inputs.shape[0]
    stream = inputs.reshape(-1, D).astype(jnp.float32)
    kept_states = []
    for layer in range(LAYERS):
        shards = tuple((array[layer] for array in stacked))
        full = (
            lax.all_gather(shards[0], ("ctx", "fsdp"), axis=1, tiled=True),
            lax.all_gather(shards[1], ("ctx", "fsdp"), axis=0, tiled=True),
            lax.all_gather(shards[2], ("ctx", "fsdp"), axis=0, tiled=True),
            lax.all_gather(shards[3], ("ctx", "fsdp"), axis=0, tiled=True),
            lax.all_gather(shards[4], ("ctx", "fsdp"), axis=1, tiled=True),
            lax.all_gather(shards[5], ("ctx", "fsdp"), axis=0, tiled=True),
            lax.all_gather(shards[6], ("ctx", "fsdp"), axis=0, tiled=True),
            lax.all_gather(shards[7], ("ctx", "fsdp"), axis=1, tiled=True),
            lax.all_gather(shards[8], ("ctx", "fsdp"), axis=1, tiled=True),
        )
        stream, states = forward_layer(stream, full, seq_count)
        kept_states.append(states)
    output = stream.astype(jnp.bfloat16).reshape(inputs.shape)
    grad = cotangent.reshape(-1, D).astype(jnp.float32)
    layer_grads = [None] * LAYERS
    for layer in reversed(range(LAYERS)):
        shards = tuple((array[layer] for array in stacked))
        full = (
            lax.all_gather(shards[0], ("ctx", "fsdp"), axis=1, tiled=True),
            lax.all_gather(shards[1], ("ctx", "fsdp"), axis=0, tiled=True),
            lax.all_gather(shards[2], ("ctx", "fsdp"), axis=0, tiled=True),
            lax.all_gather(shards[3], ("ctx", "fsdp"), axis=0, tiled=True),
            lax.all_gather(shards[4], ("ctx", "fsdp"), axis=1, tiled=True),
            lax.all_gather(shards[5], ("ctx", "fsdp"), axis=0, tiled=True),
            lax.all_gather(shards[6], ("ctx", "fsdp"), axis=0, tiled=True),
            lax.all_gather(shards[7], ("ctx", "fsdp"), axis=1, tiled=True),
            lax.all_gather(shards[8], ("ctx", "fsdp"), axis=1, tiled=True),
        )
        grad, local_sums = backward_layer(grad, full, kept_states[layer], seq_count)
        partial_sums = (
            lax.psum_scatter(local_sums[0], "ctx", scatter_dimension=0, tiled=True),
            lax.psum_scatter(local_sums[1], "ctx", scatter_dimension=0, tiled=True),
            lax.psum_scatter(local_sums[2], "ctx", scatter_dimension=0, tiled=True),
            lax.psum_scatter(local_sums[3], "ctx", scatter_dimension=0, tiled=True),
            lax.psum_scatter(local_sums[4], "ctx", scatter_dimension=0, tiled=True),
            lax.psum_scatter(local_sums[5], "ctx", scatter_dimension=0, tiled=True),
            lax.psum_scatter(local_sums[6], "ctx", scatter_dimension=0, tiled=True),
            lax.psum_scatter(local_sums[7], "ctx", scatter_dimension=0, tiled=True),
            lax.psum_scatter(local_sums[8], "ctx", scatter_dimension=0, tiled=True),
        )
        reduced = (
            lax.psum_scatter(
                partial_sums[0].astype(jnp.bfloat16), "fsdp", scatter_dimension=0, tiled=True
            ).astype(jnp.float32),
            lax.psum_scatter(
                partial_sums[1].astype(jnp.bfloat16), "fsdp", scatter_dimension=0, tiled=True
            ).astype(jnp.float32),
            lax.psum_scatter(
                partial_sums[2].astype(jnp.bfloat16), "fsdp", scatter_dimension=0, tiled=True
            ).astype(jnp.float32),
            lax.psum_scatter(
                partial_sums[3].astype(jnp.bfloat16), "fsdp", scatter_dimension=0, tiled=True
            ).astype(jnp.float32),
            lax.psum_scatter(
                partial_sums[4].astype(jnp.bfloat16), "fsdp", scatter_dimension=0, tiled=True
            ).astype(jnp.float32),
            lax.psum_scatter(
                partial_sums[5].astype(jnp.bfloat16), "fsdp", scatter_dimension=0, tiled=True
            ).astype(jnp.float32),
            lax.psum_scatter(
                partial_sums[6].astype(jnp.bfloat16), "fsdp", scatter_dimension=0, tiled=True
            ).astype(jnp.float32),
            lax.psum_scatter(
                partial_sums[7].astype(jnp.bfloat16), "fsdp", scatter_dimension=0, tiled=True
            ).astype(jnp.float32),
            lax.psum_scatter(
                partial_sums[8].astype(jnp.bfloat16), "fsdp", scatter_dimension=0, tiled=True
            ).astype(jnp.float32),
        )
        layer_grads[layer] = (
            reduced[0].transpose(1, 0, 2),
            reduced[1],
            reduced[2],
            reduced[3],
            reduced[4].T,
            reduced[5],
            reduced[6],
            reduced[7].T,
            reduced[8].T,
        )
    grad_inputs = grad.astype(jnp.bfloat16).reshape(inputs.shape)
    return (
        output,
        grad_inputs,
        jnp.stack([member[0] for member in layer_grads]),
        jnp.stack([member[1] for member in layer_grads]),
        jnp.stack([member[2] for member in layer_grads]),
        jnp.stack([member[3] for member in layer_grads]),
        jnp.stack([member[4] for member in layer_grads]),
        jnp.stack([member[5] for member in layer_grads]),
        jnp.stack([member[6] for member in layer_grads]),
        jnp.stack([member[7] for member in layer_grads]),
        jnp.stack([member[8] for member in layer_grads]),
    )


def one_group_per_sequence(mesh, seqs):
    return mesh.shape["fsdp"] == 4 and mesh.shape["ctx"] == seqs


def solution(mesh):
    def run(*arrays):
        seqs = arrays[0].shape[0]
        chosen = grouped(mesh.shape["ctx"] // 2, 2) if one_group_per_sequence(mesh, seqs) else body
        return on_devices(mesh, chosen)(*arrays)

    return run


def on_devices(mesh, chosen):
    return jax.shard_map(
        chosen,
        mesh=mesh,
        in_specs=(
            P("fsdp", "ctx", None),
            P(None, None, ("ctx", "fsdp"), None),
            P(None, ("ctx", "fsdp"), None),
            P(None, ("ctx", "fsdp"), None),
            P(None, ("ctx", "fsdp"), None),
            P(None, None, ("ctx", "fsdp")),
            P(None, ("ctx", "fsdp")),
            P(None, ("ctx", "fsdp")),
            P(None, None, ("ctx", "fsdp")),
            P(None, None, ("ctx", "fsdp")),
            P("fsdp", "ctx", None),
        ),
        out_specs=(
            P("fsdp", "ctx", None),
            P("fsdp", "ctx", None),
            P(None, None, ("ctx", "fsdp"), None),
            P(None, ("ctx", "fsdp"), None),
            P(None, ("ctx", "fsdp"), None),
            P(None, ("ctx", "fsdp"), None),
            P(None, None, ("ctx", "fsdp")),
            P(None, ("ctx", "fsdp")),
            P(None, ("ctx", "fsdp")),
            P(None, None, ("ctx", "fsdp")),
            P(None, None, ("ctx", "fsdp")),
        ),
        check_vma=False,
    )
```

```python
import functools
import types

import jax
import jax.numpy as jnp
from jax import lax
from jax.experimental import pallas as pl
from jax.experimental.pallas import tpu as pltpu
from jax.sharding import PartitionSpec as P

D = 768
HEADS = 12
HEAD_DIM = 64
LAYERS = 2
KERNEL_VMEM = 63 * 2**20


BF = jnp.bfloat16
F32 = jnp.float32
MESH = pl.DeviceIdType.MESH
MEMBERS = 4
LOCAL_HEADS = HEADS // MEMBERS
PACK = 640
SLOT = 64
PIECE = 64


def dot_nn(left, right):
    return lax.dot_general(left, right, (((1,), (0,)), ((), ())), preferred_element_type=F32)


def dot_nt(left, right):
    return lax.dot_general(left, right, (((1,), (1,)), ((), ())), preferred_element_type=F32)


def dot_tn(left, right):
    return lax.dot_general(left, right, (((0,), (0,)), ((), ())), preferred_element_type=F32)


def dot_exact(left, right):
    return lax.dot_general(
        left,
        right,
        (((1,), (0,)), ((), ())),
        precision=lax.Precision.HIGHEST,
        preferred_element_type=F32,
    )


def packed_lanes(shape, axis):
    lane = lax.broadcasted_iota(jnp.int32, shape, axis)
    slot = lane >> 6
    head = jnp.where(slot >= 6, 2, slot & 1)
    is_query = (slot < 2) | (slot == 6)
    is_value = (slot == 4) | (slot == 5) | (slot == 8)
    return (head * HEAD_DIM + (lane & 63), is_query, is_value)


def scratch_layout(nz, ny, rows, half, d_rows, f_rows):
    dma = pltpu.SemaphoreType.DMA
    two = 2 * d_rows
    ff = nz * ny * f_rows
    vm = pltpu.VMEM
    return dict(
        wq=vm((LAYERS, nz, 2, ny, two, PACK), BF),
        wu=vm((LAYERS, nz, 2, ny, two, ff), BF),
        wd=vm((LAYERS, nz, ny, f_rows, D), BF),
        wog=vm((nz, ny, two, D), BF),
        wo=vm((LAYERS, 256, D), BF),
        smg=vm((nz, ny, MEMBERS, 32, 128), BF),
        qi=vm((MEMBERS, two, PACK), BF),
        ui=vm((MEMBERS, two, ff), BF),
        oi=vm((two, D), BF),
        sf=vm((32, 128), F32),
        si=vm((32, 128), BF),
        qs=vm((MEMBERS, two, PACK), BF),
        us=vm((MEMBERS, two, ff), BF),
        pb=vm((16, D), F32),
        ub=vm((16, ff), F32),
        bq=vm((LAYERS, 8, PACK), F32),
        xf=vm((LAYERS, rows, D), BF),
        qkv=vm((LAYERS, rows, PACK), BF),
        prob=vm((LAYERS, LOCAL_HEADS, rows, rows), BF),
        mix=vm((LAYERS, rows, 256), F32),
        mixl=vm((LAYERS, rows, 256), BF),
        xh1=vm((LAYERS, half, D), F32),
        iv1=vm((LAYERS, half, 128), F32),
        nl=vm((LAYERS, rows, D), BF),
        gp=vm((LAYERS, rows, ff), F32),
        act=vm((LAYERS, rows, ff), BF),
        xh2=vm((LAYERS, half, D), F32),
        iv2=vm((LAYERS, half, 128), F32),
        stream=vm((half, D), F32),
        normed=vm((half, D), F32),
        ct=vm((half, D), BF),
        ownp=vm((half, D), F32),
        sibs=vm((2, half, D), BF),
        sibr=vm((2, half, D), BF),
        xs=vm((2, half, D), BF),
        xr=vm((2, half, D), BF),
        dl=vm((rows, D), BF),
        db=vm((rows, D), BF),
        du=vm((rows, ff), BF),
        dq=vm((rows, PACK), BF),
        dm=vm((rows, 256), BF),
        ds=vm((LOCAL_HEADS, rows, rows), BF),
        back=vm((2, half, D), BF),
        land=vm((2, 2, rows // (2 * nz), D), BF),
        gq=vm((LAYERS, nz, 2, ny, two, PACK), BF),
        gu=vm((LAYERS, nz, 2, ny, two, ff), BF),
        gd=vm((LAYERS, nz, ny, f_rows, D), BF),
        go=vm((LAYERS, nz, ny, 32, D), BF),
        ryq=vm((LAYERS, nz, 2, two, PACK), BF),
        ryu=vm((LAYERS, nz, 2, two, ff), BF),
        ryd=vm((nz, f_rows // 2, D), BF),
        ryl=vm((LAYERS, f_rows, D), BF),
        syl=vm((LAYERS, f_rows, D), BF),
        ryo=vm((LAYERS, nz, 32, D), BF),
        rzq=vm((LAYERS, 4, 2, two, PACK), BF),
        rzu=vm((LAYERS, 4, 2, two, ff), BF),
        rzd=vm((4, f_rows // 2, D), BF),
        rzl=vm((LAYERS, 4, 2, f_rows, D), BF),
        rzo=vm((LAYERS, 4, 32, D), BF),
        fq=vm((LAYERS, 2, two, PACK), F32),
        fu=vm((LAYERS, 2, two, ff), F32),
        fo=vm((LAYERS, d_rows, D), F32),
        oq=vm((LAYERS, MEMBERS, d_rows, PACK), F32),
        ou=vm((LAYERS, MEMBERS, d_rows, ff), F32),
        oo=vm((LAYERS, d_rows, D), F32),
        sg=vm((LAYERS, 8, D), F32),
        sgy=vm((LAYERS, 8, D), F32),
        sgt=vm((LAYERS, 8, D), F32),
        sgz=vm((LAYERS, nz, 8, D), F32),
        sga=vm((LAYERS, MEMBERS, 8, D), F32),
        stage_s=dma((3, 3)),
        stage_r=dma((3, 3)),
        perm=dma((2,)),
        in_s=dma((4, 2)),
        in_r=dma((4, 2)),
        inx_s=dma((2, 2)),
        inx_r=dma((2, 2)),
        ins_s=dma((1,)),
        ins_r=dma((1,)),
        gz_s=dma((8, nz)),
        gz_r=dma((8, nz)),
        gy_s=dma((8, nz)),
        gy_r=dma((8, nz)),
        sib_s=dma((2, half // PIECE)),
        sib_r=dma((2, half // PIECE)),
        x_s=dma((2, half // PIECE)),
        x_r=dma((2, half // PIECE)),
        ag_s=dma((2, half // PIECE)),
        ag_r=dma((2, half // PIECE)),
        ry_s=dma((10,)),
        ry_r=dma((10,)),
        rz_s=dma((10, nz)),
        rz_r=dma((10, nz)),
        fin_s=dma((LAYERS, 2, 3)),
        fin_r=dma((LAYERS, 2, 3)),
        fino=dma((LAYERS, 2)),
        sgy_s=dma((LAYERS,)),
        sgy_r=dma((LAYERS,)),
        sgz_s=dma((LAYERS, nz)),
        sgz_r=dma((LAYERS, nz)),
        sga_s=dma((LAYERS, 3)),
        sga_r=dma((LAYERS, 3)),
    )


def group_kernel(layout, nz, *refs):
    inp, w_qkv, w_out, w_up, d_in, biases, value_bias, up_bias, gains, shifts, cot = refs[:11]
    out, gin, g_qkv, o_out, g_up, d_out, g_biases, g_value, g_raise, g_gains, g_shifts = refs[11:22]
    S = types.SimpleNamespace(**dict(zip(layout.keys(), refs[22:])))
    q_in, u_in, o_in, s_in = S.qi, S.ui, S.oi, S.si
    rows = S.dl.shape[0]
    half = rows // 2
    block = inp.shape[1]
    d_rows = w_out.shape[1]
    f_rows = d_in.shape[1]
    two = 2 * d_rows
    ff = S.du.shape[1]
    pieces = half // PIECE
    place = lax.axis_index("ctx")
    lane_f = lax.axis_index("fsdp")
    z, x = lax.div(place, 2), lax.rem(place, 2)
    y, c = lax.div(lane_f, 2), lax.rem(lane_f, 2)
    m = 2 * x + c
    d = 4 * place + lane_f
    devices = 8 * nz

    def dev(z_at, x_at, y_at, c_at):
        return (2 * z_at + x_at, 2 * y_at + c_at)

    def rcopy(source, target, send, recv, to):
        return pltpu.make_async_remote_copy(
            src_ref=source,
            dst_ref=target,
            send_sem=send,
            recv_sem=recv,
            device_id=to,
            device_id_type=MESH,
        )

    barrier = pltpu.get_barrier_semaphore()

    def hail(step, carry):
        other = lax.rem(d + step, devices)
        pl.semaphore_signal(
            barrier, inc=1, device_id=(lax.div(other, 4), lax.rem(other, 4)), device_id_type=MESH
        )
        return carry

    lax.fori_loop(1, devices, hail, 0)

    lane_low = lax.broadcasted_iota(jnp.int32, (1, 128), 1) < HEAD_DIM

    def turn(value):
        return pltpu.roll(value, HEAD_DIM, 1)

    def pack_heads(layer, pair):
        tiles = []
        for kind in range(3):
            base = 2 * pair * LOCAL_HEADS * HEAD_DIM
            whole = w_qkv[layer, kind, :, base : base + 384].astype(F32)
            tiles.append([whole[:, 0:128], whole[:, 128:256], whole[:, 256:384]])
        (q0, q1, q2), (k0, k1, k2), (v0, v1, v2) = tiles
        even = (q0, k0, v0, jnp.where(lane_low, q1, turn(k1)), jnp.where(lane_low, v1, 0.0))
        odd = (
            jnp.where(lane_low, turn(q1), turn(q2)),
            jnp.where(lane_low, turn(k1), turn(k2)),
            jnp.where(lane_low, turn(v1), turn(v2)),
            jnp.where(lane_low, turn(q2), k2),
            jnp.where(lane_low, turn(v2), 0.0),
        )
        return [jnp.concatenate(part, axis=1) for part in (even, odd)]

    for pair in range(2):
        packed = [pack_heads(layer, pair) for layer in range(LAYERS)]
        for odd in range(2):
            both = jnp.concatenate([part[odd] for part in packed], axis=0)
            q_in[2 * pair + odd] = both.astype(BF)

    def owner_block(z_at, x_at, y_at, c_at):
        at = (8 * z_at + 4 * x_at + 2 * y_at + c_at) * f_rows
        return slice(at, at + f_rows)

    grid_places = [(z_at, y_at) for z_at in range(nz) for y_at in range(2)]

    def pack_raise():
        wide = [w_up[layer].astype(F32) for layer in range(LAYERS)]
        for x_at in range(2):
            for c_at in range(2):
                both = [
                    jnp.concatenate(
                        [part[:, owner_block(z_at, x_at, y_at, c_at)] for z_at, y_at in grid_places], axis=1
                    )
                    for part in wide
                ]
                u_in[2 * x_at + c_at] = jnp.concatenate(both, axis=0).astype(BF)

    def pack_small():
        S.sf[...] = jnp.zeros_like(S.sf)
        for layer in range(LAYERS):
            base = 8 * layer
            S.sf[base : base + 3, 0:d_rows] = biases[layer].astype(F32)
            S.sf[base + 3 : base + 4, 0:d_rows] = value_bias[layer : layer + 1].astype(F32)
            S.sf[base + 4 : base + 6, 0:d_rows] = gains[layer].astype(F32)
            S.sf[base + 6 : base + 8, 0:d_rows] = shifts[layer].astype(F32)
            S.sf[16 + layer : 17 + layer, 0:f_rows] = up_bias[layer : layer + 1].astype(F32)
        s_in[...] = S.sf[...].astype(BF)

    pack_small()
    pack_raise()
    o_in[...] = jnp.concatenate([w_out[layer].astype(F32) for layer in range(LAYERS)], axis=0).astype(BF)
    pl.semaphore_wait(barrier, devices - 1)

    relation = ((x, 1 - c), (1 - x, c), (1 - x, 1 - c))
    sibling = dev(z, x, y, 1 - c)
    peer = dev(z, 1 - x, y, c)
    across = dev(z, x, 1 - y, c)

    def stage_copy(kind, r):
        x_r, c_r = relation[r]
        m_r = 2 * x_r + c_r
        source = (s_in, q_in.at[m_r], u_in.at[m_r])[kind]
        target = (S.smg.at[z, y, m], S.qs.at[m], S.us.at[m])[kind]
        return rcopy(source, target, S.stage_s.at[kind, r], S.stage_r.at[kind, r], dev(z, x_r, y, c_r))

    def stage_wait(kind, r):
        x_r, c_r = relation[r]
        m_r = 2 * x_r + c_r
        target = (S.smg.at[z, y, m_r], S.qs.at[m_r], S.us.at[m_r])[kind]
        rcopy(
            target, target, S.stage_s.at[kind, r], S.stage_r.at[kind, r], dev(z, x_r, y, c_r)
        ).wait_recv()

    for kind in (1, 0):
        for r in (1, 2, 0):
            stage_copy(kind, r).start()

    def own_block(j):
        return (2 * c + j == z) & (lax.div(z, 2) == c)

    def scatter_in(which, source, target, position):
        for j in range(2):
            copy = rcopy(
                source.at[j],
                target.at[pl.ds(position, block)],
                S.in_s.at[which, j],
                S.in_r.at[which, lax.rem(z, 2)],
                dev(2 * c + j, x, y, lax.div(z, 2)),
            )

            @pl.when(own_block(j))
            def _():
                target[pl.ds(position, block), :] = source[j]

            @pl.when(jnp.logical_not(own_block(j)))
            def _():
                copy.start()

    def scatter_in_wait(which, source, target, base):
        for k in range(2):

            @pl.when(2 * c + k != z)
            def _():
                spot = target.at[pl.ds(base + 2 * block * k, block)]
                rcopy(
                    spot, spot, S.in_s.at[which, 0], S.in_r.at[which, k], peer
                ).wait_recv()

    def scatter_in_drain(which, source, target):
        for j in range(2):

            @pl.when(jnp.logical_not(own_block(j)))
            def _():
                rcopy(
                    source.at[j], source.at[j], S.in_s.at[which, j], S.in_r.at[which, 0], peer
                ).wait_send()

    first = S.xf.at[0]
    scatter_in(0, inp, first, block * place)

    perm_to = dev(2 * x + y, lax.div(z, 2), c, lax.rem(z, 2))
    perm_stays = (2 * x + y == z) & (lax.div(z, 2) == x) & (c == y) & (lax.rem(z, 2) == c)
    perm_copy = rcopy(o_in, S.wog.at[2 * x + y, c], S.perm.at[0], S.perm.at[1], perm_to)

    @pl.when(perm_stays)
    def _():
        S.wog[z, y] = o_in[...]

    def start_perm():
        @pl.when(jnp.logical_not(perm_stays))
        def _():
            perm_copy.start()

    start_perm()
    for r in (1, 2, 0):
        stage_copy(2, r).start()
    S.smg[z, y, m] = s_in[...]
    S.qs[m] = q_in[m]
    S.us[m] = u_in[m]
    for layer in range(LAYERS):
        S.wd[layer, z, y] = d_in[layer]

    def join(staged, target):
        for xx in range(2):
            first_part = staged[2 * xx].astype(F32)
            second_part = staged[2 * xx + 1].astype(F32)
            for layer in range(LAYERS):
                cut = slice(layer * d_rows, (layer + 1) * d_rows)
                target[layer, z, xx, y] = jnp.concatenate(
                    [first_part[cut], second_part[cut]], axis=0
                ).astype(BF)

    side = lax.div(z, 2)
    inner = (z == 1) | (z == 2)
    outer = jnp.logical_not(inner)
    near_in, near_out = 1 + side, 3 * side
    far_in, far_out = 2 - side, 3 * (1 - side)
    buddy = near_in + near_out - z

    def at_z(z_at):
        return dev(z_at, x, y, c)

    LAST = -1
    DIRECT = 0

    def slab(cls, z_at, y_at):
        return (
            lambda: S.smg.at[z_at, y_at],
            lambda: S.wq.at[0, z_at, :, y_at],
            lambda: S.wog.at[z_at, y_at],
            lambda: S.wu.at[0, z_at, :, y_at],
            lambda: S.wd.at[0, z_at, y_at],
            lambda: S.wq.at[1, z_at, :, y_at],
            lambda: S.wu.at[1, z_at, :, y_at],
            lambda: S.wd.at[1, z_at, y_at],
        )[cls]()

    def z_copy(cls, n, z_at, to):
        spot = S.wd.at[1, z_at] if cls == LAST else slab(cls, z_at, y)
        return rcopy(spot, spot, S.gz_s.at[cls, n], S.gz_r.at[cls, z_at], at_z(to))

    def y_copy(cls, z_at):
        spot = slab(cls, z_at, y)
        return rcopy(spot, spot, S.gy_s.at[cls, z_at], S.gy_r.at[cls, z_at], across)

    def gather_direct(cls):
        z_copy(cls, 0, z, buddy).start()
        z_copy(cls, 1, z, far_in).start()
        if cls < DIRECT:
            z_copy(cls, 2, z, far_out).start()

    def gather_start(cls):
        if cls != LAST:
            gather_direct(cls)
        y_copy(cls, z).start()

    def gather_cross(cls):
        if cls != LAST:
            return
        spot = slab(cls, z, 1 - y)
        rcopy(spot, spot, S.gy_s.at[cls, z], S.gy_r.at[cls, z], across).wait_recv()
        gather_direct(cls)

    def gather_take(cls, z_at, relay):
        z_copy(cls, 0, z_at, buddy).wait_recv()
        if relay is not None:
            z_copy(cls, relay, z_at, near_out).start()
        if cls != LAST:
            y_copy(cls, z_at).start()

    def gather_relay(cls):
        gather_take(cls, buddy, None)
        if cls < DIRECT:
            gather_take(cls, far_in, None)
            gather_take(cls, far_out, None)
            return

        @pl.when(inner)
        def _():
            gather_take(cls, far_in, 2)

        gather_relay_far(cls)

    def gather_relay_far(cls):
        @pl.when(inner)
        def _():
            gather_take(cls, far_out, 3)

    def gather_end(cls):
        @pl.when(outer)
        def _():
            gather_take(cls, far_in, None)
            gather_take(cls, far_out, None)

    def gather_wait(cls):
        if cls == LAST:
            spot = S.wd.at[1, z]
            return

        def one(t):
            spot = slab(cls, t, 1 - y)
            rcopy(spot, spot, S.gy_s.at[cls, t], S.gy_r.at[cls, t], across).wait_recv()

        for t in (z, buddy, far_in, far_out):
            one(t)

    def gather_drain(cls):
        z_copy(cls, 0, z, buddy).wait_send()
        z_copy(cls, 1, z, far_in).wait_send()
        if cls < DIRECT:
            z_copy(cls, 2, z, far_out).wait_send()
        else:

            @pl.when(inner)
            def _():
                z_copy(cls, 2, far_in, near_out).wait_send()
                z_copy(cls, 3, far_out, near_out).wait_send()

        def one(t, carry):
            y_copy(cls, t).wait_send()
            return carry

        if cls == LAST:
            one(z, 0)
        else:
            lax.fori_loop(0, nz, one, 0)

    for r in range(3):
        stage_wait(1, r)
    join(S.qs, S.wq)
    gather_start(1)
    for r in range(3):
        stage_wait(0, r)
    gather_start(0)

    def x_spots(target, base, mine):
        return [target.at[pl.ds(base + block * (2 * k + mine), block)] for k in range(2)]

    def swap_start(which, target, base):
        for k, spot in enumerate(x_spots(target, base, x)):
            rcopy(spot, spot, S.inx_s.at[which, k], S.inx_r.at[which, k], peer).start()

    def swap_wait(which, target, base):
        for k, spot in enumerate(x_spots(target, base, 1 - x)):
            rcopy(spot, spot, S.inx_s.at[which, k], S.inx_r.at[which, k], peer).wait_recv()
        for k, spot in enumerate(x_spots(target, base, x)):
            rcopy(spot, spot, S.inx_s.at[which, k], S.inx_r.at[which, k], peer).wait_send()

    mine = half * c
    theirs = half * (1 - c)
    scatter_in_wait(0, inp, first, mine + block * x)
    swap_start(0, first, mine)
    for r in range(3):
        stage_wait(2, r)
    join(S.us, S.wu)
    gather_relay(1)
    gather_relay(0)
    swap_wait(0, first, mine)
    spot = first.at[pl.ds(mine, half)]
    rcopy(spot, spot, S.ins_s.at[0], S.ins_r.at[0], sibling).start()
    S.stream[...] = S.xf[0, pl.ds(mine, half), :].astype(F32)

    @pl.when(jnp.logical_not(perm_stays))
    def _():
        spot = S.wog.at[z, y]
        rcopy(spot, spot, S.perm.at[0], S.perm.at[1], peer).wait_recv()

    gather_start(2)
    gather_end(1)
    gather_end(0)
    gather_relay(2)
    gather_start(3)
    gather_wait(0)

    def small_params():
        row_shape = (devices * 16, D)
        lane = lax.broadcasted_iota(jnp.int32, (128, D), 0)
        col = lax.broadcasted_iota(jnp.int32, (128, D), 1)
        tile = jnp.where(lax.rem(col, d_rows) == lane, 1.0, 0.0).astype(BF)
        packs = S.smg[:, :, :, 0:16, :].reshape(devices * 16, 128)
        spread = dot_nn(packs, tile)
        owner_row = lax.broadcasted_iota(jnp.int32, row_shape, 0) >> 4
        zz = owner_row >> 3
        yy = (owner_row >> 2) & 1
        xx = (owner_row >> 1) & 1
        cc = owner_row & 1
        owner = zz * 8 + xx * 4 + yy * 2 + cc
        at = lax.div(lax.broadcasted_iota(jnp.int32, row_shape, 1), d_rows)
        spread = jnp.where(owner == at, spread, 0.0)
        S.pb[...] = jnp.sum(spread.reshape(devices, 16, D), axis=0)
        lane = lax.broadcasted_iota(jnp.int32, (128, ff), 0)
        col = lax.broadcasted_iota(jnp.int32, (128, ff), 1)
        tile = jnp.where(lax.rem(col, f_rows) == lane, 1.0, 0.0).astype(BF)
        packs = S.smg[:, :, m, 16:32, :].reshape(2 * nz * 16, 128)
        spread = dot_nn(packs, tile)
        row_shape = (2 * nz * 16, ff)
        owner = lax.broadcasted_iota(jnp.int32, row_shape, 0) >> 4
        at = lax.div(lax.broadcasted_iota(jnp.int32, row_shape, 1), f_rows)
        spread = jnp.where(owner == at, spread, 0.0)
        S.ub[...] = jnp.sum(spread.reshape(2 * nz, 16, ff), axis=0)
        source = lax.broadcasted_iota(jnp.int32, (D, PACK), 0)
        target, unused_q, unused_v = packed_lanes((D, PACK), 1)
        pick = jnp.where(source == target + m * (LOCAL_HEADS * HEAD_DIM), 1.0, 0.0).astype(BF)
        picked = dot_nn(S.pb[...].astype(BF), pick)
        unused, is_query, is_value = packed_lanes((1, PACK), 1)
        for layer in range(LAYERS):
            base = 8 * layer
            row = jnp.where(is_query, picked[base : base + 1], 0.0)
            row = jnp.where(is_value, picked[base + 3 : base + 4], row)
            S.bq[layer, 0:1, :] = row

    small_params()
    scatter_in(1, cot, S.ct, block * (2 * lax.rem(z, 2) + x))

    def param(layer, kind):
        return S.pb[8 * layer + kind : 8 * layer + kind + 1, :]

    def piece_rows(i):
        return pl.ds(i * PIECE if isinstance(i, int) else pl.multiple_of(i * PIECE, PIECE), PIECE)

    def own_rows(i):
        return pl.ds(pl.multiple_of(mine + i * PIECE, PIECE), PIECE)

    def other_rows(i):
        return pl.ds(pl.multiple_of(theirs + i * PIECE, PIECE), PIECE)

    every = slice(None)

    def load_both(ref, i, cols=every):
        return jnp.concatenate([ref[other_rows(i), cols], ref[own_rows(i), cols]], axis=0)

    def store_both(ref, i, value, cols=every):
        ref[other_rows(i), cols] = value[:PIECE]
        ref[own_rows(i), cols] = value[PIECE:]

    def spread_start(par, i, ref, value):
        ref[own_rows(i), :] = value
        spot = ref.at[own_rows(i)]
        rcopy(spot, spot, S.ag_s.at[par, i], S.ag_r.at[par, i], sibling).start()

    def spread_wait(par, i, ref):
        got = ref.at[other_rows(i)]
        sent = ref.at[own_rows(i)]
        rcopy(got, got, S.ag_s.at[par, i], S.ag_r.at[par, i], sibling).wait_recv()
        rcopy(sent, sent, S.ag_s.at[par, i], S.ag_r.at[par, i], sibling).wait_send()

    def sib_copy(par, i):
        at = piece_rows(i)
        return rcopy(
            S.sibs.at[par, at], S.sibr.at[par, at], S.sib_s.at[par, i], S.sib_r.at[par, i], sibling
        )

    def peer_copy(par, i):
        at = piece_rows(i)
        return rcopy(S.xs.at[par, at], S.xr.at[par, at], S.x_s.at[par, i], S.x_r.at[par, i], peer)

    def part_send(par, i, value):
        at = piece_rows(i)
        S.sibs[par, at, :] = value[:PIECE].astype(BF)
        sib_copy(par, i).start()
        S.ownp[at, :] = value[PIECE:]

    def part_pass(par, i):
        at = piece_rows(i)
        sib_copy(par, i).wait_recv()
        S.xs[par, at, :] = (S.ownp[at, :] + S.sibr[par, at, :].astype(F32)).astype(BF)
        peer_copy(par, i).start()

    def part_take(par, i):
        at = piece_rows(i)
        peer_copy(par, i).wait_recv()
        return S.xs[par, at, :].astype(F32) + S.xr[par, at, :].astype(F32)

    def part_drain(par):
        for i in range(pieces):
            sib_copy(par, i).wait_send()
            peer_copy(par, i).wait_send()

    def pipeline(stages, between=None):
        for step in range(pieces + len(stages) - 1):
            for lag, stage in enumerate(stages):
                if 0 <= step - lag < pieces:
                    stage(step - lag)
            for call in (between or {}).get(step, ()):
                call()

    def norm_piece(total, at, layer, gain, shift, scaled_ref, inv_ref):
        centred = total - jnp.mean(total, axis=1, keepdims=True)
        inv = lax.rsqrt(jnp.mean(centred * centred, axis=1, keepdims=True) + 1e-12)
        scaled = centred * inv
        scaled_ref[layer, at, :] = scaled
        inv_ref[layer, at, :] = jnp.broadcast_to(inv, (PIECE, 128))
        return scaled * gain + shift

    def flat(value):
        return value.reshape(-1, value.shape[-1])

    def swap_lanes(value):
        return pltpu.roll(value.astype(F32), HEAD_DIM, 1).astype(BF)

    def mask_queries(queries, h):
        keep = jnp.logical_not(lane_low) if h == 1 else lane_low
        return jnp.where(keep, queries * jnp.asarray(HEAD_DIM**-0.5, BF), jnp.zeros((), BF))

    def query_cols(h):
        return slice(0, 128) if h < 2 else slice(384, 512)

    def head_keys(layer, h):
        if h < 2:
            return S.qkv[layer, :, 128:256]
        return swap_lanes(S.qkv[layer, :, 384:512])

    def head_values(layer, h):
        return S.qkv[layer, :, 256:384] if h < 2 else S.qkv[layer, :, 512:640]

    def project(layer, i):
        value = dot_nn(load_both(S.xf.at[layer], i), flat(S.wq[layer])) + S.bq[layer, 0:1, :]
        store_both(S.qkv.at[layer], i, value.astype(BF))

    def attend(layer, i):
        mixes = []
        for h in range(LOCAL_HEADS):
            queries = mask_queries(load_both(S.qkv.at[layer], i, query_cols(h)), h)
            scores = dot_nt(queries, head_keys(layer, h))
            weights = jnp.exp(scores - jnp.max(scores, axis=1, keepdims=True))
            weights = (weights * (1.0 / jnp.sum(weights, axis=1, keepdims=True))).astype(BF)
            store_both(S.prob.at[layer, h], i, weights)
            mixes.append(dot_nn(weights, head_values(layer, h)))
        mix = jnp.concatenate(
            [jnp.where(lane_low, mixes[0], mixes[1]), jnp.where(lane_low, mixes[2], 0.0)], axis=1
        )
        store_both(S.mix.at[layer], i, mix)
        store_both(S.mixl.at[layer], i, mix.astype(BF))
        part_send(0, i, dot_nn(mix.astype(BF), S.wo[layer]))

    def after_attention(layer, i):
        at = piece_rows(i)
        total = S.stream[at, :] + part_take(0, i) + param(layer, 1)
        normed = norm_piece(total, at, layer, param(layer, 4), param(layer, 6), S.xh1, S.iv1)
        S.normed[at, :] = normed
        spread_start(0, i, S.nl.at[layer], normed.astype(BF))

    def raise_part(layer, i):
        spread_wait(0, i, S.nl.at[layer])
        rounded = load_both(S.nl.at[layer], i)
        upward = dot_nn(rounded, flat(S.wu[layer])) + S.ub[layer : layer + 1, :]
        cdf = 0.5 * (1.0 + lax.erf(upward * (0.5**0.5)))
        density = jnp.exp(-0.5 * upward * upward) * ((2.0 * jnp.pi) ** -0.5)
        store_both(S.act.at[layer], i, (upward * cdf).astype(BF))
        store_both(S.gp.at[layer], i, cdf + upward * density)

    def lower_part(layer, i):
        part_send(1, i, dot_nn(load_both(S.act.at[layer], i), flat(S.wd[layer])))

    def after_lower(layer, i):
        at = piece_rows(i)
        total = S.normed[at, :] + part_take(1, i) + param(layer, 2)
        result = norm_piece(total, at, layer, param(layer, 5), param(layer, 7), S.xh2, S.iv2)
        if layer < LAYERS - 1:
            S.stream[at, :] = result
            spread_start(1, i, S.xf.at[layer + 1], result.astype(BF))
        else:
            S.back[0, at, :] = result.astype(BF)

    def next_project(layer, i):
        spread_wait(1, i, S.xf.at[layer])
        project(layer, i)

    def scatter_out(which, source):
        for k in range(2):
            stays = (2 * c + k == z) & (lax.div(z, 2) == c)
            spot = source.at[pl.ds(pl.multiple_of(block * (2 * k + x), block), block)]
            slot = lax.rem(z, 2)

            @pl.when(stays)
            def _():
                S.land[which, slot] = spot[...]

            @pl.when(jnp.logical_not(stays))
            def _():
                rcopy(
                    spot,
                    S.land.at[which, slot],
                    S.in_s.at[2 + which, k],
                    S.in_r.at[2 + which, slot],
                    dev(2 * c + k, x, y, lax.div(z, 2)),
                ).start()

    def scatter_out_wait(which, source, result):
        for k in range(2):
            spot = source.at[pl.ds(pl.multiple_of(block * (2 * k + x), block), block)]

            @pl.when(jnp.logical_not((2 * c + k == z) & (lax.div(z, 2) == c)))
            def _():
                rcopy(
                    spot, spot, S.in_s.at[2 + which, k], S.in_r.at[2 + which, 0], peer
                ).wait_send()

            @pl.when(jnp.logical_not(own_block(k)))
            def _():
                landed = S.land.at[which, k]
                rcopy(
                    landed, landed, S.in_s.at[2 + which, 0], S.in_r.at[2 + which, k], peer
                ).wait_recv()

        result[...] = S.land[which]

    def out_weights():
        gather_wait(2)
        for layer in range(LAYERS):
            cut = slice(layer * d_rows, (layer + 1) * d_rows)
            parts = [S.wog[t, yy].astype(F32)[cut] for t in range(nz) for yy in range(2)]
            parts.append(jnp.zeros((256 - 2 * nz * d_rows, D), F32))
            S.wo[layer] = jnp.concatenate(parts, axis=0).astype(BF)

    spot = first.at[pl.ds(theirs, half)]
    rcopy(spot, spot, S.ins_s.at[0], S.ins_r.at[0], sibling).wait_recv()
    gather_wait(1)
    for i in range(pieces):
        project(0, i)
    gather_start(4)
    gather_end(2)
    gather_relay(3)
    out_weights()
    pipeline(
        (lambda i: attend(0, i), lambda i: part_pass(0, i)),
        {1: [lambda: gather_end(3)], 2: [lambda: gather_start(5)], 3: [lambda: gather_relay(4)]},
    )
    pipeline((lambda i: after_attention(0, i),))
    part_drain(0)
    gather_start(6)
    gather_end(4)
    gather_wait(3)
    pipeline((lambda i: raise_part(0, i),))
    scatter_in_wait(1, cot, S.ct, block * x)
    gather_relay(5)
    gather_start(7)
    gather_end(5)
    gather_wait(4)
    pipeline((lambda i: lower_part(0, i), lambda i: part_pass(1, i)))
    swap_start(1, S.ct, 0)
    gather_relay(6)
    gather_wait(5)
    pipeline(
        (lambda i: after_lower(0, i), lambda i: next_project(1, i)),
        {0: [lambda: gather_end(6)], 3: [lambda: gather_cross(7)]},
    )
    part_drain(1)
    pipeline(
        (lambda i: attend(1, i), lambda i: part_pass(0, i)),
        {1: [lambda: gather_relay(7)], 3: [lambda: gather_end(7)]},
    )
    gather_wait(6)
    pipeline(
        (
            lambda i: after_attention(1, i),
            lambda i: raise_part(1, i),
            lambda i: lower_part(1, i),
            lambda i: part_pass(1, i),
        ),
        {1: [lambda: gather_wait(7)]},
    )
    part_drain(0)
    swap_wait(1, S.ct, 0)


    def add_row(layer, kind, value):
        S.sg[layer, kind : kind + 1, :] += jnp.sum(value, axis=0, keepdims=True)

    def norm_back_piece(grad, at, layer, which):
        scaled = (S.xh1 if which == 0 else S.xh2)[layer, at, :]
        inv = (S.iv1 if which == 0 else S.iv2)[layer, at, 0:1]
        add_row(layer, 2 + which, grad * scaled)
        add_row(layer, 4 + which, grad)
        weighted = grad * param(layer, 4 + which)
        back = (
            weighted
            - jnp.mean(weighted, axis=1, keepdims=True)
            - scaled * jnp.mean(weighted * scaled, axis=1, keepdims=True)
        ) * inv
        return back

    def lower_back(layer, i, grad):
        at = piece_rows(i)
        back = norm_back_piece(grad, at, layer, 1)
        S.normed[at, :] = back
        rounded = back.astype(BF)
        add_row(layer, 1, rounded.astype(F32))
        spread_start(0, i, S.dl, rounded)

    def raise_back(layer, i):
        spread_wait(0, i, S.dl)
        back = dot_nt(load_both(S.dl, i), flat(S.wd[layer])) * load_both(S.gp.at[layer], i)
        rounded = back.astype(BF)
        store_both(S.du, i, rounded)
        add_row(layer, 6, rounded.astype(F32))
        part_send(0, i, dot_nt(rounded, flat(S.wu[layer])))

    grads = (S.gq, S.gu, S.gd, S.go)
    from_y = (S.ryq, S.ryu, None, S.ryo)
    from_z = (S.rzq, S.rzu, None, S.rzo)

    half_rows = f_rows // 2
    upper, lower = pl.ds(0, half_rows), pl.ds(half_rows, half_rows)

    def down_rows(layer, kind):
        if layer == LAYERS - 1:
            return pl.ds(0, f_rows)
        return upper if kind == 2 else lower

    def grad_slab(layer, kind, t, y_at):
        if kind in (2, 4):
            return S.gd.at[layer, t, y_at, down_rows(layer, kind)]
        ref = grads[kind]
        return ref.at[layer, t, :, y_at] if kind < 2 else ref.at[layer, t, y_at]

    def z_slab(layer, kind, t):
        if kind == 2:
            return S.gd.at[layer, t, :, down_rows(layer, kind)]
        return grad_slab(layer, kind, t, y)

    def y_landing(layer, kind):
        if kind == 2:
            return S.ryl.at[layer, down_rows(layer, kind)]
        return S.ryd if kind == 4 else from_y[kind].at[layer]

    def z_landing(layer, kind, slot):
        if kind == 2:
            return S.rzl.at[layer, slot, :, down_rows(layer, kind)]
        return S.rzd.at[slot] if kind == 4 else from_z[kind].at[layer, slot]

    def reduce_y_copy(layer, kind):
        if kind == 2:
            source = S.syl.at[layer, down_rows(layer, kind)]
        elif kind == 4:
            source = S.gd.at[layer, :, 1 - y, lower]
        elif kind < 2:
            source = grads[kind].at[layer, :, :, 1 - y]
        else:
            source = grads[kind].at[layer, :, 1 - y]
        n = 5 * layer + kind
        return rcopy(source, y_landing(layer, kind), S.ry_s.at[n], S.ry_r.at[n], across)

    def reduce_z_copy(layer, kind, t, slot, to):
        n = 5 * layer + kind
        return rcopy(
            z_slab(layer, kind, t),
            z_landing(layer, kind, slot),
            S.rz_s.at[n, t],
            S.rz_r.at[n, slot],
            at_z(to),
        )

    def slab_add(target, other):
        if len(target.shape) == 3:
            for xx in range(2):
                target[xx] = (target[xx].astype(F32) + other[xx].astype(F32)).astype(BF)
        else:
            target[...] = (target[...].astype(F32) + other[...].astype(F32)).astype(BF)

    def reduce_direct(layer, kind):
        @pl.when(outer)
        def _():
            reduce_z_copy(layer, kind, far_in, 2, buddy).start()
            reduce_z_copy(layer, kind, far_out, 3, buddy).start()

        reduce_z_copy(layer, kind, buddy, 0, buddy).start()

    def reduce_start(layer, kind):
        if kind == 2:
            reduce_direct(layer, kind)
        else:
            reduce_y_copy(layer, kind).start()

    def reduce_first(layer, kind):
        reduce_y_copy(layer, kind).wait_recv()

        def one(t, carry):
            slab_add(grad_slab(layer, kind, t, y), y_landing(layer, kind).at[t])
            return carry

        lax.fori_loop(0, nz, one, 0)
        reduce_direct(layer, kind)

    def reduce_relay(layer, kind):
        @pl.when(inner)
        def _():
            for slot, t in ((2, far_in), (3, far_out)):
                reduce_z_copy(layer, kind, t, slot, buddy).wait_recv()
                slab_add(z_slab(layer, kind, t), z_landing(layer, kind, slot))
                reduce_z_copy(layer, kind, t, 1, t).start()

    def reduce_cross(layer):
        at = down_rows(layer, 2)
        d_out[layer, at, :] = S.gd[layer, z, y, at, :].astype(F32)
        other = S.gd[layer, z, 1 - y, at, :].astype(F32)
        for slot in (0, 1):
            reduce_z_copy(layer, 2, z, slot, buddy).wait_recv()
            d_out[layer, at, :] += S.rzl[layer, slot, y, at, :].astype(F32)
            other = other + S.rzl[layer, slot, 1 - y, at, :].astype(F32)
        S.syl[layer, at, :] = other.astype(BF)
        reduce_y_copy(layer, 2).start()

    def reduce_last_d(layer):
        at = down_rows(layer, 2)
        reduce_y_copy(layer, 2).wait_recv()
        d_out[layer, at, :] += S.ryl[layer, at, :].astype(F32)

    final = (S.fq, S.fu, None, S.fo)

    def reduce_last(layer, kind):
        if kind == 3:
            target = S.fo.at[layer]
            cut = lambda value: value[0:d_rows]
        elif kind == 4:
            target = d_out.at[layer, lower]
            cut = lambda value: value
        else:
            target = final[kind].at[layer]
            cut = lambda value: value
        target[...] = cut(grad_slab(layer, kind, z, y)[...].astype(F32))

        for slot in (0, 1):
            reduce_z_copy(layer, kind, z, slot, buddy).wait_recv()
            target[...] += cut(z_landing(layer, kind, slot)[...].astype(F32))

        if kind < 2:
            result = (S.oq, S.ou)[kind]
            for r in (1, 2, 0):
                hand_copy(layer, kind, r).start()
            for xx in range(2):
                for cc in range(2):

                    @pl.when((x == xx) & (c == cc))
                    def _():
                        result[layer, 2 * xx + cc] = target[xx, cc * d_rows : (cc + 1) * d_rows, :]

        if kind == 3:
            @pl.when(owner_stays)
            def _():
                S.oo[layer] = target[...]

            @pl.when(jnp.logical_not(owner_stays))
            def _():
                owner_copy(layer).start()

    def hand_copy(layer, kind, r):
        x_r, c_r = relation[r]
        source = (S.fq, S.fu)[kind].at[
            layer, x_r, pl.ds(pl.multiple_of(c_r * d_rows, 8), d_rows)
        ]
        target = (S.oq, S.ou)[kind].at[layer, m]
        return rcopy(
            source,
            target,
            S.fin_s.at[layer, kind, r],
            S.fin_r.at[layer, kind, r],
            dev(z, x_r, y, c_r),
        )

    owner_to = dev(2 * x + c, lax.div(z, 2), lax.rem(z, 2), y)
    owner_stays = (2 * x + c == z) & (lax.div(z, 2) == x) & (lax.rem(z, 2) == y) & (y == c)

    def owner_copy(layer):
        return rcopy(
            S.fo.at[layer], S.oo.at[layer], S.fino.at[layer, 0], S.fino.at[layer, 1], owner_to
        )

    def reduce_drain(layer, kind):
        reduce_y_copy(layer, kind).wait_send()
        for t in range(nz):

            @pl.when(z != t)
            def _():
                reduce_z_copy(layer, kind, t, 0, buddy).wait_send()

        if kind < 2:
            for r in range(3):
                hand_copy(layer, kind, r).wait_send()
        if kind == 3:
            @pl.when(jnp.logical_not(owner_stays))
            def _():
                owner_copy(layer).wait_send()
                owner_copy(layer).wait_recv()

    def lower_grad(layer):
        for i in range(2):
            value = dot_tn(S.act[layer, :, i * (ff // 2) : (i + 1) * (ff // 2)], S.dl[...])
            S.gd[layer, i * (nz // 2) : (i + 1) * (nz // 2)] = value.astype(BF).reshape(
                nz // 2, 2, f_rows, D
            )
        reduce_start(layer, 2)

    def raise_grad(layer):
        for i in range(2):
            value = dot_tn(S.nl[layer, :, i * (D // 2) : (i + 1) * (D // 2)], S.du[...])
            S.gu[layer, i * (nz // 2) : (i + 1) * (nz // 2)] = value.astype(BF).reshape(
                nz // 2, 2, 2, two, ff
            )
        reduce_start(layer, 1)

    def out_grad(layer):
        value = dot_tn(S.mixl[layer], S.db[...])
        empty = jnp.zeros((32 - d_rows, D), F32)
        for t in range(nz):
            for yy in range(2):
                at = (2 * t + yy) * d_rows
                S.go[layer, t, yy] = jnp.concatenate(
                    [value[at : at + d_rows], empty], axis=0
                ).astype(BF)
        reduce_start(layer, 3)

    def project_grad(layer):
        for i in range(2):
            value = dot_tn(S.xf[layer, :, i * (D // 2) : (i + 1) * (D // 2)], S.dq[...])
            S.gq[layer, i * (nz // 2) : (i + 1) * (nz // 2)] = value.astype(BF).reshape(
                nz // 2, 2, 2, two, PACK
            )
        reduce_start(layer, 0)

    def branch_back(layer, i):
        at = piece_rows(i)
        back = norm_back_piece(part_take(0, i) + S.normed[at, :], at, layer, 0)
        S.stream[at, :] = back
        rounded = back.astype(BF)
        add_row(layer, 0, rounded.astype(F32))
        spread_start(1, i, S.db, rounded)

    scale = HEAD_DIM**-0.5

    def attend_back(layer, i):
        spread_wait(1, i, S.db)
        grad_mix = dot_nt(load_both(S.db, i), S.wo[layer]).astype(BF)
        store_both(S.dm, i, grad_mix)
        mix = load_both(S.mix.at[layer], i)
        results = []
        for h in range(LOCAL_HEADS):
            keep = jnp.logical_not(lane_low) if h == 1 else lane_low
            cols = slice(0, 128) if h < 2 else slice(128, 256)
            grad = jnp.where(keep, grad_mix[:, cols], jnp.zeros((), BF))
            delta = jnp.sum(grad.astype(F32) * mix[:, cols], axis=1, keepdims=True)
            grad_weights = dot_nt(grad, head_values(layer, h))
            weights = load_both(S.prob.at[layer, h], i).astype(F32)
            rounded = (weights * (grad_weights - delta)).astype(BF)
            store_both(S.ds.at[h], i, rounded)
            results.append((dot_nn(rounded, head_keys(layer, h)) * scale).astype(BF))
        store_both(S.dq, i, jnp.where(lane_low, results[0], results[1]), slice(0, 128))
        store_both(S.dq, i, results[2], slice(384, 512))

    def attend_back_end(layer):
        keys_back, values_back = [], []
        for h in range(LOCAL_HEADS):
            cols = slice(0, 128) if h < 2 else slice(128, 256)
            queries = mask_queries(S.qkv[layer, :, query_cols(h)], h)
            keys_back.append(dot_tn(S.ds[h], queries).astype(BF))
            values_back.append(dot_tn(S.prob[layer, h], S.dm[:, cols]).astype(BF))
        S.dq[:, 128:256] = jnp.where(lane_low, keys_back[0], keys_back[1])
        S.dq[:, 256:384] = jnp.where(lane_low, values_back[0], values_back[1])
        S.dq[:, 384:512] = jnp.where(lane_low, S.dq[:, 384:512], swap_lanes(keys_back[2]))
        S.dq[:, 512:640] = jnp.where(lane_low, values_back[2], jnp.zeros((), BF))
        S.sg[layer, 7:8, 0:PACK] = jnp.sum(S.dq[...].astype(F32), axis=0, keepdims=True)

    def project_back(layer, i):
        part_send(1, i, dot_nt(load_both(S.dq, i), flat(S.wq[layer])))

    def next_back(layer, i):
        at = piece_rows(i)
        grad = part_take(1, i) + S.stream[at, :]
        if layer > 0:
            lower_back(layer - 1, i, grad)
        else:
            S.back[1, at, :] = grad.astype(BF)

    def small_y(layer):
        return rcopy(S.sg.at[layer], S.sgy.at[layer], S.sgy_s.at[layer], S.sgy_r.at[layer], across)

    def small_z(layer, k):
        to = dev(lax.rem(z + k, nz), x, y, c)
        return rcopy(
            S.sgt.at[layer], S.sgz.at[layer, k], S.sgz_s.at[layer, k], S.sgz_r.at[layer, k], to
        )

    def small_member(layer, r):
        x_r, c_r = relation[r]
        return rcopy(
            S.sgt.at[layer],
            S.sga.at[layer, m],
            S.sga_s.at[layer, r],
            S.sga_r.at[layer, r],
            dev(z, x_r, y, c_r),
        )

    def small_one(layer):
        small_y(layer).start()

    def small_two(layer):
        small_y(layer).wait_recv()
        S.sgt[layer] = S.sg[layer] + S.sgy[layer]
        for k in range(1, nz):
            small_z(layer, k).start()

    def small_three(layer):
        for k in range(1, nz):
            small_z(layer, k).wait_recv()
        for k in range(1, nz):
            small_z(layer, k).wait_send()
        total = S.sgt[layer]
        for k in range(1, nz):
            total = total + S.sgz[layer, k]
        S.sgt[layer] = total
        for r in range(3):
            small_member(layer, r).start()
        S.sga[layer, m] = total

    def small_four(layer):
        for r in range(3):
            small_member(layer, r).wait_send()
            small_member(layer, r).wait_recv()
        small_y(layer).wait_send()
        lane = lax.broadcasted_iota(jnp.int32, (D, 128), 1)
        col = lax.broadcasted_iota(jnp.int32, (D, 128), 0)
        narrow = lane < d_rows
        pick = jnp.where((col == d_rows * d + lane) & narrow, 1.0, 0.0)
        both = S.sga[layer, 2 * x] + S.sga[layer, 2 * x + 1]
        found = dot_exact(both, pick)[:, 0:d_rows]
        g_biases[layer, 1:3, :] = found[0:2]
        g_gains[layer] = found[2:4]
        g_shifts[layer] = found[4:6]
        dim, is_query, is_value = packed_lanes((D, 128), 0)
        hit = (dim == d_rows * (d - 8 * z) + lane) & narrow
        attn = S.sga[layer, z]
        found = dot_exact(attn, jnp.where(hit & is_query, 1.0, 0.0))
        g_biases[layer, 0:1, :] = found[7:8, 0:d_rows]
        found = dot_exact(attn, jnp.where(hit & is_value, 1.0, 0.0))
        g_value[layer : layer + 1, :] = found[7:8, 0:d_rows]
        pick = jnp.where((col == f_rows * (2 * z + y) + lane) & (lane < f_rows), 1.0, 0.0)
        found = dot_exact(S.sga[layer, m], pick)
        g_raise[layer : layer + 1, :] = found[6:7, 0:f_rows]

    def hand_wait(layer, kind):
        for r in range(3):
            hand_copy(layer, kind, r).wait_recv()

    def unpack_heads(layer):
        hand_wait(layer, 0)
        for pair in range(2):
            even = [S.oq[layer, 2 * pair, :, 128 * t : 128 * t + 128] for t in range(5)]
            odd = [S.oq[layer, 2 * pair + 1, :, 128 * t : 128 * t + 128] for t in range(5)]
            thirds = (
                (even[3], turn(odd[3])),
                (turn(even[3]), odd[3]),
                (even[4], turn(odd[4])),
            )
            for kind in range(3):
                turned = turn(odd[kind])
                tiles = [
                    even[kind],
                    jnp.where(lane_low, thirds[kind][0], turned),
                    jnp.where(lane_low, turned, thirds[kind][1]),
                ]
                base = 384 * pair
                g_qkv[layer, kind, :, base : base + 384] = jnp.concatenate(tiles, axis=1)

    def unpack_raise(layer):
        hand_wait(layer, 1)
        wide = [S.ou[layer, member] for member in range(MEMBERS)]
        parts = []
        for z_at in range(nz):
            for x_at in range(2):
                for y_at in range(2):
                    for c_at in range(2):
                        at = (2 * z_at + y_at) * f_rows
                        parts.append(wide[2 * x_at + c_at][:, at : at + f_rows])
        g_up[layer] = jnp.concatenate(parts, axis=1)

    S.sg[...] = jnp.zeros_like(S.sg)

    def turn_back(i):
        after_lower(1, i)
        lower_back(1, i, S.ct[piece_rows(i), :].astype(F32))

    pipeline(
        (turn_back, lambda i: raise_back(1, i), lambda i: part_pass(0, i)),
        {4: [lambda: lower_grad(1)]},
    )
    part_drain(1)
    raise_grad(1)
    scatter_out(0, S.back.at[0])
    pipeline((lambda i: branch_back(1, i), lambda i: attend_back(1, i)))
    part_drain(0)
    attend_back_end(1)
    pipeline((lambda i: project_back(1, i), lambda i: part_pass(1, i)))
    small_one(1)
    project_grad(1)
    out_grad(1)
    reduce_first(1, 1)
    pipeline(
        (
            lambda i: next_back(1, i),
            lambda i: raise_back(0, i),
            lambda i: part_pass(0, i),
        ),
        {4: [lambda: lower_grad(0)]},
    )
    part_drain(1)
    reduce_first(1, 0)
    raise_grad(0)
    pipeline(
        (lambda i: branch_back(0, i), lambda i: attend_back(0, i)),
        {1: [lambda: reduce_relay(1, 2)], 3: [lambda: reduce_first(1, 3), lambda: reduce_relay(1, 1)]},
    )
    part_drain(0)
    attend_back_end(0)
    small_one(0)
    pipeline((lambda i: project_back(0, i), lambda i: part_pass(1, i)))
    project_grad(0)
    out_grad(0)
    reduce_start(0, 4)
    small_two(1)
    pipeline(
        (lambda i: next_back(0, i),),
        {
            0: [lambda: reduce_relay(1, 0)],
            1: [lambda: reduce_relay(1, 3)],
            2: [lambda: reduce_relay(0, 2)],
        },
    )
    part_drain(1)
    scatter_out(1, S.back.at[1])
    reduce_cross(1)
    reduce_first(0, 1)
    small_three(1)
    reduce_last(1, 1)
    reduce_last(1, 0)
    small_two(0)
    reduce_relay(0, 1)
    reduce_first(0, 0)
    reduce_last(1, 3)
    reduce_cross(0)
    small_four(1)
    reduce_first(0, 3)
    small_three(0)
    reduce_relay(0, 0)
    reduce_first(0, 4)
    reduce_last_d(1)
    unpack_heads(1)
    unpack_raise(1)
    reduce_last(0, 1)
    reduce_relay(0, 3)
    reduce_last(0, 0)
    reduce_relay(0, 4)
    reduce_last_d(0)
    small_four(0)
    reduce_last(0, 3)
    reduce_last(0, 4)

    for kind in range(3):
        for r in range(3):
            stage_copy(kind, r).wait_send()
    scatter_in_drain(0, inp, first)
    scatter_in_drain(1, cot, S.ct)

    @pl.when(jnp.logical_not(perm_stays))
    def _():
        perm_copy.wait_send()

    spot = first.at[pl.ds(mine, half)]
    rcopy(spot, spot, S.ins_s.at[0], S.ins_r.at[0], sibling).wait_send()
    for cls in range(8):
        gather_drain(cls)
    scatter_out_wait(0, S.back.at[0], out)
    scatter_out_wait(1, S.back.at[1], gin)
    for layer in range(LAYERS):
        for kind in range(4 if layer == LAYERS - 1 else 5):
            reduce_drain(layer, kind)
    unpack_raise(0)
    unpack_heads(0)
    o_out[...] = S.oo[...]


def hand_over(*refs):
    for n in range(11):
        refs[n + 11][...] = refs[n][...]


def grouped(nz, ny):
    def run(inputs, w_qkv, w_out, w_up, w_down, biases, value_bias, up_bias, gains, shifts, cotangent):
        block = inputs.shape[1]
        d_rows = w_out.shape[1]
        f_rows = w_down.shape[1]
        rows = 2 * nz * block
        half = rows // 2
        layout = scratch_layout(nz, ny, rows, half, d_rows, f_rows)
        vmem = pl.BlockSpec(memory_space=pltpu.VMEM)
        weights = (w_qkv, w_out, w_up, w_down, biases, value_bias, up_bias, gains, shifts)
        shapes = [jax.ShapeDtypeStruct(inputs.shape, BF)] * 2
        shapes += [jax.ShapeDtypeStruct(array.shape, F32) for array in weights]
        results = pl.pallas_call(
            functools.partial(group_kernel, layout, nz),
            out_shape=tuple(shapes),
            in_specs=[vmem] * 11,
            out_specs=[vmem] * 11,
            scratch_shapes=list(layout.values()),
            compiler_params=pltpu.CompilerParams(
                collective_id=0, has_side_effects=True, vmem_limit_bytes=KERNEL_VMEM
            ),
        )(inputs, *weights, cotangent)
        return pl.pallas_call(
            hand_over,
            out_shape=tuple(shapes),
            in_specs=[vmem] * 11,
            out_specs=[vmem] * 11,
        )(*results)

    return run


def part_count(row_count):
    count = 1
    while row_count % count != 0 or row_count // count > 2048:
        count = count + 1
    return count


def exact_gelu(values):
    return jax.nn.gelu(values, approximate=False)


def normalize(values, gain, shift):
    centred = values - jnp.mean(values, axis=1, keepdims=True)
    inv_std = lax.rsqrt(jnp.mean(centred * centred, axis=1, keepdims=True) + 1e-12)
    scaled = centred * inv_std
    return (scaled * gain + shift, scaled, inv_std)


def norm_back(grad, scaled, inv_std, gain):
    weighted = grad * gain
    return (
        weighted
        - jnp.mean(weighted, axis=1, keepdims=True)
        - scaled * jnp.mean(weighted * scaled, axis=1, keepdims=True)
    ) * inv_std


def split_heads(seq_array, count):
    seq_count, width, unused = seq_array.shape
    return seq_array.reshape(seq_count, count, width // count, HEADS, HEAD_DIM).transpose(
        1, 0, 2, 3, 4
    )


def merge_heads(head_array):
    seq_count, unused, row_count, unused_dim = head_array.shape
    return head_array.transpose(0, 2, 1, 3).reshape(seq_count * row_count, HEADS * HEAD_DIM)


def attend_forward(queries, keys, values):
    seq_count, row_count, unused = queries.shape
    factor = HEAD_DIM ** (-0.5)
    query_heads = queries.reshape(seq_count, row_count, HEADS, HEAD_DIM)
    start_state = (
        jnp.full((seq_count, HEADS, row_count), -1e30, jnp.float32),
        jnp.zeros((seq_count, HEADS, row_count), jnp.float32),
        jnp.zeros((seq_count, HEADS, row_count, HEAD_DIM), jnp.float32),
    )
    piece = (
        lax.all_gather(keys, "ctx", axis=1, tiled=True),
        lax.all_gather(values, "ctx", axis=1, tiled=True),
    )
    count = part_count(piece[0].shape[1])

    def attend_advance(inner, parts):
        peak, totals, accum = inner
        key_part, value_part = parts
        scores = (
            jnp.einsum("sthd,skhd->shtk", query_heads, key_part, preferred_element_type=jnp.float32)
            * factor
        )
        new_peak = jnp.maximum(peak, jnp.max(scores, axis=3))
        decay = jnp.exp(peak - new_peak)
        weights = jnp.exp(scores - new_peak[..., None])
        totals = totals * decay + jnp.sum(weights, axis=3)
        accum = accum * decay[..., None] + jnp.einsum(
            "shtk,skhd->shtd",
            weights.astype(jnp.bfloat16),
            value_part,
            preferred_element_type=jnp.float32,
        )
        return ((new_peak, totals, accum), None)

    result, _ = lax.scan(
        attend_advance, start_state, (split_heads(piece[0], count), split_heads(piece[1], count))
    )
    peak, totals, accum = result
    mixed = merge_heads(accum / totals[..., None])
    return (mixed, peak + jnp.log(totals))


def query_fold(queries, grad_mixed, logsum, row_delta, keys, values):
    seq_count, row_count, unused = queries.shape
    factor = HEAD_DIM ** (-0.5)
    query_heads = queries.reshape(seq_count, row_count, HEADS, HEAD_DIM)
    grad_heads = grad_mixed.reshape(seq_count, row_count, HEADS, HEAD_DIM)
    start_state = jnp.zeros((seq_count, HEADS, row_count, HEAD_DIM), jnp.float32)
    piece = (
        lax.all_gather(keys, "ctx", axis=1, tiled=True),
        lax.all_gather(values, "ctx", axis=1, tiled=True),
    )
    count = part_count(piece[0].shape[1])

    def query_advance(totals, parts):
        key_part, value_part = parts
        scores = (
            jnp.einsum("sthd,skhd->shtk", query_heads, key_part, preferred_element_type=jnp.float32)
            * factor
        )
        weights = jnp.exp(scores - logsum[..., None])
        grad_weights = jnp.einsum(
            "sthd,skhd->shtk", grad_heads, value_part, preferred_element_type=jnp.float32
        )
        grad_scores = (weights * (grad_weights - row_delta[..., None])).astype(jnp.bfloat16)
        return (
            totals
            + jnp.einsum(
                "shtk,skhd->shtd", grad_scores, key_part, preferred_element_type=jnp.float32
            )
            * factor,
            None,
        )

    result, _ = lax.scan(
        query_advance, start_state, (split_heads(piece[0], count), split_heads(piece[1], count))
    )
    return result


def key_fold(queries, grad_mixed, keys, values, all_logsum, all_delta):
    seq_count, row_count, unused = keys.shape
    factor = HEAD_DIM ** (-0.5)
    key_heads = keys.reshape(seq_count, row_count, HEADS, HEAD_DIM)
    value_heads = values.reshape(seq_count, row_count, HEADS, HEAD_DIM)
    start_state = (
        jnp.zeros((seq_count, HEADS, row_count, HEAD_DIM), jnp.float32),
        jnp.zeros((seq_count, HEADS, row_count, HEAD_DIM), jnp.float32),
    )
    piece = (
        lax.all_gather(queries, "ctx", axis=1, tiled=True),
        lax.all_gather(grad_mixed, "ctx", axis=1, tiled=True),
    )
    width = piece[0].shape[1]
    count = part_count(width)
    block = width // count
    log_parts = all_logsum.reshape(seq_count, HEADS, count, block).transpose(2, 0, 1, 3)
    delta_parts = all_delta.reshape(seq_count, HEADS, count, block).transpose(2, 0, 1, 3)

    def key_advance(inner, parts):
        grad_keys, grad_values = inner
        query_part, grad_part, log_part, delta_part = parts
        scores = (
            jnp.einsum("sqhd,skhd->shqk", query_part, key_heads, preferred_element_type=jnp.float32)
            * factor
        )
        weights = jnp.exp(scores - log_part[..., None])
        grad_values = grad_values + jnp.einsum(
            "shqk,sqhd->shkd",
            weights.astype(jnp.bfloat16),
            grad_part,
            preferred_element_type=jnp.float32,
        )
        grad_weights = jnp.einsum(
            "sqhd,skhd->shqk", grad_part, value_heads, preferred_element_type=jnp.float32
        )
        grad_scores = (weights * (grad_weights - delta_part[..., None])).astype(jnp.bfloat16)
        grad_keys = (
            grad_keys
            + jnp.einsum(
                "shqk,sqhd->shkd", grad_scores, query_part, preferred_element_type=jnp.float32
            )
            * factor
        )
        return ((grad_keys, grad_values), None)

    result, _ = lax.scan(
        key_advance,
        start_state,
        (split_heads(piece[0], count), split_heads(piece[1], count), log_parts, delta_parts),
    )
    return result


def forward_layer(stream, full, seq_count):
    w_attn, w_mix, w_raise, w_lower, bias_rows, bias_value, bias_raise, gain_rows, shift_rows = full
    total_rows = stream.shape[0]
    rounded = stream.astype(jnp.bfloat16)
    projected = jnp.einsum("td,cde->cte", rounded, w_attn, preferred_element_type=jnp.float32)
    queries = (projected[0] + bias_rows[0].astype(jnp.float32)).astype(jnp.bfloat16)
    keys = projected[1].astype(jnp.bfloat16)
    values = (projected[2] + bias_value.astype(jnp.float32)).astype(jnp.bfloat16)
    seq_shape = (seq_count, total_rows // seq_count, D)
    mixed, logsum = attend_forward(
        queries.reshape(seq_shape), keys.reshape(seq_shape), values.reshape(seq_shape)
    )
    mixed_low = mixed.astype(jnp.bfloat16)
    branch = jnp.dot(mixed_low, w_mix, preferred_element_type=jnp.float32) + bias_rows[1].astype(
        jnp.float32
    )
    normed, scaled_one, inv_one = normalize(
        stream + branch, gain_rows[0].astype(jnp.float32), shift_rows[0].astype(jnp.float32)
    )
    normed_low = normed.astype(jnp.bfloat16)
    upward = jnp.dot(normed_low, w_raise, preferred_element_type=jnp.float32) + bias_raise.astype(
        jnp.float32
    )
    active = exact_gelu(upward).astype(jnp.bfloat16)
    lowered = jnp.dot(active, w_lower, preferred_element_type=jnp.float32) + bias_rows[2].astype(
        jnp.float32
    )
    result, scaled_two, inv_two = normalize(
        normed + lowered, gain_rows[1].astype(jnp.float32), shift_rows[1].astype(jnp.float32)
    )
    states = (
        rounded,
        queries,
        keys,
        values,
        mixed,
        mixed_low,
        logsum,
        scaled_one,
        inv_one,
        normed_low,
        upward,
        active,
        scaled_two,
        inv_two,
    )
    return (result, states)


def backward_layer(grad, full, states, seq_count):
    w_attn, w_mix, w_raise, w_lower, bias_rows, bias_value, bias_raise, gain_rows, shift_rows = full
    (
        rounded,
        queries,
        keys,
        values,
        mixed,
        mixed_low,
        logsum,
        scaled_one,
        inv_one,
        normed_low,
        upward,
        active,
        scaled_two,
        inv_two,
    ) = states
    total_rows = grad.shape[0]
    row_count = total_rows // seq_count
    seq_shape = (seq_count, row_count, D)
    grad_gain_two = jnp.sum(grad * scaled_two, axis=0)
    grad_shift_two = jnp.sum(grad, axis=0)
    grad_resid = norm_back(grad, scaled_two, inv_two, gain_rows[1].astype(jnp.float32))
    grad_lowered = grad_resid.astype(jnp.bfloat16)
    grad_w_lower = jnp.einsum("tf,td->fd", active, grad_lowered, preferred_element_type=jnp.float32)
    grad_active = jnp.einsum("td,fd->tf", grad_lowered, w_lower, preferred_element_type=jnp.float32)
    unused, gelu_back = jax.vjp(exact_gelu, upward)
    grad_upward = gelu_back(grad_active)[0].astype(jnp.bfloat16)
    grad_w_raise = jnp.einsum(
        "td,tf->df", normed_low, grad_upward, preferred_element_type=jnp.float32
    )
    grad_normed = (
        jnp.einsum("tf,df->td", grad_upward, w_raise, preferred_element_type=jnp.float32)
        + grad_resid
    )
    grad_gain_one = jnp.sum(grad_normed * scaled_one, axis=0)
    grad_shift_one = jnp.sum(grad_normed, axis=0)
    grad_inner = norm_back(grad_normed, scaled_one, inv_one, gain_rows[0].astype(jnp.float32))
    grad_branch = grad_inner.astype(jnp.bfloat16)
    grad_w_mix = jnp.einsum("td,te->de", mixed_low, grad_branch, preferred_element_type=jnp.float32)
    grad_mixed = jnp.einsum(
        "te,de->td", grad_branch, w_mix, preferred_element_type=jnp.float32
    ).astype(jnp.bfloat16)
    row_delta = jnp.sum(
        (grad_mixed.astype(jnp.float32) * mixed).reshape(seq_count, row_count, HEADS, HEAD_DIM),
        axis=3,
    ).transpose(0, 2, 1)
    seq_queries = queries.reshape(seq_shape)
    seq_keys = keys.reshape(seq_shape)
    seq_values = values.reshape(seq_shape)
    seq_grad_mixed = grad_mixed.reshape(seq_shape)
    grad_queries = query_fold(seq_queries, seq_grad_mixed, logsum, row_delta, seq_keys, seq_values)
    grad_queries = merge_heads(grad_queries).astype(jnp.bfloat16)
    all_logsum, all_delta = (
        lax.all_gather(logsum, "ctx", axis=2, tiled=True),
        lax.all_gather(row_delta, "ctx", axis=2, tiled=True),
    )
    grad_keys, grad_values = key_fold(
        seq_queries, seq_grad_mixed, seq_keys, seq_values, all_logsum, all_delta
    )
    grad_keys = merge_heads(grad_keys).astype(jnp.bfloat16)
    grad_values = merge_heads(grad_values).astype(jnp.bfloat16)
    grad_project = jnp.stack([grad_queries, grad_keys, grad_values])
    grad_w_attn = jnp.einsum(
        "td,cte->dce", rounded, grad_project, preferred_element_type=jnp.float32
    )
    grad_stream = (
        jnp.einsum("cte,cde->td", grad_project, w_attn, preferred_element_type=jnp.float32)
        + grad_inner
    )
    grad_bias_rows = jnp.stack(
        [
            jnp.sum(grad_queries.astype(jnp.float32), axis=0),
            jnp.sum(grad_branch.astype(jnp.float32), axis=0),
            jnp.sum(grad_lowered.astype(jnp.float32), axis=0),
        ],
        axis=1,
    )
    grad_bias_value = jnp.sum(grad_values.astype(jnp.float32), axis=0)
    grad_bias_raise = jnp.sum(grad_upward.astype(jnp.float32), axis=0)
    local_sums = (
        grad_w_attn,
        grad_w_mix,
        grad_w_raise,
        grad_w_lower,
        grad_bias_rows,
        grad_bias_value,
        grad_bias_raise,
        jnp.stack([grad_gain_one, grad_gain_two], axis=1),
        jnp.stack([grad_shift_one, grad_shift_two], axis=1),
    )
    return (grad_stream, local_sums)


def body(inputs, w_qkv, w_out, w_up, w_down, biases, value_bias, up_bias, gains, shifts, cotangent):
    stacked = (w_qkv, w_out, w_up, w_down, biases, value_bias, up_bias, gains, shifts)
    seq_count = inputs.shape[0]
    stream = inputs.reshape(-1, D).astype(jnp.float32)
    kept_states = []
    for layer in range(LAYERS):
        shards = tuple((array[layer] for array in stacked))
        full = (
            lax.all_gather(shards[0], ("ctx", "fsdp"), axis=1, tiled=True),
            lax.all_gather(shards[1], ("ctx", "fsdp"), axis=0, tiled=True),
            lax.all_gather(shards[2], ("ctx", "fsdp"), axis=0, tiled=True),
            lax.all_gather(shards[3], ("ctx", "fsdp"), axis=0, tiled=True),
            lax.all_gather(shards[4], ("ctx", "fsdp"), axis=1, tiled=True),
            lax.all_gather(shards[5], ("ctx", "fsdp"), axis=0, tiled=True),
            lax.all_gather(shards[6], ("ctx", "fsdp"), axis=0, tiled=True),
            lax.all_gather(shards[7], ("ctx", "fsdp"), axis=1, tiled=True),
            lax.all_gather(shards[8], ("ctx", "fsdp"), axis=1, tiled=True),
        )
        stream, states = forward_layer(stream, full, seq_count)
        kept_states.append(states)
    output = stream.astype(jnp.bfloat16).reshape(inputs.shape)
    grad = cotangent.reshape(-1, D).astype(jnp.float32)
    layer_grads = [None] * LAYERS
    for layer in reversed(range(LAYERS)):
        shards = tuple((array[layer] for array in stacked))
        full = (
            lax.all_gather(shards[0], ("ctx", "fsdp"), axis=1, tiled=True),
            lax.all_gather(shards[1], ("ctx", "fsdp"), axis=0, tiled=True),
            lax.all_gather(shards[2], ("ctx", "fsdp"), axis=0, tiled=True),
            lax.all_gather(shards[3], ("ctx", "fsdp"), axis=0, tiled=True),
            lax.all_gather(shards[4], ("ctx", "fsdp"), axis=1, tiled=True),
            lax.all_gather(shards[5], ("ctx", "fsdp"), axis=0, tiled=True),
            lax.all_gather(shards[6], ("ctx", "fsdp"), axis=0, tiled=True),
            lax.all_gather(shards[7], ("ctx", "fsdp"), axis=1, tiled=True),
            lax.all_gather(shards[8], ("ctx", "fsdp"), axis=1, tiled=True),
        )
        grad, local_sums = backward_layer(grad, full, kept_states[layer], seq_count)
        partial_sums = (
            lax.psum_scatter(local_sums[0], "ctx", scatter_dimension=0, tiled=True),
            lax.psum_scatter(local_sums[1], "ctx", scatter_dimension=0, tiled=True),
            lax.psum_scatter(local_sums[2], "ctx", scatter_dimension=0, tiled=True),
            lax.psum_scatter(local_sums[3], "ctx", scatter_dimension=0, tiled=True),
            lax.psum_scatter(local_sums[4], "ctx", scatter_dimension=0, tiled=True),
            lax.psum_scatter(local_sums[5], "ctx", scatter_dimension=0, tiled=True),
            lax.psum_scatter(local_sums[6], "ctx", scatter_dimension=0, tiled=True),
            lax.psum_scatter(local_sums[7], "ctx", scatter_dimension=0, tiled=True),
            lax.psum_scatter(local_sums[8], "ctx", scatter_dimension=0, tiled=True),
        )
        reduced = (
            lax.psum_scatter(
                partial_sums[0].astype(jnp.bfloat16), "fsdp", scatter_dimension=0, tiled=True
            ).astype(jnp.float32),
            lax.psum_scatter(
                partial_sums[1].astype(jnp.bfloat16), "fsdp", scatter_dimension=0, tiled=True
            ).astype(jnp.float32),
            lax.psum_scatter(
                partial_sums[2].astype(jnp.bfloat16), "fsdp", scatter_dimension=0, tiled=True
            ).astype(jnp.float32),
            lax.psum_scatter(
                partial_sums[3].astype(jnp.bfloat16), "fsdp", scatter_dimension=0, tiled=True
            ).astype(jnp.float32),
            lax.psum_scatter(
                partial_sums[4].astype(jnp.bfloat16), "fsdp", scatter_dimension=0, tiled=True
            ).astype(jnp.float32),
            lax.psum_scatter(
                partial_sums[5].astype(jnp.bfloat16), "fsdp", scatter_dimension=0, tiled=True
            ).astype(jnp.float32),
            lax.psum_scatter(
                partial_sums[6].astype(jnp.bfloat16), "fsdp", scatter_dimension=0, tiled=True
            ).astype(jnp.float32),
            lax.psum_scatter(
                partial_sums[7].astype(jnp.bfloat16), "fsdp", scatter_dimension=0, tiled=True
            ).astype(jnp.float32),
            lax.psum_scatter(
                partial_sums[8].astype(jnp.bfloat16), "fsdp", scatter_dimension=0, tiled=True
            ).astype(jnp.float32),
        )
        layer_grads[layer] = (
            reduced[0].transpose(1, 0, 2),
            reduced[1],
            reduced[2],
            reduced[3],
            reduced[4].T,
            reduced[5],
            reduced[6],
            reduced[7].T,
            reduced[8].T,
        )
    grad_inputs = grad.astype(jnp.bfloat16).reshape(inputs.shape)
    return (
        output,
        grad_inputs,
        jnp.stack([member[0] for member in layer_grads]),
        jnp.stack([member[1] for member in layer_grads]),
        jnp.stack([member[2] for member in layer_grads]),
        jnp.stack([member[3] for member in layer_grads]),
        jnp.stack([member[4] for member in layer_grads]),
        jnp.stack([member[5] for member in layer_grads]),
        jnp.stack([member[6] for member in layer_grads]),
        jnp.stack([member[7] for member in layer_grads]),
        jnp.stack([member[8] for member in layer_grads]),
    )


def one_group_per_sequence(mesh, seqs):
    return mesh.shape["fsdp"] == 4 and mesh.shape["ctx"] == seqs


def solution(mesh):
    def run(*arrays):
        seqs = arrays[0].shape[0]
        chosen = grouped(mesh.shape["ctx"] // 2, 2) if one_group_per_sequence(mesh, seqs) else body
        return on_devices(mesh, chosen)(*arrays)

    return run


def on_devices(mesh, chosen):
    return jax.shard_map(
        chosen,
        mesh=mesh,
        in_specs=(
            P("fsdp", "ctx", None),
            P(None, None, ("ctx", "fsdp"), None),
            P(None, ("ctx", "fsdp"), None),
            P(None, ("ctx", "fsdp"), None),
            P(None, ("ctx", "fsdp"), None),
            P(None, None, ("ctx", "fsdp")),
            P(None, ("ctx", "fsdp")),
            P(None, ("ctx", "fsdp")),
            P(None, None, ("ctx", "fsdp")),
            P(None, None, ("ctx", "fsdp")),
            P("fsdp", "ctx", None),
        ),
        out_specs=(
            P("fsdp", "ctx", None),
            P("fsdp", "ctx", None),
            P(None, None, ("ctx", "fsdp"), None),
            P(None, ("ctx", "fsdp"), None),
            P(None, ("ctx", "fsdp"), None),
            P(None, ("ctx", "fsdp"), None),
            P(None, None, ("ctx", "fsdp")),
            P(None, ("ctx", "fsdp")),
            P(None, ("ctx", "fsdp")),
            P(None, None, ("ctx", "fsdp")),
            P(None, None, ("ctx", "fsdp")),
        ),
        check_vma=False,
    )
```

```python
import functools
import types

import jax
import jax.numpy as jnp
from jax import lax
from jax.experimental import pallas as pl
from jax.experimental.pallas import tpu as pltpu
from jax.sharding import PartitionSpec as P

D = 768
HEADS = 12
HEAD_DIM = 64
LAYERS = 2
KERNEL_VMEM = 63 * 2**20


BF = jnp.bfloat16
F32 = jnp.float32
MESH = pl.DeviceIdType.MESH
MEMBERS = 4
LOCAL_HEADS = HEADS // MEMBERS
PACK = 640
SLOT = 64
PIECE = 64


def dot_nn(left, right):
    return lax.dot_general(left, right, (((1,), (0,)), ((), ())), preferred_element_type=F32)


def dot_nt(left, right):
    return lax.dot_general(left, right, (((1,), (1,)), ((), ())), preferred_element_type=F32)


def dot_tn(left, right):
    return lax.dot_general(left, right, (((0,), (0,)), ((), ())), preferred_element_type=F32)


def dot_exact(left, right):
    return lax.dot_general(
        left,
        right,
        (((1,), (0,)), ((), ())),
        precision=lax.Precision.HIGHEST,
        preferred_element_type=F32,
    )


def packed_lanes(shape, axis):
    lane = lax.broadcasted_iota(jnp.int32, shape, axis)
    slot = lane >> 6
    head = jnp.where(slot >= 6, 2, slot & 1)
    is_query = (slot < 2) | (slot == 6)
    is_value = (slot == 4) | (slot == 5) | (slot == 8)
    return (head * HEAD_DIM + (lane & 63), is_query, is_value)


def scratch_layout(nz, ny, rows, half, d_rows, f_rows):
    dma = pltpu.SemaphoreType.DMA
    two = 2 * d_rows
    ff = nz * ny * f_rows
    vm = pltpu.VMEM
    return dict(
        wq=vm((LAYERS, nz, 2, ny, two, PACK), BF),
        wu=vm((LAYERS, nz, 2, ny, two, ff), BF),
        wd=vm((LAYERS, nz, ny, f_rows, D), BF),
        wog=vm((nz, ny, two, D), BF),
        wo=vm((LAYERS, 256, D), BF),
        smg=vm((nz, ny, MEMBERS, 32, 128), BF),
        qi=vm((MEMBERS, two, PACK), BF),
        ui=vm((MEMBERS, two, ff), BF),
        oi=vm((two, D), BF),
        sf=vm((32, 128), F32),
        si=vm((32, 128), BF),
        qs=vm((MEMBERS, two, PACK), BF),
        us=vm((MEMBERS, two, ff), BF),
        pb=vm((16, D), F32),
        ub=vm((16, ff), F32),
        bq=vm((LAYERS, 8, PACK), F32),
        xf=vm((LAYERS, rows, D), BF),
        qkv=vm((LAYERS, rows, PACK), BF),
        prob=vm((LAYERS, LOCAL_HEADS, rows, rows), BF),
        mix=vm((LAYERS, rows, 256), F32),
        mixl=vm((LAYERS, rows, 256), BF),
        xh1=vm((LAYERS, half, D), F32),
        iv1=vm((LAYERS, half, 128), F32),
        nl=vm((LAYERS, rows, D), BF),
        gp=vm((LAYERS, rows, ff), F32),
        act=vm((LAYERS, rows, ff), BF),
        xh2=vm((LAYERS, half, D), F32),
        iv2=vm((LAYERS, half, 128), F32),
        stream=vm((half, D), F32),
        normed=vm((half, D), F32),
        ct=vm((half, D), BF),
        ownp=vm((half, D), F32),
        sibs=vm((2, half, D), BF),
        sibr=vm((2, half, D), BF),
        xs=vm((2, half, D), BF),
        xr=vm((2, half, D), BF),
        dl=vm((rows, D), BF),
        db=vm((rows, D), BF),
        du=vm((rows, ff), BF),
        dq=vm((rows, PACK), BF),
        dm=vm((rows, 256), BF),
        ds=vm((LOCAL_HEADS, rows, rows), BF),
        back=vm((2, half, D), BF),
        land=vm((2, 2, rows // (2 * nz), D), BF),
        gq=vm((LAYERS, nz, 2, ny, two, PACK), BF),
        gu=vm((LAYERS, nz, 2, ny, two, ff), BF),
        gd=vm((LAYERS, nz, ny, f_rows, D), BF),
        go=vm((LAYERS, nz, ny, 32, D), BF),
        ryq=vm((LAYERS, nz, 2, two, PACK), BF),
        ryu=vm((LAYERS, nz, 2, two, ff), BF),
        ryd=vm((nz, f_rows, D), BF),
        ryl=vm((f_rows, D), BF),
        syl=vm((f_rows, D), BF),
        ryo=vm((LAYERS, nz, 32, D), BF),
        rzq=vm((LAYERS, 4, 2, two, PACK), BF),
        rzu=vm((LAYERS, 4, 2, two, ff), BF),
        rzd=vm((4, f_rows, D), BF),
        rzl=vm((4, 2, f_rows, D), BF),
        rzo=vm((LAYERS, 4, 32, D), BF),
        fq=vm((LAYERS, 2, two, PACK), F32),
        fu=vm((LAYERS, 2, two, ff), F32),
        fo=vm((LAYERS, d_rows, D), F32),
        oq=vm((LAYERS, MEMBERS, d_rows, PACK), F32),
        ou=vm((LAYERS, MEMBERS, d_rows, ff), F32),
        oo=vm((LAYERS, d_rows, D), F32),
        sg=vm((LAYERS, 8, D), F32),
        sgy=vm((LAYERS, 8, D), F32),
        sgt=vm((LAYERS, 8, D), F32),
        sgz=vm((LAYERS, nz, 8, D), F32),
        sga=vm((LAYERS, MEMBERS, 8, D), F32),
        stage_s=dma((3, 3)),
        stage_r=dma((3, 3)),
        perm=dma((2,)),
        in_s=dma((4, 2)),
        in_r=dma((4, 2)),
        inx_s=dma((2, 2)),
        inx_r=dma((2, 2)),
        ins_s=dma((1,)),
        ins_r=dma((1,)),
        gz_s=dma((8, nz)),
        gz_r=dma((8, nz)),
        gy_s=dma((8, nz)),
        gy_r=dma((8, nz)),
        sib_s=dma((2, half // PIECE)),
        sib_r=dma((2, half // PIECE)),
        x_s=dma((2, half // PIECE)),
        x_r=dma((2, half // PIECE)),
        ag_s=dma((2, half // PIECE)),
        ag_r=dma((2, half // PIECE)),
        ry_s=dma((8,)),
        ry_r=dma((8,)),
        rz_s=dma((8, nz)),
        rz_r=dma((8, nz)),
        fin_s=dma((LAYERS, 2, 3)),
        fin_r=dma((LAYERS, 2, 3)),
        fino=dma((LAYERS, 2)),
        sgy_s=dma((LAYERS,)),
        sgy_r=dma((LAYERS,)),
        sgz_s=dma((LAYERS, nz)),
        sgz_r=dma((LAYERS, nz)),
        sga_s=dma((LAYERS, 3)),
        sga_r=dma((LAYERS, 3)),
    )


def group_kernel(layout, nz, *refs):
    inp, w_qkv, w_out, w_up, d_in, biases, value_bias, up_bias, gains, shifts, cot = refs[:11]
    out, gin, g_qkv, o_out, g_up, d_out, g_biases, g_value, g_raise, g_gains, g_shifts = refs[11:22]
    S = types.SimpleNamespace(**dict(zip(layout.keys(), refs[22:])))
    q_in, u_in, o_in, s_in = S.qi, S.ui, S.oi, S.si
    rows = S.dl.shape[0]
    half = rows // 2
    block = inp.shape[1]
    d_rows = w_out.shape[1]
    f_rows = d_in.shape[1]
    two = 2 * d_rows
    ff = S.du.shape[1]
    pieces = half // PIECE
    place = lax.axis_index("ctx")
    lane_f = lax.axis_index("fsdp")
    z, x = lax.div(place, 2), lax.rem(place, 2)
    y, c = lax.div(lane_f, 2), lax.rem(lane_f, 2)
    m = 2 * x + c
    d = 4 * place + lane_f
    devices = 8 * nz

    def dev(z_at, x_at, y_at, c_at):
        return (2 * z_at + x_at, 2 * y_at + c_at)

    def rcopy(source, target, send, recv, to):
        return pltpu.make_async_remote_copy(
            src_ref=source,
            dst_ref=target,
            send_sem=send,
            recv_sem=recv,
            device_id=to,
            device_id_type=MESH,
        )

    barrier = pltpu.get_barrier_semaphore()

    def hail(step, carry):
        other = lax.rem(d + step, devices)
        pl.semaphore_signal(
            barrier, inc=1, device_id=(lax.div(other, 4), lax.rem(other, 4)), device_id_type=MESH
        )
        return carry

    lax.fori_loop(1, devices, hail, 0)

    lane_low = lax.broadcasted_iota(jnp.int32, (1, 128), 1) < HEAD_DIM

    def turn(value):
        return pltpu.roll(value, HEAD_DIM, 1)

    def pack_heads(layer, pair):
        tiles = []
        for kind in range(3):
            base = 2 * pair * LOCAL_HEADS * HEAD_DIM
            whole = w_qkv[layer, kind, :, base : base + 384].astype(F32)
            tiles.append([whole[:, 0:128], whole[:, 128:256], whole[:, 256:384]])
        (q0, q1, q2), (k0, k1, k2), (v0, v1, v2) = tiles
        even = (q0, k0, v0, jnp.where(lane_low, q1, turn(k1)), jnp.where(lane_low, v1, 0.0))
        odd = (
            jnp.where(lane_low, turn(q1), turn(q2)),
            jnp.where(lane_low, turn(k1), turn(k2)),
            jnp.where(lane_low, turn(v1), turn(v2)),
            jnp.where(lane_low, turn(q2), k2),
            jnp.where(lane_low, turn(v2), 0.0),
        )
        return [jnp.concatenate(part, axis=1) for part in (even, odd)]

    for pair in range(2):
        packed = [pack_heads(layer, pair) for layer in range(LAYERS)]
        for odd in range(2):
            both = jnp.concatenate([part[odd] for part in packed], axis=0)
            q_in[2 * pair + odd] = both.astype(BF)

    def owner_block(z_at, x_at, y_at, c_at):
        at = (8 * z_at + 4 * x_at + 2 * y_at + c_at) * f_rows
        return slice(at, at + f_rows)

    grid_places = [(z_at, y_at) for z_at in range(nz) for y_at in range(2)]

    def pack_raise():
        wide = [w_up[layer].astype(F32) for layer in range(LAYERS)]
        for x_at in range(2):
            for c_at in range(2):
                both = [
                    jnp.concatenate(
                        [part[:, owner_block(z_at, x_at, y_at, c_at)] for z_at, y_at in grid_places], axis=1
                    )
                    for part in wide
                ]
                u_in[2 * x_at + c_at] = jnp.concatenate(both, axis=0).astype(BF)

    def pack_small():
        S.sf[...] = jnp.zeros_like(S.sf)
        for layer in range(LAYERS):
            base = 8 * layer
            S.sf[base : base + 3, 0:d_rows] = biases[layer].astype(F32)
            S.sf[base + 3 : base + 4, 0:d_rows] = value_bias[layer : layer + 1].astype(F32)
            S.sf[base + 4 : base + 6, 0:d_rows] = gains[layer].astype(F32)
            S.sf[base + 6 : base + 8, 0:d_rows] = shifts[layer].astype(F32)
            S.sf[16 + layer : 17 + layer, 0:f_rows] = up_bias[layer : layer + 1].astype(F32)
        s_in[...] = S.sf[...].astype(BF)

    pack_small()
    pack_raise()
    o_in[...] = jnp.concatenate([w_out[layer].astype(F32) for layer in range(LAYERS)], axis=0).astype(BF)
    pl.semaphore_wait(barrier, devices - 1)

    relation = ((x, 1 - c), (1 - x, c), (1 - x, 1 - c))
    sibling = dev(z, x, y, 1 - c)
    peer = dev(z, 1 - x, y, c)
    across = dev(z, x, 1 - y, c)

    def stage_copy(kind, r):
        x_r, c_r = relation[r]
        m_r = 2 * x_r + c_r
        source = (s_in, q_in.at[m_r], u_in.at[m_r])[kind]
        target = (S.smg.at[z, y, m], S.qs.at[m], S.us.at[m])[kind]
        return rcopy(source, target, S.stage_s.at[kind, r], S.stage_r.at[kind, r], dev(z, x_r, y, c_r))

    def stage_wait(kind, r):
        x_r, c_r = relation[r]
        m_r = 2 * x_r + c_r
        target = (S.smg.at[z, y, m_r], S.qs.at[m_r], S.us.at[m_r])[kind]
        rcopy(
            target, target, S.stage_s.at[kind, r], S.stage_r.at[kind, r], dev(z, x_r, y, c_r)
        ).wait_recv()

    for kind in (1, 0):
        for r in (1, 2, 0):
            stage_copy(kind, r).start()

    def own_block(j):
        return (2 * c + j == z) & (lax.div(z, 2) == c)

    def scatter_in(which, source, target, position):
        for j in range(2):
            copy = rcopy(
                source.at[j],
                target.at[pl.ds(position, block)],
                S.in_s.at[which, j],
                S.in_r.at[which, lax.rem(z, 2)],
                dev(2 * c + j, x, y, lax.div(z, 2)),
            )

            @pl.when(own_block(j))
            def _():
                target[pl.ds(position, block), :] = source[j]

            @pl.when(jnp.logical_not(own_block(j)))
            def _():
                copy.start()

    def scatter_in_wait(which, source, target, base):
        for k in range(2):

            @pl.when(2 * c + k != z)
            def _():
                spot = target.at[pl.ds(base + 2 * block * k, block)]
                rcopy(
                    spot, spot, S.in_s.at[which, 0], S.in_r.at[which, k], peer
                ).wait_recv()

    def scatter_in_drain(which, source, target):
        for j in range(2):

            @pl.when(jnp.logical_not(own_block(j)))
            def _():
                rcopy(
                    source.at[j], source.at[j], S.in_s.at[which, j], S.in_r.at[which, 0], peer
                ).wait_send()

    first = S.xf.at[0]
    scatter_in(0, inp, first, block * place)

    perm_to = dev(2 * x + y, lax.div(z, 2), c, lax.rem(z, 2))
    perm_stays = (2 * x + y == z) & (lax.div(z, 2) == x) & (c == y) & (lax.rem(z, 2) == c)
    perm_copy = rcopy(o_in, S.wog.at[2 * x + y, c], S.perm.at[0], S.perm.at[1], perm_to)

    @pl.when(perm_stays)
    def _():
        S.wog[z, y] = o_in[...]

    def start_perm():
        @pl.when(jnp.logical_not(perm_stays))
        def _():
            perm_copy.start()

    start_perm()
    for r in (1, 2, 0):
        stage_copy(2, r).start()
    S.smg[z, y, m] = s_in[...]
    S.qs[m] = q_in[m]
    S.us[m] = u_in[m]
    for layer in range(LAYERS):
        S.wd[layer, z, y] = d_in[layer]

    def join(staged, target):
        for xx in range(2):
            first_part = staged[2 * xx].astype(F32)
            second_part = staged[2 * xx + 1].astype(F32)
            for layer in range(LAYERS):
                cut = slice(layer * d_rows, (layer + 1) * d_rows)
                target[layer, z, xx, y] = jnp.concatenate(
                    [first_part[cut], second_part[cut]], axis=0
                ).astype(BF)

    side = lax.div(z, 2)
    inner = (z == 1) | (z == 2)
    outer = jnp.logical_not(inner)
    near_in, near_out = 1 + side, 3 * side
    far_in, far_out = 2 - side, 3 * (1 - side)
    buddy = near_in + near_out - z

    def at_z(z_at):
        return dev(z_at, x, y, c)

    LAST = -1
    DIRECT = 0

    def slab(cls, z_at, y_at):
        return (
            lambda: S.smg.at[z_at, y_at],
            lambda: S.wq.at[0, z_at, :, y_at],
            lambda: S.wog.at[z_at, y_at],
            lambda: S.wu.at[0, z_at, :, y_at],
            lambda: S.wd.at[0, z_at, y_at],
            lambda: S.wq.at[1, z_at, :, y_at],
            lambda: S.wu.at[1, z_at, :, y_at],
            lambda: S.wd.at[1, z_at, y_at],
        )[cls]()

    def z_copy(cls, n, z_at, to):
        spot = S.wd.at[1, z_at] if cls == LAST else slab(cls, z_at, y)
        return rcopy(spot, spot, S.gz_s.at[cls, n], S.gz_r.at[cls, z_at], at_z(to))

    def y_copy(cls, z_at):
        spot = slab(cls, z_at, y)
        return rcopy(spot, spot, S.gy_s.at[cls, z_at], S.gy_r.at[cls, z_at], across)

    def gather_direct(cls):
        z_copy(cls, 0, z, buddy).start()
        z_copy(cls, 1, z, far_in).start()
        if cls < DIRECT:
            z_copy(cls, 2, z, far_out).start()

    def gather_start(cls):
        if cls != LAST:
            gather_direct(cls)
        y_copy(cls, z).start()

    def gather_cross(cls):
        if cls != LAST:
            return
        spot = slab(cls, z, 1 - y)
        rcopy(spot, spot, S.gy_s.at[cls, z], S.gy_r.at[cls, z], across).wait_recv()
        gather_direct(cls)

    def gather_take(cls, z_at, relay):
        z_copy(cls, 0, z_at, buddy).wait_recv()
        if relay is not None:
            z_copy(cls, relay, z_at, near_out).start()
        if cls != LAST:
            y_copy(cls, z_at).start()

    def gather_relay(cls):
        gather_take(cls, buddy, None)
        if cls < DIRECT:
            gather_take(cls, far_in, None)
            gather_take(cls, far_out, None)
            return

        @pl.when(inner)
        def _():
            gather_take(cls, far_in, 2)

        gather_relay_far(cls)

    def gather_relay_far(cls):
        @pl.when(inner)
        def _():
            gather_take(cls, far_out, 3)

    def gather_end(cls):
        @pl.when(outer)
        def _():
            gather_take(cls, far_in, None)
            gather_take(cls, far_out, None)

    def gather_wait(cls):
        if cls == LAST:
            spot = S.wd.at[1, z]
            return

        def one(t):
            spot = slab(cls, t, 1 - y)
            rcopy(spot, spot, S.gy_s.at[cls, t], S.gy_r.at[cls, t], across).wait_recv()

        for t in (z, buddy, far_in, far_out):
            one(t)

    def gather_drain(cls):
        z_copy(cls, 0, z, buddy).wait_send()
        z_copy(cls, 1, z, far_in).wait_send()
        if cls < DIRECT:
            z_copy(cls, 2, z, far_out).wait_send()
        else:

            @pl.when(inner)
            def _():
                z_copy(cls, 2, far_in, near_out).wait_send()
                z_copy(cls, 3, far_out, near_out).wait_send()

        def one(t, carry):
            y_copy(cls, t).wait_send()
            return carry

        if cls == LAST:
            one(z, 0)
        else:
            lax.fori_loop(0, nz, one, 0)

    for r in range(3):
        stage_wait(1, r)
    join(S.qs, S.wq)
    gather_start(1)
    for r in range(3):
        stage_wait(0, r)
    gather_start(0)

    def x_spots(target, base, mine):
        return [target.at[pl.ds(base + block * (2 * k + mine), block)] for k in range(2)]

    def swap_start(which, target, base):
        for k, spot in enumerate(x_spots(target, base, x)):
            rcopy(spot, spot, S.inx_s.at[which, k], S.inx_r.at[which, k], peer).start()

    def swap_wait(which, target, base):
        for k, spot in enumerate(x_spots(target, base, 1 - x)):
            rcopy(spot, spot, S.inx_s.at[which, k], S.inx_r.at[which, k], peer).wait_recv()
        for k, spot in enumerate(x_spots(target, base, x)):
            rcopy(spot, spot, S.inx_s.at[which, k], S.inx_r.at[which, k], peer).wait_send()

    mine = half * c
    theirs = half * (1 - c)
    scatter_in_wait(0, inp, first, mine + block * x)
    swap_start(0, first, mine)
    for r in range(3):
        stage_wait(2, r)
    join(S.us, S.wu)
    gather_relay(1)
    gather_relay(0)
    swap_wait(0, first, mine)
    spot = first.at[pl.ds(mine, half)]
    rcopy(spot, spot, S.ins_s.at[0], S.ins_r.at[0], sibling).start()
    S.stream[...] = S.xf[0, pl.ds(mine, half), :].astype(F32)

    @pl.when(jnp.logical_not(perm_stays))
    def _():
        spot = S.wog.at[z, y]
        rcopy(spot, spot, S.perm.at[0], S.perm.at[1], peer).wait_recv()

    gather_start(2)
    gather_end(1)
    gather_end(0)
    gather_relay(2)
    gather_start(3)
    gather_wait(0)

    def small_params():
        row_shape = (devices * 16, D)
        lane = lax.broadcasted_iota(jnp.int32, (128, D), 0)
        col = lax.broadcasted_iota(jnp.int32, (128, D), 1)
        tile = jnp.where(lax.rem(col, d_rows) == lane, 1.0, 0.0).astype(BF)
        packs = S.smg[:, :, :, 0:16, :].reshape(devices * 16, 128)
        spread = dot_nn(packs, tile)
        owner_row = lax.broadcasted_iota(jnp.int32, row_shape, 0) >> 4
        zz = owner_row >> 3
        yy = (owner_row >> 2) & 1
        xx = (owner_row >> 1) & 1
        cc = owner_row & 1
        owner = zz * 8 + xx * 4 + yy * 2 + cc
        at = lax.div(lax.broadcasted_iota(jnp.int32, row_shape, 1), d_rows)
        spread = jnp.where(owner == at, spread, 0.0)
        S.pb[...] = jnp.sum(spread.reshape(devices, 16, D), axis=0)
        lane = lax.broadcasted_iota(jnp.int32, (128, ff), 0)
        col = lax.broadcasted_iota(jnp.int32, (128, ff), 1)
        tile = jnp.where(lax.rem(col, f_rows) == lane, 1.0, 0.0).astype(BF)
        packs = S.smg[:, :, m, 16:32, :].reshape(2 * nz * 16, 128)
        spread = dot_nn(packs, tile)
        row_shape = (2 * nz * 16, ff)
        owner = lax.broadcasted_iota(jnp.int32, row_shape, 0) >> 4
        at = lax.div(lax.broadcasted_iota(jnp.int32, row_shape, 1), f_rows)
        spread = jnp.where(owner == at, spread, 0.0)
        S.ub[...] = jnp.sum(spread.reshape(2 * nz, 16, ff), axis=0)
        source = lax.broadcasted_iota(jnp.int32, (D, PACK), 0)
        target, unused_q, unused_v = packed_lanes((D, PACK), 1)
        pick = jnp.where(source == target + m * (LOCAL_HEADS * HEAD_DIM), 1.0, 0.0).astype(BF)
        picked = dot_nn(S.pb[...].astype(BF), pick)
        unused, is_query, is_value = packed_lanes((1, PACK), 1)
        for layer in range(LAYERS):
            base = 8 * layer
            row = jnp.where(is_query, picked[base : base + 1], 0.0)
            row = jnp.where(is_value, picked[base + 3 : base + 4], row)
            S.bq[layer, 0:1, :] = row

    small_params()
    scatter_in(1, cot, S.ct, block * (2 * lax.rem(z, 2) + x))

    def param(layer, kind):
        return S.pb[8 * layer + kind : 8 * layer + kind + 1, :]

    def piece_rows(i):
        return pl.ds(i * PIECE if isinstance(i, int) else pl.multiple_of(i * PIECE, PIECE), PIECE)

    def own_rows(i):
        return pl.ds(pl.multiple_of(mine + i * PIECE, PIECE), PIECE)

    def other_rows(i):
        return pl.ds(pl.multiple_of(theirs + i * PIECE, PIECE), PIECE)

    every = slice(None)

    def load_both(ref, i, cols=every):
        return jnp.concatenate([ref[other_rows(i), cols], ref[own_rows(i), cols]], axis=0)

    def store_both(ref, i, value, cols=every):
        ref[other_rows(i), cols] = value[:PIECE]
        ref[own_rows(i), cols] = value[PIECE:]

    def spread_start(par, i, ref, value):
        ref[own_rows(i), :] = value
        spot = ref.at[own_rows(i)]
        rcopy(spot, spot, S.ag_s.at[par, i], S.ag_r.at[par, i], sibling).start()

    def spread_wait(par, i, ref):
        got = ref.at[other_rows(i)]
        sent = ref.at[own_rows(i)]
        rcopy(got, got, S.ag_s.at[par, i], S.ag_r.at[par, i], sibling).wait_recv()
        rcopy(sent, sent, S.ag_s.at[par, i], S.ag_r.at[par, i], sibling).wait_send()

    def sib_copy(par, i):
        at = piece_rows(i)
        return rcopy(
            S.sibs.at[par, at], S.sibr.at[par, at], S.sib_s.at[par, i], S.sib_r.at[par, i], sibling
        )

    def peer_copy(par, i):
        at = piece_rows(i)
        return rcopy(S.xs.at[par, at], S.xr.at[par, at], S.x_s.at[par, i], S.x_r.at[par, i], peer)

    def part_send(par, i, value):
        at = piece_rows(i)
        S.sibs[par, at, :] = value[:PIECE].astype(BF)
        sib_copy(par, i).start()
        S.ownp[at, :] = value[PIECE:]

    def part_pass(par, i):
        at = piece_rows(i)
        sib_copy(par, i).wait_recv()
        S.xs[par, at, :] = (S.ownp[at, :] + S.sibr[par, at, :].astype(F32)).astype(BF)
        peer_copy(par, i).start()

    def part_take(par, i):
        at = piece_rows(i)
        peer_copy(par, i).wait_recv()
        return S.xs[par, at, :].astype(F32) + S.xr[par, at, :].astype(F32)

    def part_drain(par):
        for i in range(pieces):
            sib_copy(par, i).wait_send()
            peer_copy(par, i).wait_send()

    def pipeline(stages, between=None):
        def one(step, carry):
            for lag, stage in enumerate(stages):
                if len(stages) == 1:
                    stage(step)
                    continue

                @pl.when((step >= lag) & (step < pieces + lag))
                def _():
                    stage(step - lag)

            for after, calls in (between or {}).items():

                @pl.when(step == after)
                def _():
                    for call in calls:
                        call()

            return carry

        lax.fori_loop(0, pieces + len(stages) - 1, one, 0)

    def norm_piece(total, at, layer, gain, shift, scaled_ref, inv_ref):
        centred = total - jnp.mean(total, axis=1, keepdims=True)
        inv = lax.rsqrt(jnp.mean(centred * centred, axis=1, keepdims=True) + 1e-12)
        scaled = centred * inv
        scaled_ref[layer, at, :] = scaled
        inv_ref[layer, at, :] = jnp.broadcast_to(inv, (PIECE, 128))
        return scaled * gain + shift

    def flat(value):
        return value.reshape(-1, value.shape[-1])

    def swap_lanes(value):
        return pltpu.roll(value.astype(F32), HEAD_DIM, 1).astype(BF)

    def mask_queries(queries, h):
        keep = jnp.logical_not(lane_low) if h == 1 else lane_low
        return jnp.where(keep, queries * jnp.asarray(HEAD_DIM**-0.5, BF), jnp.zeros((), BF))

    def query_cols(h):
        return slice(0, 128) if h < 2 else slice(384, 512)

    def head_keys(layer, h):
        if h < 2:
            return S.qkv[layer, :, 128:256]
        return swap_lanes(S.qkv[layer, :, 384:512])

    def head_values(layer, h):
        return S.qkv[layer, :, 256:384] if h < 2 else S.qkv[layer, :, 512:640]

    def project(layer, i):
        value = dot_nn(load_both(S.xf.at[layer], i), flat(S.wq[layer])) + S.bq[layer, 0:1, :]
        store_both(S.qkv.at[layer], i, value.astype(BF))

    def attend(layer, i):
        mixes = []
        for h in range(LOCAL_HEADS):
            queries = mask_queries(load_both(S.qkv.at[layer], i, query_cols(h)), h)
            scores = dot_nt(queries, head_keys(layer, h))
            weights = jnp.exp(scores - jnp.max(scores, axis=1, keepdims=True))
            weights = (weights * (1.0 / jnp.sum(weights, axis=1, keepdims=True))).astype(BF)
            store_both(S.prob.at[layer, h], i, weights)
            mixes.append(dot_nn(weights, head_values(layer, h)))
        mix = jnp.concatenate(
            [jnp.where(lane_low, mixes[0], mixes[1]), jnp.where(lane_low, mixes[2], 0.0)], axis=1
        )
        store_both(S.mix.at[layer], i, mix)
        store_both(S.mixl.at[layer], i, mix.astype(BF))
        part_send(0, i, dot_nn(mix.astype(BF), S.wo[layer]))

    def after_attention(layer, i):
        at = piece_rows(i)
        total = S.stream[at, :] + part_take(0, i) + param(layer, 1)
        normed = norm_piece(total, at, layer, param(layer, 4), param(layer, 6), S.xh1, S.iv1)
        S.normed[at, :] = normed
        spread_start(0, i, S.nl.at[layer], normed.astype(BF))

    def raise_part(layer, i):
        spread_wait(0, i, S.nl.at[layer])
        rounded = load_both(S.nl.at[layer], i)
        upward = dot_nn(rounded, flat(S.wu[layer])) + S.ub[layer : layer + 1, :]
        cdf = 0.5 * (1.0 + lax.erf(upward * (0.5**0.5)))
        density = jnp.exp(-0.5 * upward * upward) * ((2.0 * jnp.pi) ** -0.5)
        store_both(S.act.at[layer], i, (upward * cdf).astype(BF))
        store_both(S.gp.at[layer], i, cdf + upward * density)

    def lower_part(layer, i):
        part_send(1, i, dot_nn(load_both(S.act.at[layer], i), flat(S.wd[layer])))

    def after_lower(layer, i):
        at = piece_rows(i)
        total = S.normed[at, :] + part_take(1, i) + param(layer, 2)
        result = norm_piece(total, at, layer, param(layer, 5), param(layer, 7), S.xh2, S.iv2)
        if layer < LAYERS - 1:
            S.stream[at, :] = result
            spread_start(1, i, S.xf.at[layer + 1], result.astype(BF))
        else:
            S.back[0, at, :] = result.astype(BF)

    def next_project(layer, i):
        spread_wait(1, i, S.xf.at[layer])
        project(layer, i)

    def scatter_out(which, source):
        for k in range(2):
            stays = (2 * c + k == z) & (lax.div(z, 2) == c)
            spot = source.at[pl.ds(pl.multiple_of(block * (2 * k + x), block), block)]
            slot = lax.rem(z, 2)

            @pl.when(stays)
            def _():
                S.land[which, slot] = spot[...]

            @pl.when(jnp.logical_not(stays))
            def _():
                rcopy(
                    spot,
                    S.land.at[which, slot],
                    S.in_s.at[2 + which, k],
                    S.in_r.at[2 + which, slot],
                    dev(2 * c + k, x, y, lax.div(z, 2)),
                ).start()

    def scatter_out_wait(which, source, result):
        for k in range(2):
            spot = source.at[pl.ds(pl.multiple_of(block * (2 * k + x), block), block)]

            @pl.when(jnp.logical_not((2 * c + k == z) & (lax.div(z, 2) == c)))
            def _():
                rcopy(
                    spot, spot, S.in_s.at[2 + which, k], S.in_r.at[2 + which, 0], peer
                ).wait_send()

            @pl.when(jnp.logical_not(own_block(k)))
            def _():
                landed = S.land.at[which, k]
                rcopy(
                    landed, landed, S.in_s.at[2 + which, 0], S.in_r.at[2 + which, k], peer
                ).wait_recv()

        result[...] = S.land[which]

    def out_weights():
        gather_wait(2)
        for layer in range(LAYERS):
            cut = slice(layer * d_rows, (layer + 1) * d_rows)
            parts = [S.wog[t, yy].astype(F32)[cut] for t in range(nz) for yy in range(2)]
            parts.append(jnp.zeros((256 - 2 * nz * d_rows, D), F32))
            S.wo[layer] = jnp.concatenate(parts, axis=0).astype(BF)

    spot = first.at[pl.ds(theirs, half)]
    rcopy(spot, spot, S.ins_s.at[0], S.ins_r.at[0], sibling).wait_recv()
    gather_wait(1)
    for i in range(pieces):
        project(0, i)
    gather_start(4)
    gather_end(2)
    gather_relay(3)
    out_weights()
    pipeline(
        (lambda i: attend(0, i), lambda i: part_pass(0, i)),
        {1: [lambda: gather_end(3)], 2: [lambda: gather_start(5)], 3: [lambda: gather_relay(4)]},
    )
    pipeline((lambda i: after_attention(0, i),))
    part_drain(0)
    gather_start(6)
    gather_end(4)
    gather_wait(3)
    pipeline((lambda i: raise_part(0, i),))
    scatter_in_wait(1, cot, S.ct, block * x)
    gather_relay(5)
    gather_start(7)
    gather_end(5)
    gather_wait(4)
    pipeline((lambda i: lower_part(0, i), lambda i: part_pass(1, i)))
    swap_start(1, S.ct, 0)
    gather_relay(6)
    gather_wait(5)
    pipeline(
        (lambda i: after_lower(0, i), lambda i: next_project(1, i)),
        {0: [lambda: gather_end(6)], 3: [lambda: gather_cross(7)]},
    )
    part_drain(1)
    pipeline(
        (lambda i: attend(1, i), lambda i: part_pass(0, i)),
        {1: [lambda: gather_relay(7)], 3: [lambda: gather_end(7)]},
    )
    gather_wait(6)
    pipeline(
        (
            lambda i: after_attention(1, i),
            lambda i: raise_part(1, i),
            lambda i: lower_part(1, i),
            lambda i: part_pass(1, i),
        ),
        {1: [lambda: gather_wait(7)]},
    )
    part_drain(0)
    swap_wait(1, S.ct, 0)


    def add_row(layer, kind, value):
        S.sg[layer, kind : kind + 1, :] += jnp.sum(value, axis=0, keepdims=True)

    def norm_back_piece(grad, at, layer, which):
        scaled = (S.xh1 if which == 0 else S.xh2)[layer, at, :]
        inv = (S.iv1 if which == 0 else S.iv2)[layer, at, 0:1]
        add_row(layer, 2 + which, grad * scaled)
        add_row(layer, 4 + which, grad)
        weighted = grad * param(layer, 4 + which)
        back = (
            weighted
            - jnp.mean(weighted, axis=1, keepdims=True)
            - scaled * jnp.mean(weighted * scaled, axis=1, keepdims=True)
        ) * inv
        return back

    def lower_back(layer, i, grad):
        at = piece_rows(i)
        back = norm_back_piece(grad, at, layer, 1)
        S.normed[at, :] = back
        rounded = back.astype(BF)
        add_row(layer, 1, rounded.astype(F32))
        spread_start(0, i, S.dl, rounded)

    def raise_back(layer, i):
        spread_wait(0, i, S.dl)
        back = dot_nt(load_both(S.dl, i), flat(S.wd[layer])) * load_both(S.gp.at[layer], i)
        rounded = back.astype(BF)
        store_both(S.du, i, rounded)
        add_row(layer, 6, rounded.astype(F32))
        part_send(0, i, dot_nt(rounded, flat(S.wu[layer])))

    grads = (S.gq, S.gu, S.gd, S.go)
    from_y = (S.ryq, S.ryu, None, S.ryo)
    from_z = (S.rzq, S.rzu, None, S.rzo)

    def grad_slab(layer, kind, t, y_at):
        ref = grads[kind]
        return ref.at[layer, t, :, y_at] if kind < 2 else ref.at[layer, t, y_at]

    def z_first(layer, kind):
        return kind == 2 and layer == LAYERS - 1

    def z_slab(layer, kind, t):
        return S.gd.at[layer, t] if z_first(layer, kind) else grad_slab(layer, kind, t, y)

    def y_landing(layer, kind):
        if kind == 2:
            return S.ryl if z_first(layer, kind) else S.ryd
        return from_y[kind].at[layer]

    def z_landing(layer, kind, slot):
        if kind == 2:
            return (S.rzl if z_first(layer, kind) else S.rzd).at[slot]
        return from_z[kind].at[layer, slot]

    def reduce_y_copy(layer, kind):
        ref = grads[kind]
        if z_first(layer, kind):
            source = S.syl
        else:
            source = ref.at[layer, :, :, 1 - y] if kind < 2 else ref.at[layer, :, 1 - y]
        n = 4 * layer + kind
        return rcopy(source, y_landing(layer, kind), S.ry_s.at[n], S.ry_r.at[n], across)

    def reduce_z_copy(layer, kind, t, slot, to):
        n = 4 * layer + kind
        return rcopy(
            z_slab(layer, kind, t),
            z_landing(layer, kind, slot),
            S.rz_s.at[n, t],
            S.rz_r.at[n, slot],
            at_z(to),
        )

    def slab_add(target, other):
        if len(target.shape) == 3:
            for xx in range(2):
                target[xx] = (target[xx].astype(F32) + other[xx].astype(F32)).astype(BF)
        else:
            target[...] = (target[...].astype(F32) + other[...].astype(F32)).astype(BF)

    def reduce_direct(layer, kind):
        @pl.when(outer)
        def _():
            reduce_z_copy(layer, kind, far_in, 2, buddy).start()
            reduce_z_copy(layer, kind, far_out, 3, buddy).start()

        reduce_z_copy(layer, kind, buddy, 0, buddy).start()

    def reduce_start(layer, kind):
        if z_first(layer, kind):
            reduce_direct(layer, kind)
        else:
            reduce_y_copy(layer, kind).start()

    def reduce_first(layer, kind):
        reduce_y_copy(layer, kind).wait_recv()

        def one(t, carry):
            slab_add(grad_slab(layer, kind, t, y), y_landing(layer, kind).at[t])
            return carry

        lax.fori_loop(0, nz, one, 0)
        reduce_direct(layer, kind)

    def reduce_relay(layer, kind):
        @pl.when(inner)
        def _():
            for slot, t in ((2, far_in), (3, far_out)):
                reduce_z_copy(layer, kind, t, slot, buddy).wait_recv()
                slab_add(z_slab(layer, kind, t), z_landing(layer, kind, slot))
                reduce_z_copy(layer, kind, t, 1, t).start()

    def reduce_cross(layer):
        d_out[layer] = S.gd[layer, z, y].astype(F32)
        other = S.gd[layer, z, 1 - y].astype(F32)
        for slot in (0, 1):
            reduce_z_copy(layer, 2, z, slot, buddy).wait_recv()
            d_out[layer] += S.rzl[slot, y].astype(F32)
            other = other + S.rzl[slot, 1 - y].astype(F32)
        S.syl[...] = other.astype(BF)
        reduce_y_copy(layer, 2).start()

    def reduce_last_d(layer):
        reduce_y_copy(layer, 2).wait_recv()
        d_out[layer] += S.ryl[...].astype(F32)

    final = (S.fq, S.fu, d_out, S.fo)

    def reduce_last(layer, kind):
        if kind == 3:
            target = S.fo.at[layer]
            cut = lambda value: value[0:d_rows]
        else:
            target = final[kind].at[layer]
            cut = lambda value: value
        target[...] = cut(grad_slab(layer, kind, z, y)[...].astype(F32))

        for slot in (0, 1):
            reduce_z_copy(layer, kind, z, slot, buddy).wait_recv()
            target[...] += cut(z_landing(layer, kind, slot)[...].astype(F32))

        if kind < 2:
            result = (S.oq, S.ou)[kind]
            for r in (1, 2, 0):
                hand_copy(layer, kind, r).start()
            for xx in range(2):
                for cc in range(2):

                    @pl.when((x == xx) & (c == cc))
                    def _():
                        result[layer, 2 * xx + cc] = target[xx, cc * d_rows : (cc + 1) * d_rows, :]

        if kind == 3:
            @pl.when(owner_stays)
            def _():
                S.oo[layer] = target[...]

            @pl.when(jnp.logical_not(owner_stays))
            def _():
                owner_copy(layer).start()

    def hand_copy(layer, kind, r):
        x_r, c_r = relation[r]
        source = (S.fq, S.fu)[kind].at[
            layer, x_r, pl.ds(pl.multiple_of(c_r * d_rows, 8), d_rows)
        ]
        target = (S.oq, S.ou)[kind].at[layer, m]
        return rcopy(
            source,
            target,
            S.fin_s.at[layer, kind, r],
            S.fin_r.at[layer, kind, r],
            dev(z, x_r, y, c_r),
        )

    owner_to = dev(2 * x + c, lax.div(z, 2), lax.rem(z, 2), y)
    owner_stays = (2 * x + c == z) & (lax.div(z, 2) == x) & (lax.rem(z, 2) == y) & (y == c)

    def owner_copy(layer):
        return rcopy(
            S.fo.at[layer], S.oo.at[layer], S.fino.at[layer, 0], S.fino.at[layer, 1], owner_to
        )

    def reduce_drain(layer, kind):
        reduce_y_copy(layer, kind).wait_send()
        for t in range(nz):

            @pl.when(z != t)
            def _():
                reduce_z_copy(layer, kind, t, 0, buddy).wait_send()

        if kind < 2:
            for r in range(3):
                hand_copy(layer, kind, r).wait_send()
        if kind == 3:
            @pl.when(jnp.logical_not(owner_stays))
            def _():
                owner_copy(layer).wait_send()
                owner_copy(layer).wait_recv()

    def lower_grad(layer):
        for i in range(2):
            value = dot_tn(S.act[layer, :, i * (ff // 2) : (i + 1) * (ff // 2)], S.dl[...])
            S.gd[layer, i * (nz // 2) : (i + 1) * (nz // 2)] = value.astype(BF).reshape(
                nz // 2, 2, f_rows, D
            )
        reduce_start(layer, 2)

    def raise_grad(layer):
        for i in range(2):
            value = dot_tn(S.nl[layer, :, i * (D // 2) : (i + 1) * (D // 2)], S.du[...])
            S.gu[layer, i * (nz // 2) : (i + 1) * (nz // 2)] = value.astype(BF).reshape(
                nz // 2, 2, 2, two, ff
            )
        reduce_start(layer, 1)

    def out_grad(layer):
        value = dot_tn(S.mixl[layer], S.db[...])
        empty = jnp.zeros((32 - d_rows, D), F32)
        for t in range(nz):
            for yy in range(2):
                at = (2 * t + yy) * d_rows
                S.go[layer, t, yy] = jnp.concatenate(
                    [value[at : at + d_rows], empty], axis=0
                ).astype(BF)
        reduce_start(layer, 3)

    def project_grad(layer):
        for i in range(2):
            value = dot_tn(S.xf[layer, :, i * (D // 2) : (i + 1) * (D // 2)], S.dq[...])
            S.gq[layer, i * (nz // 2) : (i + 1) * (nz // 2)] = value.astype(BF).reshape(
                nz // 2, 2, 2, two, PACK
            )
        reduce_start(layer, 0)

    def branch_back(layer, i):
        at = piece_rows(i)
        back = norm_back_piece(part_take(0, i) + S.normed[at, :], at, layer, 0)
        S.stream[at, :] = back
        rounded = back.astype(BF)
        add_row(layer, 0, rounded.astype(F32))
        spread_start(1, i, S.db, rounded)

    scale = HEAD_DIM**-0.5

    def attend_back(layer, i):
        spread_wait(1, i, S.db)
        grad_mix = dot_nt(load_both(S.db, i), S.wo[layer]).astype(BF)
        store_both(S.dm, i, grad_mix)
        mix = load_both(S.mix.at[layer], i)
        results = []
        for h in range(LOCAL_HEADS):
            keep = jnp.logical_not(lane_low) if h == 1 else lane_low
            cols = slice(0, 128) if h < 2 else slice(128, 256)
            grad = jnp.where(keep, grad_mix[:, cols], jnp.zeros((), BF))
            delta = jnp.sum(grad.astype(F32) * mix[:, cols], axis=1, keepdims=True)
            grad_weights = dot_nt(grad, head_values(layer, h))
            weights = load_both(S.prob.at[layer, h], i).astype(F32)
            rounded = (weights * (grad_weights - delta)).astype(BF)
            store_both(S.ds.at[h], i, rounded)
            results.append((dot_nn(rounded, head_keys(layer, h)) * scale).astype(BF))
        store_both(S.dq, i, jnp.where(lane_low, results[0], results[1]), slice(0, 128))
        store_both(S.dq, i, results[2], slice(384, 512))

    def attend_back_end(layer):
        keys_back, values_back = [], []
        for h in range(LOCAL_HEADS):
            cols = slice(0, 128) if h < 2 else slice(128, 256)
            queries = mask_queries(S.qkv[layer, :, query_cols(h)], h)
            keys_back.append(dot_tn(S.ds[h], queries).astype(BF))
            values_back.append(dot_tn(S.prob[layer, h], S.dm[:, cols]).astype(BF))
        S.dq[:, 128:256] = jnp.where(lane_low, keys_back[0], keys_back[1])
        S.dq[:, 256:384] = jnp.where(lane_low, values_back[0], values_back[1])
        S.dq[:, 384:512] = jnp.where(lane_low, S.dq[:, 384:512], swap_lanes(keys_back[2]))
        S.dq[:, 512:640] = jnp.where(lane_low, values_back[2], jnp.zeros((), BF))
        S.sg[layer, 7:8, 0:PACK] = jnp.sum(S.dq[...].astype(F32), axis=0, keepdims=True)

    def project_back(layer, i):
        part_send(1, i, dot_nt(load_both(S.dq, i), flat(S.wq[layer])))

    def next_back(layer, i):
        at = piece_rows(i)
        grad = part_take(1, i) + S.stream[at, :]
        if layer > 0:
            lower_back(layer - 1, i, grad)
        else:
            S.back[1, at, :] = grad.astype(BF)

    def small_y(layer):
        return rcopy(S.sg.at[layer], S.sgy.at[layer], S.sgy_s.at[layer], S.sgy_r.at[layer], across)

    def small_z(layer, k):
        to = dev(lax.rem(z + k, nz), x, y, c)
        return rcopy(
            S.sgt.at[layer], S.sgz.at[layer, k], S.sgz_s.at[layer, k], S.sgz_r.at[layer, k], to
        )

    def small_member(layer, r):
        x_r, c_r = relation[r]
        return rcopy(
            S.sgt.at[layer],
            S.sga.at[layer, m],
            S.sga_s.at[layer, r],
            S.sga_r.at[layer, r],
            dev(z, x_r, y, c_r),
        )

    def small_one(layer):
        small_y(layer).start()

    def small_two(layer):
        small_y(layer).wait_recv()
        S.sgt[layer] = S.sg[layer] + S.sgy[layer]
        for k in range(1, nz):
            small_z(layer, k).start()

    def small_three(layer):
        for k in range(1, nz):
            small_z(layer, k).wait_recv()
        for k in range(1, nz):
            small_z(layer, k).wait_send()
        total = S.sgt[layer]
        for k in range(1, nz):
            total = total + S.sgz[layer, k]
        S.sgt[layer] = total
        for r in range(3):
            small_member(layer, r).start()
        S.sga[layer, m] = total

    def small_four(layer):
        for r in range(3):
            small_member(layer, r).wait_send()
            small_member(layer, r).wait_recv()
        small_y(layer).wait_send()
        lane = lax.broadcasted_iota(jnp.int32, (D, 128), 1)
        col = lax.broadcasted_iota(jnp.int32, (D, 128), 0)
        narrow = lane < d_rows
        pick = jnp.where((col == d_rows * d + lane) & narrow, 1.0, 0.0)
        both = S.sga[layer, 2 * x] + S.sga[layer, 2 * x + 1]
        found = dot_exact(both, pick)[:, 0:d_rows]
        g_biases[layer, 1:3, :] = found[0:2]
        g_gains[layer] = found[2:4]
        g_shifts[layer] = found[4:6]
        dim, is_query, is_value = packed_lanes((D, 128), 0)
        hit = (dim == d_rows * (d - 8 * z) + lane) & narrow
        attn = S.sga[layer, z]
        found = dot_exact(attn, jnp.where(hit & is_query, 1.0, 0.0))
        g_biases[layer, 0:1, :] = found[7:8, 0:d_rows]
        found = dot_exact(attn, jnp.where(hit & is_value, 1.0, 0.0))
        g_value[layer : layer + 1, :] = found[7:8, 0:d_rows]
        pick = jnp.where((col == f_rows * (2 * z + y) + lane) & (lane < f_rows), 1.0, 0.0)
        found = dot_exact(S.sga[layer, m], pick)
        g_raise[layer : layer + 1, :] = found[6:7, 0:f_rows]

    def hand_wait(layer, kind):
        for r in range(3):
            hand_copy(layer, kind, r).wait_recv()

    def unpack_heads(layer):
        hand_wait(layer, 0)
        for pair in range(2):
            even = [S.oq[layer, 2 * pair, :, 128 * t : 128 * t + 128] for t in range(5)]
            odd = [S.oq[layer, 2 * pair + 1, :, 128 * t : 128 * t + 128] for t in range(5)]
            thirds = (
                (even[3], turn(odd[3])),
                (turn(even[3]), odd[3]),
                (even[4], turn(odd[4])),
            )
            for kind in range(3):
                turned = turn(odd[kind])
                tiles = [
                    even[kind],
                    jnp.where(lane_low, thirds[kind][0], turned),
                    jnp.where(lane_low, turned, thirds[kind][1]),
                ]
                base = 384 * pair
                g_qkv[layer, kind, :, base : base + 384] = jnp.concatenate(tiles, axis=1)

    def unpack_raise(layer):
        hand_wait(layer, 1)
        wide = [S.ou[layer, member] for member in range(MEMBERS)]
        parts = []
        for z_at in range(nz):
            for x_at in range(2):
                for y_at in range(2):
                    for c_at in range(2):
                        at = (2 * z_at + y_at) * f_rows
                        parts.append(wide[2 * x_at + c_at][:, at : at + f_rows])
        g_up[layer] = jnp.concatenate(parts, axis=1)

    S.sg[...] = jnp.zeros_like(S.sg)

    def turn_back(i):
        after_lower(1, i)
        lower_back(1, i, S.ct[piece_rows(i), :].astype(F32))

    pipeline(
        (turn_back, lambda i: raise_back(1, i), lambda i: part_pass(0, i)),
        {4: [lambda: lower_grad(1)]},
    )
    part_drain(1)
    raise_grad(1)
    scatter_out(0, S.back.at[0])
    pipeline((lambda i: branch_back(1, i), lambda i: attend_back(1, i)))
    part_drain(0)
    attend_back_end(1)
    pipeline((lambda i: project_back(1, i), lambda i: part_pass(1, i)))
    small_one(1)
    project_grad(1)
    out_grad(1)
    reduce_first(1, 1)
    pipeline(
        (
            lambda i: next_back(1, i),
            lambda i: raise_back(0, i),
            lambda i: part_pass(0, i),
        ),
        {1: [lambda: reduce_relay(1, 2)], 4: [lambda: lower_grad(0)]},
    )
    part_drain(1)
    reduce_first(1, 0)
    raise_grad(0)
    pipeline(
        (lambda i: branch_back(0, i), lambda i: attend_back(0, i)),
        {1: [lambda: reduce_relay(1, 1)], 3: [lambda: reduce_first(1, 3)]},
    )
    part_drain(0)
    attend_back_end(0)
    reduce_cross(1)
    small_one(0)
    pipeline((lambda i: project_back(0, i), lambda i: part_pass(1, i)))
    project_grad(0)
    out_grad(0)
    reduce_relay(1, 0)
    small_two(1)
    pipeline((lambda i: next_back(0, i),), {1: [lambda: reduce_relay(1, 3)]})
    part_drain(1)
    scatter_out(1, S.back.at[1])
    reduce_first(0, 2)
    small_three(1)
    reduce_last(1, 1)
    reduce_last(1, 0)
    reduce_first(0, 1)
    reduce_relay(0, 2)
    reduce_last(1, 3)
    small_two(0)
    reduce_last_d(1)
    small_four(1)
    reduce_first(0, 0)
    reduce_relay(0, 1)
    small_three(0)
    reduce_first(0, 3)
    reduce_last(0, 2)
    reduce_relay(0, 0)
    reduce_last(0, 1)
    reduce_relay(0, 3)
    small_four(0)
    unpack_heads(1)
    unpack_raise(1)
    reduce_last(0, 0)
    reduce_last(0, 3)

    for kind in range(3):
        for r in range(3):
            stage_copy(kind, r).wait_send()
    scatter_in_drain(0, inp, first)
    scatter_in_drain(1, cot, S.ct)

    @pl.when(jnp.logical_not(perm_stays))
    def _():
        perm_copy.wait_send()

    spot = first.at[pl.ds(mine, half)]
    rcopy(spot, spot, S.ins_s.at[0], S.ins_r.at[0], sibling).wait_send()
    for cls in range(8):
        gather_drain(cls)
    scatter_out_wait(0, S.back.at[0], out)
    scatter_out_wait(1, S.back.at[1], gin)
    for layer in range(LAYERS):
        for kind in range(4):
            reduce_drain(layer, kind)
    unpack_raise(0)
    unpack_heads(0)
    o_out[...] = S.oo[...]


def hand_over(*refs):
    for n in range(11):
        refs[n + 11][...] = refs[n][...]


def grouped(nz, ny):
    def run(inputs, w_qkv, w_out, w_up, w_down, biases, value_bias, up_bias, gains, shifts, cotangent):
        block = inputs.shape[1]
        d_rows = w_out.shape[1]
        f_rows = w_down.shape[1]
        rows = 2 * nz * block
        half = rows // 2
        layout = scratch_layout(nz, ny, rows, half, d_rows, f_rows)
        vmem = pl.BlockSpec(memory_space=pltpu.VMEM)
        weights = (w_qkv, w_out, w_up, w_down, biases, value_bias, up_bias, gains, shifts)
        shapes = [jax.ShapeDtypeStruct(inputs.shape, BF)] * 2
        shapes += [jax.ShapeDtypeStruct(array.shape, F32) for array in weights]
        results = pl.pallas_call(
            functools.partial(group_kernel, layout, nz),
            out_shape=tuple(shapes),
            in_specs=[vmem] * 11,
            out_specs=[vmem] * 11,
            scratch_shapes=list(layout.values()),
            compiler_params=pltpu.CompilerParams(
                collective_id=0, has_side_effects=True, vmem_limit_bytes=KERNEL_VMEM
            ),
        )(inputs, *weights, cotangent)
        return pl.pallas_call(
            hand_over,
            out_shape=tuple(shapes),
            in_specs=[vmem] * 11,
            out_specs=[vmem] * 11,
        )(*results)

    return run


def part_count(row_count):
    count = 1
    while row_count % count != 0 or row_count // count > 2048:
        count = count + 1
    return count


def exact_gelu(values):
    return jax.nn.gelu(values, approximate=False)


def normalize(values, gain, shift):
    centred = values - jnp.mean(values, axis=1, keepdims=True)
    inv_std = lax.rsqrt(jnp.mean(centred * centred, axis=1, keepdims=True) + 1e-12)
    scaled = centred * inv_std
    return (scaled * gain + shift, scaled, inv_std)


def norm_back(grad, scaled, inv_std, gain):
    weighted = grad * gain
    return (
        weighted
        - jnp.mean(weighted, axis=1, keepdims=True)
        - scaled * jnp.mean(weighted * scaled, axis=1, keepdims=True)
    ) * inv_std


def split_heads(seq_array, count):
    seq_count, width, unused = seq_array.shape
    return seq_array.reshape(seq_count, count, width // count, HEADS, HEAD_DIM).transpose(
        1, 0, 2, 3, 4
    )


def merge_heads(head_array):
    seq_count, unused, row_count, unused_dim = head_array.shape
    return head_array.transpose(0, 2, 1, 3).reshape(seq_count * row_count, HEADS * HEAD_DIM)


def attend_forward(queries, keys, values):
    seq_count, row_count, unused = queries.shape
    factor = HEAD_DIM ** (-0.5)
    query_heads = queries.reshape(seq_count, row_count, HEADS, HEAD_DIM)
    start_state = (
        jnp.full((seq_count, HEADS, row_count), -1e30, jnp.float32),
        jnp.zeros((seq_count, HEADS, row_count), jnp.float32),
        jnp.zeros((seq_count, HEADS, row_count, HEAD_DIM), jnp.float32),
    )
    piece = (
        lax.all_gather(keys, "ctx", axis=1, tiled=True),
        lax.all_gather(values, "ctx", axis=1, tiled=True),
    )
    count = part_count(piece[0].shape[1])

    def attend_advance(inner, parts):
        peak, totals, accum = inner
        key_part, value_part = parts
        scores = (
            jnp.einsum("sthd,skhd->shtk", query_heads, key_part, preferred_element_type=jnp.float32)
            * factor
        )
        new_peak = jnp.maximum(peak, jnp.max(scores, axis=3))
        decay = jnp.exp(peak - new_peak)
        weights = jnp.exp(scores - new_peak[..., None])
        totals = totals * decay + jnp.sum(weights, axis=3)
        accum = accum * decay[..., None] + jnp.einsum(
            "shtk,skhd->shtd",
            weights.astype(jnp.bfloat16),
            value_part,
            preferred_element_type=jnp.float32,
        )
        return ((new_peak, totals, accum), None)

    result, _ = lax.scan(
        attend_advance, start_state, (split_heads(piece[0], count), split_heads(piece[1], count))
    )
    peak, totals, accum = result
    mixed = merge_heads(accum / totals[..., None])
    return (mixed, peak + jnp.log(totals))


def query_fold(queries, grad_mixed, logsum, row_delta, keys, values):
    seq_count, row_count, unused = queries.shape
    factor = HEAD_DIM ** (-0.5)
    query_heads = queries.reshape(seq_count, row_count, HEADS, HEAD_DIM)
    grad_heads = grad_mixed.reshape(seq_count, row_count, HEADS, HEAD_DIM)
    start_state = jnp.zeros((seq_count, HEADS, row_count, HEAD_DIM), jnp.float32)
    piece = (
        lax.all_gather(keys, "ctx", axis=1, tiled=True),
        lax.all_gather(values, "ctx", axis=1, tiled=True),
    )
    count = part_count(piece[0].shape[1])

    def query_advance(totals, parts):
        key_part, value_part = parts
        scores = (
            jnp.einsum("sthd,skhd->shtk", query_heads, key_part, preferred_element_type=jnp.float32)
            * factor
        )
        weights = jnp.exp(scores - logsum[..., None])
        grad_weights = jnp.einsum(
            "sthd,skhd->shtk", grad_heads, value_part, preferred_element_type=jnp.float32
        )
        grad_scores = (weights * (grad_weights - row_delta[..., None])).astype(jnp.bfloat16)
        return (
            totals
            + jnp.einsum(
                "shtk,skhd->shtd", grad_scores, key_part, preferred_element_type=jnp.float32
            )
            * factor,
            None,
        )

    result, _ = lax.scan(
        query_advance, start_state, (split_heads(piece[0], count), split_heads(piece[1], count))
    )
    return result


def key_fold(queries, grad_mixed, keys, values, all_logsum, all_delta):
    seq_count, row_count, unused = keys.shape
    factor = HEAD_DIM ** (-0.5)
    key_heads = keys.reshape(seq_count, row_count, HEADS, HEAD_DIM)
    value_heads = values.reshape(seq_count, row_count, HEADS, HEAD_DIM)
    start_state = (
        jnp.zeros((seq_count, HEADS, row_count, HEAD_DIM), jnp.float32),
        jnp.zeros((seq_count, HEADS, row_count, HEAD_DIM), jnp.float32),
    )
    piece = (
        lax.all_gather(queries, "ctx", axis=1, tiled=True),
        lax.all_gather(grad_mixed, "ctx", axis=1, tiled=True),
    )
    width = piece[0].shape[1]
    count = part_count(width)
    block = width // count
    log_parts = all_logsum.reshape(seq_count, HEADS, count, block).transpose(2, 0, 1, 3)
    delta_parts = all_delta.reshape(seq_count, HEADS, count, block).transpose(2, 0, 1, 3)

    def key_advance(inner, parts):
        grad_keys, grad_values = inner
        query_part, grad_part, log_part, delta_part = parts
        scores = (
            jnp.einsum("sqhd,skhd->shqk", query_part, key_heads, preferred_element_type=jnp.float32)
            * factor
        )
        weights = jnp.exp(scores - log_part[..., None])
        grad_values = grad_values + jnp.einsum(
            "shqk,sqhd->shkd",
            weights.astype(jnp.bfloat16),
            grad_part,
            preferred_element_type=jnp.float32,
        )
        grad_weights = jnp.einsum(
            "sqhd,skhd->shqk", grad_part, value_heads, preferred_element_type=jnp.float32
        )
        grad_scores = (weights * (grad_weights - delta_part[..., None])).astype(jnp.bfloat16)
        grad_keys = (
            grad_keys
            + jnp.einsum(
                "shqk,sqhd->shkd", grad_scores, query_part, preferred_element_type=jnp.float32
            )
            * factor
        )
        return ((grad_keys, grad_values), None)

    result, _ = lax.scan(
        key_advance,
        start_state,
        (split_heads(piece[0], count), split_heads(piece[1], count), log_parts, delta_parts),
    )
    return result


def forward_layer(stream, full, seq_count):
    w_attn, w_mix, w_raise, w_lower, bias_rows, bias_value, bias_raise, gain_rows, shift_rows = full
    total_rows = stream.shape[0]
    rounded = stream.astype(jnp.bfloat16)
    projected = jnp.einsum("td,cde->cte", rounded, w_attn, preferred_element_type=jnp.float32)
    queries = (projected[0] + bias_rows[0].astype(jnp.float32)).astype(jnp.bfloat16)
    keys = projected[1].astype(jnp.bfloat16)
    values = (projected[2] + bias_value.astype(jnp.float32)).astype(jnp.bfloat16)
    seq_shape = (seq_count, total_rows // seq_count, D)
    mixed, logsum = attend_forward(
        queries.reshape(seq_shape), keys.reshape(seq_shape), values.reshape(seq_shape)
    )
    mixed_low = mixed.astype(jnp.bfloat16)
    branch = jnp.dot(mixed_low, w_mix, preferred_element_type=jnp.float32) + bias_rows[1].astype(
        jnp.float32
    )
    normed, scaled_one, inv_one = normalize(
        stream + branch, gain_rows[0].astype(jnp.float32), shift_rows[0].astype(jnp.float32)
    )
    normed_low = normed.astype(jnp.bfloat16)
    upward = jnp.dot(normed_low, w_raise, preferred_element_type=jnp.float32) + bias_raise.astype(
        jnp.float32
    )
    active = exact_gelu(upward).astype(jnp.bfloat16)
    lowered = jnp.dot(active, w_lower, preferred_element_type=jnp.float32) + bias_rows[2].astype(
        jnp.float32
    )
    result, scaled_two, inv_two = normalize(
        normed + lowered, gain_rows[1].astype(jnp.float32), shift_rows[1].astype(jnp.float32)
    )
    states = (
        rounded,
        queries,
        keys,
        values,
        mixed,
        mixed_low,
        logsum,
        scaled_one,
        inv_one,
        normed_low,
        upward,
        active,
        scaled_two,
        inv_two,
    )
    return (result, states)


def backward_layer(grad, full, states, seq_count):
    w_attn, w_mix, w_raise, w_lower, bias_rows, bias_value, bias_raise, gain_rows, shift_rows = full
    (
        rounded,
        queries,
        keys,
        values,
        mixed,
        mixed_low,
        logsum,
        scaled_one,
        inv_one,
        normed_low,
        upward,
        active,
        scaled_two,
        inv_two,
    ) = states
    total_rows = grad.shape[0]
    row_count = total_rows // seq_count
    seq_shape = (seq_count, row_count, D)
    grad_gain_two = jnp.sum(grad * scaled_two, axis=0)
    grad_shift_two = jnp.sum(grad, axis=0)
    grad_resid = norm_back(grad, scaled_two, inv_two, gain_rows[1].astype(jnp.float32))
    grad_lowered = grad_resid.astype(jnp.bfloat16)
    grad_w_lower = jnp.einsum("tf,td->fd", active, grad_lowered, preferred_element_type=jnp.float32)
    grad_active = jnp.einsum("td,fd->tf", grad_lowered, w_lower, preferred_element_type=jnp.float32)
    unused, gelu_back = jax.vjp(exact_gelu, upward)
    grad_upward = gelu_back(grad_active)[0].astype(jnp.bfloat16)
    grad_w_raise = jnp.einsum(
        "td,tf->df", normed_low, grad_upward, preferred_element_type=jnp.float32
    )
    grad_normed = (
        jnp.einsum("tf,df->td", grad_upward, w_raise, preferred_element_type=jnp.float32)
        + grad_resid
    )
    grad_gain_one = jnp.sum(grad_normed * scaled_one, axis=0)
    grad_shift_one = jnp.sum(grad_normed, axis=0)
    grad_inner = norm_back(grad_normed, scaled_one, inv_one, gain_rows[0].astype(jnp.float32))
    grad_branch = grad_inner.astype(jnp.bfloat16)
    grad_w_mix = jnp.einsum("td,te->de", mixed_low, grad_branch, preferred_element_type=jnp.float32)
    grad_mixed = jnp.einsum(
        "te,de->td", grad_branch, w_mix, preferred_element_type=jnp.float32
    ).astype(jnp.bfloat16)
    row_delta = jnp.sum(
        (grad_mixed.astype(jnp.float32) * mixed).reshape(seq_count, row_count, HEADS, HEAD_DIM),
        axis=3,
    ).transpose(0, 2, 1)
    seq_queries = queries.reshape(seq_shape)
    seq_keys = keys.reshape(seq_shape)
    seq_values = values.reshape(seq_shape)
    seq_grad_mixed = grad_mixed.reshape(seq_shape)
    grad_queries = query_fold(seq_queries, seq_grad_mixed, logsum, row_delta, seq_keys, seq_values)
    grad_queries = merge_heads(grad_queries).astype(jnp.bfloat16)
    all_logsum, all_delta = (
        lax.all_gather(logsum, "ctx", axis=2, tiled=True),
        lax.all_gather(row_delta, "ctx", axis=2, tiled=True),
    )
    grad_keys, grad_values = key_fold(
        seq_queries, seq_grad_mixed, seq_keys, seq_values, all_logsum, all_delta
    )
    grad_keys = merge_heads(grad_keys).astype(jnp.bfloat16)
    grad_values = merge_heads(grad_values).astype(jnp.bfloat16)
    grad_project = jnp.stack([grad_queries, grad_keys, grad_values])
    grad_w_attn = jnp.einsum(
        "td,cte->dce", rounded, grad_project, preferred_element_type=jnp.float32
    )
    grad_stream = (
        jnp.einsum("cte,cde->td", grad_project, w_attn, preferred_element_type=jnp.float32)
        + grad_inner
    )
    grad_bias_rows = jnp.stack(
        [
            jnp.sum(grad_queries.astype(jnp.float32), axis=0),
            jnp.sum(grad_branch.astype(jnp.float32), axis=0),
            jnp.sum(grad_lowered.astype(jnp.float32), axis=0),
        ],
        axis=1,
    )
    grad_bias_value = jnp.sum(grad_values.astype(jnp.float32), axis=0)
    grad_bias_raise = jnp.sum(grad_upward.astype(jnp.float32), axis=0)
    local_sums = (
        grad_w_attn,
        grad_w_mix,
        grad_w_raise,
        grad_w_lower,
        grad_bias_rows,
        grad_bias_value,
        grad_bias_raise,
        jnp.stack([grad_gain_one, grad_gain_two], axis=1),
        jnp.stack([grad_shift_one, grad_shift_two], axis=1),
    )
    return (grad_stream, local_sums)


def body(inputs, w_qkv, w_out, w_up, w_down, biases, value_bias, up_bias, gains, shifts, cotangent):
    stacked = (w_qkv, w_out, w_up, w_down, biases, value_bias, up_bias, gains, shifts)
    seq_count = inputs.shape[0]
    stream = inputs.reshape(-1, D).astype(jnp.float32)
    kept_states = []
    for layer in range(LAYERS):
        shards = tuple((array[layer] for array in stacked))
        full = (
            lax.all_gather(shards[0], ("ctx", "fsdp"), axis=1, tiled=True),
            lax.all_gather(shards[1], ("ctx", "fsdp"), axis=0, tiled=True),
            lax.all_gather(shards[2], ("ctx", "fsdp"), axis=0, tiled=True),
            lax.all_gather(shards[3], ("ctx", "fsdp"), axis=0, tiled=True),
            lax.all_gather(shards[4], ("ctx", "fsdp"), axis=1, tiled=True),
            lax.all_gather(shards[5], ("ctx", "fsdp"), axis=0, tiled=True),
            lax.all_gather(shards[6], ("ctx", "fsdp"), axis=0, tiled=True),
            lax.all_gather(shards[7], ("ctx", "fsdp"), axis=1, tiled=True),
            lax.all_gather(shards[8], ("ctx", "fsdp"), axis=1, tiled=True),
        )
        stream, states = forward_layer(stream, full, seq_count)
        kept_states.append(states)
    output = stream.astype(jnp.bfloat16).reshape(inputs.shape)
    grad = cotangent.reshape(-1, D).astype(jnp.float32)
    layer_grads = [None] * LAYERS
    for layer in reversed(range(LAYERS)):
        shards = tuple((array[layer] for array in stacked))
        full = (
            lax.all_gather(shards[0], ("ctx", "fsdp"), axis=1, tiled=True),
            lax.all_gather(shards[1], ("ctx", "fsdp"), axis=0, tiled=True),
            lax.all_gather(shards[2], ("ctx", "fsdp"), axis=0, tiled=True),
            lax.all_gather(shards[3], ("ctx", "fsdp"), axis=0, tiled=True),
            lax.all_gather(shards[4], ("ctx", "fsdp"), axis=1, tiled=True),
            lax.all_gather(shards[5], ("ctx", "fsdp"), axis=0, tiled=True),
            lax.all_gather(shards[6], ("ctx", "fsdp"), axis=0, tiled=True),
            lax.all_gather(shards[7], ("ctx", "fsdp"), axis=1, tiled=True),
            lax.all_gather(shards[8], ("ctx", "fsdp"), axis=1, tiled=True),
        )
        grad, local_sums = backward_layer(grad, full, kept_states[layer], seq_count)
        partial_sums = (
            lax.psum_scatter(local_sums[0], "ctx", scatter_dimension=0, tiled=True),
            lax.psum_scatter(local_sums[1], "ctx", scatter_dimension=0, tiled=True),
            lax.psum_scatter(local_sums[2], "ctx", scatter_dimension=0, tiled=True),
            lax.psum_scatter(local_sums[3], "ctx", scatter_dimension=0, tiled=True),
            lax.psum_scatter(local_sums[4], "ctx", scatter_dimension=0, tiled=True),
            lax.psum_scatter(local_sums[5], "ctx", scatter_dimension=0, tiled=True),
            lax.psum_scatter(local_sums[6], "ctx", scatter_dimension=0, tiled=True),
            lax.psum_scatter(local_sums[7], "ctx", scatter_dimension=0, tiled=True),
            lax.psum_scatter(local_sums[8], "ctx", scatter_dimension=0, tiled=True),
        )
        reduced = (
            lax.psum_scatter(
                partial_sums[0].astype(jnp.bfloat16), "fsdp", scatter_dimension=0, tiled=True
            ).astype(jnp.float32),
            lax.psum_scatter(
                partial_sums[1].astype(jnp.bfloat16), "fsdp", scatter_dimension=0, tiled=True
            ).astype(jnp.float32),
            lax.psum_scatter(
                partial_sums[2].astype(jnp.bfloat16), "fsdp", scatter_dimension=0, tiled=True
            ).astype(jnp.float32),
            lax.psum_scatter(
                partial_sums[3].astype(jnp.bfloat16), "fsdp", scatter_dimension=0, tiled=True
            ).astype(jnp.float32),
            lax.psum_scatter(
                partial_sums[4].astype(jnp.bfloat16), "fsdp", scatter_dimension=0, tiled=True
            ).astype(jnp.float32),
            lax.psum_scatter(
                partial_sums[5].astype(jnp.bfloat16), "fsdp", scatter_dimension=0, tiled=True
            ).astype(jnp.float32),
            lax.psum_scatter(
                partial_sums[6].astype(jnp.bfloat16), "fsdp", scatter_dimension=0, tiled=True
            ).astype(jnp.float32),
            lax.psum_scatter(
                partial_sums[7].astype(jnp.bfloat16), "fsdp", scatter_dimension=0, tiled=True
            ).astype(jnp.float32),
            lax.psum_scatter(
                partial_sums[8].astype(jnp.bfloat16), "fsdp", scatter_dimension=0, tiled=True
            ).astype(jnp.float32),
        )
        layer_grads[layer] = (
            reduced[0].transpose(1, 0, 2),
            reduced[1],
            reduced[2],
            reduced[3],
            reduced[4].T,
            reduced[5],
            reduced[6],
            reduced[7].T,
            reduced[8].T,
        )
    grad_inputs = grad.astype(jnp.bfloat16).reshape(inputs.shape)
    return (
        output,
        grad_inputs,
        jnp.stack([member[0] for member in layer_grads]),
        jnp.stack([member[1] for member in layer_grads]),
        jnp.stack([member[2] for member in layer_grads]),
        jnp.stack([member[3] for member in layer_grads]),
        jnp.stack([member[4] for member in layer_grads]),
        jnp.stack([member[5] for member in layer_grads]),
        jnp.stack([member[6] for member in layer_grads]),
        jnp.stack([member[7] for member in layer_grads]),
        jnp.stack([member[8] for member in layer_grads]),
    )


def one_group_per_sequence(mesh, seqs):
    return mesh.shape["fsdp"] == 4 and mesh.shape["ctx"] == seqs


def solution(mesh):
    def run(*arrays):
        seqs = arrays[0].shape[0]
        chosen = grouped(mesh.shape["ctx"] // 2, 2) if one_group_per_sequence(mesh, seqs) else body
        return on_devices(mesh, chosen)(*arrays)

    return run


def on_devices(mesh, chosen):
    return jax.shard_map(
        chosen,
        mesh=mesh,
        in_specs=(
            P("fsdp", "ctx", None),
            P(None, None, ("ctx", "fsdp"), None),
            P(None, ("ctx", "fsdp"), None),
            P(None, ("ctx", "fsdp"), None),
            P(None, ("ctx", "fsdp"), None),
            P(None, None, ("ctx", "fsdp")),
            P(None, ("ctx", "fsdp")),
            P(None, ("ctx", "fsdp")),
            P(None, None, ("ctx", "fsdp")),
            P(None, None, ("ctx", "fsdp")),
            P("fsdp", "ctx", None),
        ),
        out_specs=(
            P("fsdp", "ctx", None),
            P("fsdp", "ctx", None),
            P(None, None, ("ctx", "fsdp"), None),
            P(None, ("ctx", "fsdp"), None),
            P(None, ("ctx", "fsdp"), None),
            P(None, ("ctx", "fsdp"), None),
            P(None, None, ("ctx", "fsdp")),
            P(None, ("ctx", "fsdp")),
            P(None, ("ctx", "fsdp")),
            P(None, None, ("ctx", "fsdp")),
            P(None, None, ("ctx", "fsdp")),
        ),
        check_vma=False,
    )
```

```python
import functools
import types

import jax
import jax.numpy as jnp
from jax import lax
from jax.experimental import pallas as pl
from jax.experimental.pallas import tpu as pltpu
from jax.sharding import PartitionSpec as P

D = 768
HEADS = 12
HEAD_DIM = 64
LAYERS = 2
KERNEL_VMEM = 63 * 2**20


BF = jnp.bfloat16
F32 = jnp.float32
MESH = pl.DeviceIdType.MESH
MEMBERS = 4
LOCAL_HEADS = HEADS // MEMBERS
PACK = 640
SLOT = 64
PIECE = 64


def dot_nn(left, right):
    return lax.dot_general(left, right, (((1,), (0,)), ((), ())), preferred_element_type=F32)


def dot_nt(left, right):
    return lax.dot_general(left, right, (((1,), (1,)), ((), ())), preferred_element_type=F32)


def dot_tn(left, right):
    return lax.dot_general(left, right, (((0,), (0,)), ((), ())), preferred_element_type=F32)


def dot_exact(left, right):
    return lax.dot_general(
        left,
        right,
        (((1,), (0,)), ((), ())),
        precision=lax.Precision.HIGHEST,
        preferred_element_type=F32,
    )


def packed_lanes(shape, axis):
    lane = lax.broadcasted_iota(jnp.int32, shape, axis)
    slot = lane >> 6
    head = jnp.where(slot >= 6, 2, slot & 1)
    is_query = (slot < 2) | (slot == 6)
    is_value = (slot == 4) | (slot == 5) | (slot == 8)
    return (head * HEAD_DIM + (lane & 63), is_query, is_value)


def scratch_layout(nz, ny, rows, half, d_rows, f_rows):
    dma = pltpu.SemaphoreType.DMA
    two = 2 * d_rows
    ff = nz * ny * f_rows
    vm = pltpu.VMEM
    return dict(
        wq=vm((LAYERS, nz, 2, ny, two, PACK), BF),
        wu=vm((LAYERS, nz, 2, ny, two, ff), BF),
        wd=vm((LAYERS, nz, ny, f_rows, D), BF),
        wog=vm((nz, ny, two, D), BF),
        wo=vm((LAYERS, 256, D), BF),
        smg=vm((nz, ny, MEMBERS, 32, 128), BF),
        qi=vm((MEMBERS, two, PACK), BF),
        ui=vm((MEMBERS, two, ff), BF),
        oi=vm((two, D), BF),
        sf=vm((32, 128), F32),
        si=vm((32, 128), BF),
        qs=vm((MEMBERS, two, PACK), BF),
        us=vm((MEMBERS, two, ff), BF),
        pb=vm((16, D), F32),
        ub=vm((16, ff), F32),
        bq=vm((LAYERS, 8, PACK), F32),
        xf=vm((LAYERS, rows, D), BF),
        qkv=vm((LAYERS, rows, PACK), BF),
        prob=vm((LAYERS, LOCAL_HEADS, rows, rows), BF),
        mix=vm((LAYERS, rows, 256), F32),
        mixl=vm((LAYERS, rows, 256), BF),
        xh1=vm((LAYERS, half, D), F32),
        iv1=vm((LAYERS, half, 128), F32),
        nl=vm((LAYERS, rows, D), BF),
        gp=vm((LAYERS, rows, ff), F32),
        act=vm((LAYERS, rows, ff), BF),
        xh2=vm((LAYERS, half, D), F32),
        iv2=vm((LAYERS, half, 128), F32),
        stream=vm((half, D), F32),
        normed=vm((half, D), F32),
        ct=vm((half, D), BF),
        ownp=vm((half, D), F32),
        sibs=vm((2, half, D), BF),
        sibr=vm((2, half, D), BF),
        xs=vm((2, half, D), BF),
        xr=vm((2, half, D), BF),
        dl=vm((rows, D), BF),
        db=vm((rows, D), BF),
        du=vm((rows, ff), BF),
        dq=vm((rows, PACK), BF),
        dm=vm((rows, 256), BF),
        ds=vm((LOCAL_HEADS, rows, rows), BF),
        back=vm((2, half, D), BF),
        land=vm((2, 2, rows // (2 * nz), D), BF),
        gq=vm((LAYERS, nz, 2, ny, two, PACK), BF),
        gu=vm((LAYERS, nz, 2, ny, two, ff), BF),
        gd=vm((LAYERS, nz, ny, f_rows, D), BF),
        go=vm((LAYERS, nz, ny, 32, D), BF),
        ryq=vm((LAYERS, nz, 2, two, PACK), BF),
        ryu=vm((LAYERS, nz, 2, two, ff), BF),
        ryd=vm((nz, f_rows, D), BF),
        ryl=vm((f_rows, D), BF),
        syl=vm((f_rows, D), BF),
        ryo=vm((LAYERS, nz, 32, D), BF),
        rzq=vm((LAYERS, 4, 2, two, PACK), BF),
        rzu=vm((LAYERS, 4, 2, two, ff), BF),
        rzd=vm((4, f_rows, D), BF),
        rzl=vm((4, 2, f_rows, D), BF),
        rzo=vm((LAYERS, 4, 32, D), BF),
        fq=vm((LAYERS, 2, two, PACK), F32),
        fu=vm((LAYERS, 2, two, ff), F32),
        fo=vm((LAYERS, d_rows, D), F32),
        oq=vm((LAYERS, MEMBERS, d_rows, PACK), F32),
        ou=vm((LAYERS, MEMBERS, d_rows, ff), F32),
        oo=vm((LAYERS, d_rows, D), F32),
        sg=vm((LAYERS, 8, D), F32),
        sgy=vm((LAYERS, 8, D), F32),
        sgt=vm((LAYERS, 8, D), F32),
        sgz=vm((LAYERS, nz, 8, D), F32),
        sga=vm((LAYERS, MEMBERS, 8, D), F32),
        stage_s=dma((3, 3)),
        stage_r=dma((3, 3)),
        perm=dma((2,)),
        in_s=dma((4, 2)),
        in_r=dma((4, 2)),
        inx_s=dma((2, 2)),
        inx_r=dma((2, 2)),
        ins_s=dma((1,)),
        ins_r=dma((1,)),
        gz_s=dma((10, nz)),
        gz_r=dma((10, nz)),
        gy_s=dma((10, nz)),
        gy_r=dma((10, nz)),
        sib_s=dma((2, half // PIECE)),
        sib_r=dma((2, half // PIECE)),
        x_s=dma((2, half // PIECE)),
        x_r=dma((2, half // PIECE)),
        ag_s=dma((2, half // PIECE)),
        ag_r=dma((2, half // PIECE)),
        ry_s=dma((8,)),
        ry_r=dma((8,)),
        rz_s=dma((8, nz)),
        rz_r=dma((8, nz)),
        fin_s=dma((LAYERS, 2, 3)),
        fin_r=dma((LAYERS, 2, 3)),
        fino=dma((LAYERS, 2)),
        sgy_s=dma((LAYERS,)),
        sgy_r=dma((LAYERS,)),
        sgz_s=dma((LAYERS, nz)),
        sgz_r=dma((LAYERS, nz)),
        sga_s=dma((LAYERS, 3)),
        sga_r=dma((LAYERS, 3)),
    )


def group_kernel(layout, nz, *refs):
    inp, w_qkv, w_out, w_up, d_in, biases, value_bias, up_bias, gains, shifts, cot = refs[:11]
    out, gin, g_qkv, o_out, g_up, d_out, g_biases, g_value, g_raise, g_gains, g_shifts = refs[11:22]
    S = types.SimpleNamespace(**dict(zip(layout.keys(), refs[22:])))
    q_in, u_in, o_in, s_in = S.qi, S.ui, S.oi, S.si
    rows = S.dl.shape[0]
    half = rows // 2
    block = inp.shape[1]
    d_rows = w_out.shape[1]
    f_rows = d_in.shape[1]
    two = 2 * d_rows
    ff = S.du.shape[1]
    pieces = half // PIECE
    place = lax.axis_index("ctx")
    lane_f = lax.axis_index("fsdp")
    z, x = lax.div(place, 2), lax.rem(place, 2)
    y, c = lax.div(lane_f, 2), lax.rem(lane_f, 2)
    m = 2 * x + c
    d = 4 * place + lane_f
    devices = 8 * nz

    def dev(z_at, x_at, y_at, c_at):
        return (2 * z_at + x_at, 2 * y_at + c_at)

    def rcopy(source, target, send, recv, to):
        return pltpu.make_async_remote_copy(
            src_ref=source,
            dst_ref=target,
            send_sem=send,
            recv_sem=recv,
            device_id=to,
            device_id_type=MESH,
        )

    barrier = pltpu.get_barrier_semaphore()

    def hail(step, carry):
        other = lax.rem(d + step, devices)
        pl.semaphore_signal(
            barrier, inc=1, device_id=(lax.div(other, 4), lax.rem(other, 4)), device_id_type=MESH
        )
        return carry

    lax.fori_loop(1, devices, hail, 0)

    lane_low = lax.broadcasted_iota(jnp.int32, (1, 128), 1) < HEAD_DIM

    def turn(value):
        return pltpu.roll(value, HEAD_DIM, 1)

    def pack_heads(layer, pair):
        tiles = []
        for kind in range(3):
            base = 2 * pair * LOCAL_HEADS * HEAD_DIM
            whole = w_qkv[layer, kind, :, base : base + 384].astype(F32)
            tiles.append([whole[:, 0:128], whole[:, 128:256], whole[:, 256:384]])
        (q0, q1, q2), (k0, k1, k2), (v0, v1, v2) = tiles
        even = (q0, k0, v0, jnp.where(lane_low, q1, turn(k1)), jnp.where(lane_low, v1, 0.0))
        odd = (
            jnp.where(lane_low, turn(q1), turn(q2)),
            jnp.where(lane_low, turn(k1), turn(k2)),
            jnp.where(lane_low, turn(v1), turn(v2)),
            jnp.where(lane_low, turn(q2), k2),
            jnp.where(lane_low, turn(v2), 0.0),
        )
        return [jnp.concatenate(part, axis=1) for part in (even, odd)]

    for pair in range(2):
        packed = [pack_heads(layer, pair) for layer in range(LAYERS)]
        for odd in range(2):
            both = jnp.concatenate([part[odd] for part in packed], axis=0)
            q_in[2 * pair + odd] = both.astype(BF)

    def owner_block(z_at, x_at, y_at, c_at):
        at = (8 * z_at + 4 * x_at + 2 * y_at + c_at) * f_rows
        return slice(at, at + f_rows)

    grid_places = [(z_at, y_at) for z_at in range(nz) for y_at in range(2)]

    def pack_raise():
        wide = [w_up[layer].astype(F32) for layer in range(LAYERS)]
        for x_at in range(2):
            for c_at in range(2):
                both = [
                    jnp.concatenate(
                        [part[:, owner_block(z_at, x_at, y_at, c_at)] for z_at, y_at in grid_places], axis=1
                    )
                    for part in wide
                ]
                u_in[2 * x_at + c_at] = jnp.concatenate(both, axis=0).astype(BF)

    def pack_small():
        S.sf[...] = jnp.zeros_like(S.sf)
        for layer in range(LAYERS):
            base = 8 * layer
            for kind in range(3):
                S.sf[base + kind : base + kind + 1, 0:d_rows] = biases[kind, layer : layer + 1].astype(F32)
            S.sf[base + 3 : base + 4, 0:d_rows] = value_bias[layer : layer + 1].astype(F32)
            S.sf[base + 4 : base + 6, 0:d_rows] = gains[layer].astype(F32)
            S.sf[base + 6 : base + 8, 0:d_rows] = shifts[layer].astype(F32)
            S.sf[16 + layer : 17 + layer, 0:f_rows] = up_bias[layer : layer + 1].astype(F32)
        s_in[...] = S.sf[...].astype(BF)

    pack_small()
    pack_raise()
    o_in[...] = jnp.concatenate([w_out[layer].astype(F32) for layer in range(LAYERS)], axis=0).astype(BF)
    pl.semaphore_wait(barrier, devices - 1)

    relation = ((x, 1 - c), (1 - x, c), (1 - x, 1 - c))
    sibling = dev(z, x, y, 1 - c)
    peer = dev(z, 1 - x, y, c)
    across = dev(z, x, 1 - y, c)

    def stage_copy(kind, r):
        x_r, c_r = relation[r]
        m_r = 2 * x_r + c_r
        source = (s_in, q_in.at[m_r], u_in.at[m_r])[kind]
        target = (S.smg.at[z, y, m], S.qs.at[m], S.us.at[m])[kind]
        return rcopy(source, target, S.stage_s.at[kind, r], S.stage_r.at[kind, r], dev(z, x_r, y, c_r))

    def stage_wait(kind, r):
        x_r, c_r = relation[r]
        m_r = 2 * x_r + c_r
        target = (S.smg.at[z, y, m_r], S.qs.at[m_r], S.us.at[m_r])[kind]
        rcopy(
            target, target, S.stage_s.at[kind, r], S.stage_r.at[kind, r], dev(z, x_r, y, c_r)
        ).wait_recv()

    for kind in (1, 0):
        for r in (1, 2, 0):
            stage_copy(kind, r).start()

    def own_block(j):
        return (2 * c + j == z) & (lax.div(z, 2) == c)

    def scatter_in(which, source, target, position):
        for j in range(2):
            copy = rcopy(
                source.at[j],
                target.at[pl.ds(position, block)],
                S.in_s.at[which, j],
                S.in_r.at[which, lax.rem(z, 2)],
                dev(2 * c + j, x, y, lax.div(z, 2)),
            )

            @pl.when(own_block(j))
            def _():
                target[pl.ds(position, block), :] = source[j]

            @pl.when(jnp.logical_not(own_block(j)))
            def _():
                copy.start()

    def scatter_in_wait(which, source, target, base):
        for k in range(2):

            @pl.when(2 * c + k != z)
            def _():
                spot = target.at[pl.ds(base + 2 * block * k, block)]
                rcopy(
                    spot, spot, S.in_s.at[which, 0], S.in_r.at[which, k], peer
                ).wait_recv()

    def scatter_in_drain(which, source, target):
        for j in range(2):

            @pl.when(jnp.logical_not(own_block(j)))
            def _():
                rcopy(
                    source.at[j], source.at[j], S.in_s.at[which, j], S.in_r.at[which, 0], peer
                ).wait_send()

    first = S.xf.at[0]
    scatter_in(0, inp, first, block * place)

    perm_to = dev(2 * x + y, lax.div(z, 2), c, lax.rem(z, 2))
    perm_stays = (2 * x + y == z) & (lax.div(z, 2) == x) & (c == y) & (lax.rem(z, 2) == c)
    perm_copy = rcopy(o_in, S.wog.at[2 * x + y, c], S.perm.at[0], S.perm.at[1], perm_to)

    @pl.when(perm_stays)
    def _():
        S.wog[z, y] = o_in[...]

    def start_perm():
        @pl.when(jnp.logical_not(perm_stays))
        def _():
            perm_copy.start()

    for r in (1, 2, 0):
        stage_copy(2, r).start()
    S.smg[z, y, m] = s_in[...]
    S.qs[m] = q_in[m]
    S.us[m] = u_in[m]
    for layer in range(LAYERS):
        S.wd[layer, z, y] = d_in[layer]

    def join(staged, target):
        for xx in range(2):
            first_part = staged[2 * xx].astype(F32)
            second_part = staged[2 * xx + 1].astype(F32)
            for layer in range(LAYERS):
                cut = slice(layer * d_rows, (layer + 1) * d_rows)
                target[layer, z, xx, y] = jnp.concatenate(
                    [first_part[cut], second_part[cut]], axis=0
                ).astype(BF)

    side = lax.div(z, 2)
    inner = (z == 1) | (z == 2)
    outer = jnp.logical_not(inner)
    near_in, near_out = 1 + side, 3 * side
    far_in, far_out = 2 - side, 3 * (1 - side)
    buddy = near_in + near_out - z

    def at_z(z_at):
        return dev(z_at, x, y, c)

    half_rows = f_rows // 2
    upper, lower = pl.ds(0, half_rows), pl.ds(half_rows, half_rows)

    def slab(cls, z_at, y_at):
        return (
            lambda: S.smg.at[z_at, y_at],
            lambda: S.wq.at[0, z_at, :, y_at],
            lambda: S.wog.at[z_at, y_at],
            lambda: S.wu.at[0, z_at, :, y_at],
            lambda: S.wd.at[0, z_at, y_at],
            lambda: S.wq.at[1, z_at, :, y_at],
            lambda: S.wu.at[1, z_at, :, y_at],
            lambda: S.wd.at[1, z_at, y_at, upper],
            lambda: S.wd.at[1, z_at, y_at, lower],
        )[cls]()

    def y_first(cls):
        return cls >= 8

    def z_copy(cls, n, z_at, to):
        spot = S.wd.at[1, z_at, :, lower] if y_first(cls) else slab(cls, z_at, y)
        return rcopy(spot, spot, S.gz_s.at[cls, n], S.gz_r.at[cls, z_at], at_z(to))

    def y_copy(cls, z_at):
        spot = slab(cls, z_at, y)
        return rcopy(spot, spot, S.gy_s.at[cls, z_at], S.gy_r.at[cls, z_at], across)

    def y_wait(cls, t):
        spot = slab(cls, t, 1 - y)
        rcopy(spot, spot, S.gy_s.at[cls, t], S.gy_r.at[cls, t], across).wait_recv()

    def gather_start(cls):
        if not y_first(cls):
            z_copy(cls, 0, z, buddy).start()
            z_copy(cls, 1, z, far_in).start()
        y_copy(cls, z).start()

    def gather_cross(cls):
        y_wait(cls, z)
        for n, to in enumerate((buddy, far_in, far_out)):
            z_copy(cls, n, z, to).start()

    def gather_take(cls, z_at, relay):
        z_copy(cls, 0, z_at, buddy).wait_recv()
        if relay is not None:
            z_copy(cls, relay, z_at, near_out).start()
        y_copy(cls, z_at).start()

    def gather_relay(cls):
        gather_take(cls, buddy, None)

        @pl.when(inner)
        def _():
            gather_take(cls, far_in, 2)
            gather_take(cls, far_out, 3)

    def gather_end(cls):
        @pl.when(outer)
        def _():
            gather_take(cls, far_in, None)
            gather_take(cls, far_out, None)

    def gather_wait(cls):
        if y_first(cls):
            for t in (buddy, far_in, far_out):
                z_copy(cls, 0, t, buddy).wait_recv()
            return

        for t in (z, buddy, far_in, far_out):
            y_wait(cls, t)

    def gather_drain(cls):
        z_copy(cls, 0, z, buddy).wait_send()
        z_copy(cls, 1, z, far_in).wait_send()
        if y_first(cls):
            z_copy(cls, 2, z, far_out).wait_send()
            y_copy(cls, z).wait_send()
            return

        @pl.when(inner)
        def _():
            z_copy(cls, 2, far_in, near_out).wait_send()
            z_copy(cls, 3, far_out, near_out).wait_send()

        def one(t, carry):
            y_copy(cls, t).wait_send()
            return carry

        lax.fori_loop(0, nz, one, 0)

    for r in range(3):
        stage_wait(1, r)
    join(S.qs, S.wq)
    gather_start(1)
    for r in range(3):
        stage_wait(0, r)
    gather_start(0)

    def x_spots(target, base, mine):
        return [target.at[pl.ds(base + block * (2 * k + mine), block)] for k in range(2)]

    def swap_start(which, target, base):
        for k, spot in enumerate(x_spots(target, base, x)):
            rcopy(spot, spot, S.inx_s.at[which, k], S.inx_r.at[which, k], peer).start()

    def swap_wait(which, target, base):
        for k, spot in enumerate(x_spots(target, base, 1 - x)):
            rcopy(spot, spot, S.inx_s.at[which, k], S.inx_r.at[which, k], peer).wait_recv()
        for k, spot in enumerate(x_spots(target, base, x)):
            rcopy(spot, spot, S.inx_s.at[which, k], S.inx_r.at[which, k], peer).wait_send()

    mine = half * c
    theirs = half * (1 - c)
    scatter_in_wait(0, inp, first, mine + block * x)
    swap_start(0, first, mine)
    start_perm()
    for r in range(3):
        stage_wait(2, r)
    join(S.us, S.wu)
    gather_relay(1)
    gather_relay(0)
    swap_wait(0, first, mine)
    spot = first.at[pl.ds(mine, half)]
    rcopy(spot, spot, S.ins_s.at[0], S.ins_r.at[0], sibling).start()
    S.stream[...] = S.xf[0, pl.ds(mine, half), :].astype(F32)

    @pl.when(jnp.logical_not(perm_stays))
    def _():
        spot = S.wog.at[z, y]
        rcopy(spot, spot, S.perm.at[0], S.perm.at[1], peer).wait_recv()

    gather_start(2)
    gather_end(1)
    gather_end(0)
    gather_relay(2)
    gather_start(3)
    gather_wait(0)

    def small_params():
        row_shape = (devices * 16, D)
        lane = lax.broadcasted_iota(jnp.int32, (128, D), 0)
        col = lax.broadcasted_iota(jnp.int32, (128, D), 1)
        tile = jnp.where(lax.rem(col, d_rows) == lane, 1.0, 0.0).astype(BF)
        packs = S.smg[:, :, :, 0:16, :].reshape(devices * 16, 128)
        spread = dot_nn(packs, tile)
        owner_row = lax.broadcasted_iota(jnp.int32, row_shape, 0) >> 4
        zz = owner_row >> 3
        yy = (owner_row >> 2) & 1
        xx = (owner_row >> 1) & 1
        cc = owner_row & 1
        owner = zz * 8 + xx * 4 + yy * 2 + cc
        at = lax.div(lax.broadcasted_iota(jnp.int32, row_shape, 1), d_rows)
        spread = jnp.where(owner == at, spread, 0.0)
        S.pb[...] = jnp.sum(spread.reshape(devices, 16, D), axis=0)
        lane = lax.broadcasted_iota(jnp.int32, (128, ff), 0)
        col = lax.broadcasted_iota(jnp.int32, (128, ff), 1)
        tile = jnp.where(lax.rem(col, f_rows) == lane, 1.0, 0.0).astype(BF)
        packs = S.smg[:, :, m, 16:32, :].reshape(2 * nz * 16, 128)
        spread = dot_nn(packs, tile)
        row_shape = (2 * nz * 16, ff)
        owner = lax.broadcasted_iota(jnp.int32, row_shape, 0) >> 4
        at = lax.div(lax.broadcasted_iota(jnp.int32, row_shape, 1), f_rows)
        spread = jnp.where(owner == at, spread, 0.0)
        S.ub[...] = jnp.sum(spread.reshape(2 * nz, 16, ff), axis=0)
        source = lax.broadcasted_iota(jnp.int32, (D, PACK), 0)
        target, unused_q, unused_v = packed_lanes((D, PACK), 1)
        pick = jnp.where(source == target + m * (LOCAL_HEADS * HEAD_DIM), 1.0, 0.0).astype(BF)
        picked = dot_nn(S.pb[...].astype(BF), pick)
        unused, is_query, is_value = packed_lanes((1, PACK), 1)
        for layer in range(LAYERS):
            base = 8 * layer
            row = jnp.where(is_query, picked[base : base + 1], 0.0)
            row = jnp.where(is_value, picked[base + 3 : base + 4], row)
            S.bq[layer, 0:1, :] = row

    small_params()
    scatter_in(1, cot, S.ct, block * (2 * lax.rem(z, 2) + x))

    def param(layer, kind):
        return S.pb[8 * layer + kind : 8 * layer + kind + 1, :]

    def piece_rows(i):
        return pl.ds(i * PIECE if isinstance(i, int) else pl.multiple_of(i * PIECE, PIECE), PIECE)

    def own_rows(i):
        return pl.ds(pl.multiple_of(mine + i * PIECE, PIECE), PIECE)

    def other_rows(i):
        return pl.ds(pl.multiple_of(theirs + i * PIECE, PIECE), PIECE)

    every = slice(None)

    def load_both(ref, i, cols=every):
        return jnp.concatenate([ref[other_rows(i), cols], ref[own_rows(i), cols]], axis=0)

    def store_both(ref, i, value, cols=every):
        ref[other_rows(i), cols] = value[:PIECE]
        ref[own_rows(i), cols] = value[PIECE:]

    def spread_start(par, i, ref, value):
        ref[own_rows(i), :] = value
        spot = ref.at[own_rows(i)]
        rcopy(spot, spot, S.ag_s.at[par, i], S.ag_r.at[par, i], sibling).start()

    def spread_wait(par, i, ref):
        got = ref.at[other_rows(i)]
        sent = ref.at[own_rows(i)]
        rcopy(got, got, S.ag_s.at[par, i], S.ag_r.at[par, i], sibling).wait_recv()
        rcopy(sent, sent, S.ag_s.at[par, i], S.ag_r.at[par, i], sibling).wait_send()

    def sib_copy(par, i):
        at = piece_rows(i)
        return rcopy(
            S.sibs.at[par, at], S.sibr.at[par, at], S.sib_s.at[par, i], S.sib_r.at[par, i], sibling
        )

    def peer_copy(par, i):
        at = piece_rows(i)
        return rcopy(S.xs.at[par, at], S.xr.at[par, at], S.x_s.at[par, i], S.x_r.at[par, i], peer)

    def part_send(par, i, value):
        at = piece_rows(i)
        S.sibs[par, at, :] = value[:PIECE].astype(BF)
        sib_copy(par, i).start()
        S.ownp[at, :] = value[PIECE:]

    def part_pass(par, i):
        at = piece_rows(i)
        sib_copy(par, i).wait_recv()
        S.xs[par, at, :] = (S.ownp[at, :] + S.sibr[par, at, :].astype(F32)).astype(BF)
        peer_copy(par, i).start()

    def part_take(par, i):
        at = piece_rows(i)
        peer_copy(par, i).wait_recv()
        return S.xs[par, at, :].astype(F32) + S.xr[par, at, :].astype(F32)

    def part_drain(par):
        for i in range(pieces):
            sib_copy(par, i).wait_send()
            peer_copy(par, i).wait_send()

    def pipeline(stages, between=None):
        def one(step, carry):
            for lag, stage in enumerate(stages):
                if len(stages) == 1:
                    stage(step)
                    continue

                @pl.when((step >= lag) & (step < pieces + lag))
                def _():
                    stage(step - lag)

            for after, calls in (between or {}).items():

                @pl.when(step == after)
                def _():
                    for call in calls:
                        call()

            return carry

        lax.fori_loop(0, pieces + len(stages) - 1, one, 0)

    def norm_piece(total, at, layer, gain, shift, scaled_ref, inv_ref):
        centred = total - jnp.mean(total, axis=1, keepdims=True)
        inv = lax.rsqrt(jnp.mean(centred * centred, axis=1, keepdims=True) + 1e-12)
        scaled = centred * inv
        scaled_ref[layer, at, :] = scaled
        inv_ref[layer, at, :] = jnp.broadcast_to(inv, (PIECE, 128))
        return scaled * gain + shift

    def flat(value):
        return value.reshape(-1, value.shape[-1])

    def swap_lanes(value):
        return pltpu.roll(value.astype(F32), HEAD_DIM, 1).astype(BF)

    def mask_queries(queries, h):
        keep = jnp.logical_not(lane_low) if h == 1 else lane_low
        return jnp.where(keep, queries * jnp.asarray(HEAD_DIM**-0.5, BF), jnp.zeros((), BF))

    def query_cols(h):
        return slice(0, 128) if h < 2 else slice(384, 512)

    def head_keys(layer, h):
        if h < 2:
            return S.qkv[layer, :, 128:256]
        return swap_lanes(S.qkv[layer, :, 384:512])

    def head_values(layer, h):
        return S.qkv[layer, :, 256:384] if h < 2 else S.qkv[layer, :, 512:640]

    def project(layer, i):
        value = dot_nn(load_both(S.xf.at[layer], i), flat(S.wq[layer])) + S.bq[layer, 0:1, :]
        store_both(S.qkv.at[layer], i, value.astype(BF))

    def attend(layer, i):
        mixes = []
        for h in range(LOCAL_HEADS):
            queries = mask_queries(load_both(S.qkv.at[layer], i, query_cols(h)), h)
            scores = dot_nt(queries, head_keys(layer, h))
            weights = jnp.exp(scores - jnp.max(scores, axis=1, keepdims=True))
            weights = (weights * (1.0 / jnp.sum(weights, axis=1, keepdims=True))).astype(BF)
            store_both(S.prob.at[layer, h], i, weights)
            mixes.append(dot_nn(weights, head_values(layer, h)))
        mix = jnp.concatenate(
            [jnp.where(lane_low, mixes[0], mixes[1]), jnp.where(lane_low, mixes[2], 0.0)], axis=1
        )
        store_both(S.mix.at[layer], i, mix)
        store_both(S.mixl.at[layer], i, mix.astype(BF))
        part_send(0, i, dot_nn(mix.astype(BF), S.wo[layer]))

    def after_attention(layer, i):
        at = piece_rows(i)
        total = S.stream[at, :] + part_take(0, i) + param(layer, 1)
        normed = norm_piece(total, at, layer, param(layer, 4), param(layer, 6), S.xh1, S.iv1)
        S.normed[at, :] = normed
        spread_start(0, i, S.nl.at[layer], normed.astype(BF))

    def raise_part(layer, i):
        spread_wait(0, i, S.nl.at[layer])
        rounded = load_both(S.nl.at[layer], i)
        upward = dot_nn(rounded, flat(S.wu[layer])) + S.ub[layer : layer + 1, :]
        cdf = 0.5 * (1.0 + lax.erf(upward * (0.5**0.5)))
        density = jnp.exp(-0.5 * upward * upward) * ((2.0 * jnp.pi) ** -0.5)
        store_both(S.act.at[layer], i, (upward * cdf).astype(BF))
        store_both(S.gp.at[layer], i, cdf + upward * density)

    def lower_part(layer, i):
        part_send(1, i, dot_nn(load_both(S.act.at[layer], i), flat(S.wd[layer])))

    def after_lower(layer, i):
        at = piece_rows(i)
        total = S.normed[at, :] + part_take(1, i) + param(layer, 2)
        result = norm_piece(total, at, layer, param(layer, 5), param(layer, 7), S.xh2, S.iv2)
        if layer < LAYERS - 1:
            S.stream[at, :] = result
            spread_start(1, i, S.xf.at[layer + 1], result.astype(BF))
        else:
            S.back[0, at, :] = result.astype(BF)

    def next_project(layer, i):
        spread_wait(1, i, S.xf.at[layer])
        project(layer, i)

    def scatter_out(which, source):
        for k in range(2):
            stays = (2 * c + k == z) & (lax.div(z, 2) == c)
            spot = source.at[pl.ds(pl.multiple_of(block * (2 * k + x), block), block)]
            slot = lax.rem(z, 2)

            @pl.when(stays)
            def _():
                S.land[which, slot] = spot[...]

            @pl.when(jnp.logical_not(stays))
            def _():
                rcopy(
                    spot,
                    S.land.at[which, slot],
                    S.in_s.at[2 + which, k],
                    S.in_r.at[2 + which, slot],
                    dev(2 * c + k, x, y, lax.div(z, 2)),
                ).start()

    def scatter_out_wait(which, source, result):
        for k in range(2):
            spot = source.at[pl.ds(pl.multiple_of(block * (2 * k + x), block), block)]

            @pl.when(jnp.logical_not((2 * c + k == z) & (lax.div(z, 2) == c)))
            def _():
                rcopy(
                    spot, spot, S.in_s.at[2 + which, k], S.in_r.at[2 + which, 0], peer
                ).wait_send()

            @pl.when(jnp.logical_not(own_block(k)))
            def _():
                landed = S.land.at[which, k]
                rcopy(
                    landed, landed, S.in_s.at[2 + which, 0], S.in_r.at[2 + which, k], peer
                ).wait_recv()

        result[...] = S.land[which]

    def out_weights():
        gather_wait(2)
        for layer in range(LAYERS):
            cut = slice(layer * d_rows, (layer + 1) * d_rows)
            parts = [S.wog[t, yy].astype(F32)[cut] for t in range(nz) for yy in range(2)]
            parts.append(jnp.zeros((256 - 2 * nz * d_rows, D), F32))
            S.wo[layer] = jnp.concatenate(parts, axis=0).astype(BF)

    spot = first.at[pl.ds(theirs, half)]
    rcopy(spot, spot, S.ins_s.at[0], S.ins_r.at[0], sibling).wait_recv()
    gather_wait(1)
    for i in range(pieces):
        project(0, i)
    gather_end(2)
    gather_relay(3)
    gather_start(4)
    out_weights()
    pipeline(
        (lambda i: attend(0, i), lambda i: part_pass(0, i)),
        {1: [lambda: gather_end(3)], 2: [lambda: gather_start(5)], 3: [lambda: gather_relay(4)]},
    )
    pipeline((lambda i: after_attention(0, i),))
    part_drain(0)
    gather_start(6)
    gather_start(8)
    gather_end(4)
    gather_wait(3)
    pipeline((lambda i: raise_part(0, i),))
    scatter_in_wait(1, cot, S.ct, block * x)
    gather_relay(5)
    gather_start(7)
    gather_end(5)
    gather_wait(4)
    pipeline((lambda i: lower_part(0, i), lambda i: part_pass(1, i)))
    swap_start(1, S.ct, 0)
    gather_relay(6)
    gather_cross(8)
    gather_wait(5)
    pipeline(
        (lambda i: after_lower(0, i), lambda i: next_project(1, i)),
        {0: [lambda: gather_end(6)]},
    )
    part_drain(1)
    pipeline(
        (lambda i: attend(1, i), lambda i: part_pass(0, i)),
        {1: [lambda: gather_relay(7)], 3: [lambda: gather_end(7)]},
    )
    gather_wait(6)
    pipeline(
        (
            lambda i: after_attention(1, i),
            lambda i: raise_part(1, i),
            lambda i: lower_part(1, i),
            lambda i: part_pass(1, i),
        ),
        {1: [lambda: gather_wait(7), lambda: gather_wait(8)]},
    )
    part_drain(0)
    swap_wait(1, S.ct, 0)


    def add_row(layer, kind, value):
        S.sg[layer, kind : kind + 1, :] += jnp.sum(value, axis=0, keepdims=True)

    def norm_back_piece(grad, at, layer, which):
        scaled = (S.xh1 if which == 0 else S.xh2)[layer, at, :]
        inv = (S.iv1 if which == 0 else S.iv2)[layer, at, 0:1]
        add_row(layer, 2 + which, grad * scaled)
        add_row(layer, 4 + which, grad)
        weighted = grad * param(layer, 4 + which)
        back = (
            weighted
            - jnp.mean(weighted, axis=1, keepdims=True)
            - scaled * jnp.mean(weighted * scaled, axis=1, keepdims=True)
        ) * inv
        return back

    def lower_back(layer, i, grad):
        at = piece_rows(i)
        back = norm_back_piece(grad, at, layer, 1)
        S.normed[at, :] = back
        rounded = back.astype(BF)
        add_row(layer, 1, rounded.astype(F32))
        spread_start(0, i, S.dl, rounded)

    def raise_back(layer, i):
        spread_wait(0, i, S.dl)
        back = dot_nt(load_both(S.dl, i), flat(S.wd[layer])) * load_both(S.gp.at[layer], i)
        rounded = back.astype(BF)
        store_both(S.du, i, rounded)
        add_row(layer, 6, rounded.astype(F32))
        part_send(0, i, dot_nt(rounded, flat(S.wu[layer])))

    grads = (S.gq, S.gu, S.gd, S.go)
    from_y = (S.ryq, S.ryu, None, S.ryo)
    from_z = (S.rzq, S.rzu, None, S.rzo)

    def grad_slab(layer, kind, t, y_at):
        ref = grads[kind]
        return ref.at[layer, t, :, y_at] if kind < 2 else ref.at[layer, t, y_at]

    def z_first(layer, kind):
        return kind == 2 and layer == LAYERS - 1

    def z_slab(layer, kind, t):
        return S.gd.at[layer, t] if z_first(layer, kind) else grad_slab(layer, kind, t, y)

    def y_landing(layer, kind):
        if kind == 2:
            return S.ryl if z_first(layer, kind) else S.ryd
        return from_y[kind].at[layer]

    def z_landing(layer, kind, slot):
        if kind == 2:
            return (S.rzl if z_first(layer, kind) else S.rzd).at[slot]
        return from_z[kind].at[layer, slot]

    def reduce_y_copy(layer, kind):
        ref = grads[kind]
        if z_first(layer, kind):
            source = S.syl
        else:
            source = ref.at[layer, :, :, 1 - y] if kind < 2 else ref.at[layer, :, 1 - y]
        n = 4 * layer + kind
        return rcopy(source, y_landing(layer, kind), S.ry_s.at[n], S.ry_r.at[n], across)

    def reduce_z_copy(layer, kind, t, slot, to):
        n = 4 * layer + kind
        return rcopy(
            z_slab(layer, kind, t),
            z_landing(layer, kind, slot),
            S.rz_s.at[n, t],
            S.rz_r.at[n, slot],
            at_z(to),
        )

    def slab_add(target, other):
        if len(target.shape) == 3:
            for xx in range(2):
                target[xx] = (target[xx].astype(F32) + other[xx].astype(F32)).astype(BF)
        else:
            target[...] = (target[...].astype(F32) + other[...].astype(F32)).astype(BF)

    def reduce_direct(layer, kind):
        @pl.when(outer)
        def _():
            reduce_z_copy(layer, kind, far_in, 2, buddy).start()
            reduce_z_copy(layer, kind, far_out, 3, buddy).start()

        reduce_z_copy(layer, kind, buddy, 0, buddy).start()

    def reduce_start(layer, kind):
        if z_first(layer, kind):
            reduce_direct(layer, kind)
        else:
            reduce_y_copy(layer, kind).start()

    def reduce_first(layer, kind):
        reduce_y_copy(layer, kind).wait_recv()

        def one(t, carry):
            slab_add(grad_slab(layer, kind, t, y), y_landing(layer, kind).at[t])
            return carry

        lax.fori_loop(0, nz, one, 0)
        reduce_direct(layer, kind)

    def reduce_relay(layer, kind):
        @pl.when(inner)
        def _():
            for slot, t in ((2, far_in), (3, far_out)):
                reduce_z_copy(layer, kind, t, slot, buddy).wait_recv()
                slab_add(z_slab(layer, kind, t), z_landing(layer, kind, slot))
                reduce_z_copy(layer, kind, t, 1, t).start()

    def reduce_cross(layer):
        d_out[layer] = S.gd[layer, z, y].astype(F32)
        other = S.gd[layer, z, 1 - y].astype(F32)
        for slot in (0, 1):
            reduce_z_copy(layer, 2, z, slot, buddy).wait_recv()
            d_out[layer] += S.rzl[slot, y].astype(F32)
            other = other + S.rzl[slot, 1 - y].astype(F32)
        S.syl[...] = other.astype(BF)
        reduce_y_copy(layer, 2).start()

    def reduce_last_d(layer):
        reduce_y_copy(layer, 2).wait_recv()
        d_out[layer] += S.ryl[...].astype(F32)

    final = (S.fq, S.fu, d_out, S.fo)

    def reduce_last(layer, kind):
        if kind == 3:
            target = S.fo.at[layer]
            cut = lambda value: value[0:d_rows]
        else:
            target = final[kind].at[layer]
            cut = lambda value: value
        target[...] = cut(grad_slab(layer, kind, z, y)[...].astype(F32))

        for slot in (0, 1):
            reduce_z_copy(layer, kind, z, slot, buddy).wait_recv()
            target[...] += cut(z_landing(layer, kind, slot)[...].astype(F32))

        if kind < 2:
            result = (S.oq, S.ou)[kind]
            for r in (1, 2, 0):
                hand_copy(layer, kind, r).start()
            for xx in range(2):
                for cc in range(2):

                    @pl.when((x == xx) & (c == cc))
                    def _():
                        result[layer, 2 * xx + cc] = target[xx, cc * d_rows : (cc + 1) * d_rows, :]

        if kind == 3:
            @pl.when(owner_stays)
            def _():
                S.oo[layer] = target[...]

            @pl.when(jnp.logical_not(owner_stays))
            def _():
                owner_copy(layer).start()

    def hand_copy(layer, kind, r):
        x_r, c_r = relation[r]
        source = (S.fq, S.fu)[kind].at[
            layer, x_r, pl.ds(pl.multiple_of(c_r * d_rows, 8), d_rows)
        ]
        target = (S.oq, S.ou)[kind].at[layer, m]
        return rcopy(
            source,
            target,
            S.fin_s.at[layer, kind, r],
            S.fin_r.at[layer, kind, r],
            dev(z, x_r, y, c_r),
        )

    owner_to = dev(2 * x + c, lax.div(z, 2), lax.rem(z, 2), y)
    owner_stays = (2 * x + c == z) & (lax.div(z, 2) == x) & (lax.rem(z, 2) == y) & (y == c)

    def owner_copy(layer):
        return rcopy(
            S.fo.at[layer], S.oo.at[layer], S.fino.at[layer, 0], S.fino.at[layer, 1], owner_to
        )

    def reduce_drain(layer, kind):
        reduce_y_copy(layer, kind).wait_send()
        for t in range(nz):

            @pl.when(z != t)
            def _():
                reduce_z_copy(layer, kind, t, 0, buddy).wait_send()

        if kind < 2:
            for r in range(3):
                hand_copy(layer, kind, r).wait_send()
        if kind == 3:
            @pl.when(jnp.logical_not(owner_stays))
            def _():
                owner_copy(layer).wait_send()
                owner_copy(layer).wait_recv()

    def lower_grad(layer):
        for i in range(2):
            value = dot_tn(S.act[layer, :, i * (ff // 2) : (i + 1) * (ff // 2)], S.dl[...])
            S.gd[layer, i * (nz // 2) : (i + 1) * (nz // 2)] = value.astype(BF).reshape(
                nz // 2, 2, f_rows, D
            )
        reduce_start(layer, 2)

    def raise_grad(layer):
        for i in range(2):
            value = dot_tn(S.nl[layer, :, i * (D // 2) : (i + 1) * (D // 2)], S.du[...])
            S.gu[layer, i * (nz // 2) : (i + 1) * (nz // 2)] = value.astype(BF).reshape(
                nz // 2, 2, 2, two, ff
            )
        reduce_start(layer, 1)

    def out_grad(layer):
        value = dot_tn(S.mixl[layer], S.db[...])
        empty = jnp.zeros((32 - d_rows, D), F32)
        for t in range(nz):
            for yy in range(2):
                at = (2 * t + yy) * d_rows
                S.go[layer, t, yy] = jnp.concatenate(
                    [value[at : at + d_rows], empty], axis=0
                ).astype(BF)
        reduce_start(layer, 3)

    def project_grad(layer):
        for i in range(2):
            value = dot_tn(S.xf[layer, :, i * (D // 2) : (i + 1) * (D // 2)], S.dq[...])
            S.gq[layer, i * (nz // 2) : (i + 1) * (nz // 2)] = value.astype(BF).reshape(
                nz // 2, 2, 2, two, PACK
            )
        reduce_start(layer, 0)

    def branch_back(layer, i):
        at = piece_rows(i)
        back = norm_back_piece(part_take(0, i) + S.normed[at, :], at, layer, 0)
        S.stream[at, :] = back
        rounded = back.astype(BF)
        add_row(layer, 0, rounded.astype(F32))
        spread_start(1, i, S.db, rounded)

    scale = HEAD_DIM**-0.5

    def attend_back(layer, i):
        spread_wait(1, i, S.db)
        grad_mix = dot_nt(load_both(S.db, i), S.wo[layer]).astype(BF)
        store_both(S.dm, i, grad_mix)
        mix = load_both(S.mix.at[layer], i)
        results = []
        for h in range(LOCAL_HEADS):
            keep = jnp.logical_not(lane_low) if h == 1 else lane_low
            cols = slice(0, 128) if h < 2 else slice(128, 256)
            grad = jnp.where(keep, grad_mix[:, cols], jnp.zeros((), BF))
            delta = jnp.sum(grad.astype(F32) * mix[:, cols], axis=1, keepdims=True)
            grad_weights = dot_nt(grad, head_values(layer, h))
            weights = load_both(S.prob.at[layer, h], i).astype(F32)
            rounded = (weights * (grad_weights - delta)).astype(BF)
            store_both(S.ds.at[h], i, rounded)
            results.append((dot_nn(rounded, head_keys(layer, h)) * scale).astype(BF))
        store_both(S.dq, i, jnp.where(lane_low, results[0], results[1]), slice(0, 128))
        store_both(S.dq, i, results[2], slice(384, 512))

    def attend_back_end(layer):
        keys_back, values_back = [], []
        for h in range(LOCAL_HEADS):
            cols = slice(0, 128) if h < 2 else slice(128, 256)
            queries = mask_queries(S.qkv[layer, :, query_cols(h)], h)
            keys_back.append(dot_tn(S.ds[h], queries).astype(BF))
            values_back.append(dot_tn(S.prob[layer, h], S.dm[:, cols]).astype(BF))
        S.dq[:, 128:256] = jnp.where(lane_low, keys_back[0], keys_back[1])
        S.dq[:, 256:384] = jnp.where(lane_low, values_back[0], values_back[1])
        S.dq[:, 384:512] = jnp.where(lane_low, S.dq[:, 384:512], swap_lanes(keys_back[2]))
        S.dq[:, 512:640] = jnp.where(lane_low, values_back[2], jnp.zeros((), BF))
        S.sg[layer, 7:8, 0:PACK] = jnp.sum(S.dq[...].astype(F32), axis=0, keepdims=True)

    def project_back(layer, i):
        part_send(1, i, dot_nt(load_both(S.dq, i), flat(S.wq[layer])))

    def next_back(layer, i):
        at = piece_rows(i)
        grad = part_take(1, i) + S.stream[at, :]
        if layer > 0:
            lower_back(layer - 1, i, grad)
        else:
            S.back[1, at, :] = grad.astype(BF)

    def small_y(layer):
        return rcopy(S.sg.at[layer], S.sgy.at[layer], S.sgy_s.at[layer], S.sgy_r.at[layer], across)

    def small_z(layer, k):
        to = dev(lax.rem(z + k, nz), x, y, c)
        return rcopy(
            S.sgt.at[layer], S.sgz.at[layer, k], S.sgz_s.at[layer, k], S.sgz_r.at[layer, k], to
        )

    def small_member(layer, r):
        x_r, c_r = relation[r]
        return rcopy(
            S.sgt.at[layer],
            S.sga.at[layer, m],
            S.sga_s.at[layer, r],
            S.sga_r.at[layer, r],
            dev(z, x_r, y, c_r),
        )

    def small_one(layer):
        small_y(layer).start()

    def small_two(layer):
        small_y(layer).wait_recv()
        S.sgt[layer] = S.sg[layer] + S.sgy[layer]
        for k in range(1, nz):
            small_z(layer, k).start()

    def small_three(layer):
        for k in range(1, nz):
            small_z(layer, k).wait_recv()
        for k in range(1, nz):
            small_z(layer, k).wait_send()
        total = S.sgt[layer]
        for k in range(1, nz):
            total = total + S.sgz[layer, k]
        S.sgt[layer] = total
        for r in range(3):
            small_member(layer, r).start()
        S.sga[layer, m] = total

    def small_four(layer):
        for r in range(3):
            small_member(layer, r).wait_send()
            small_member(layer, r).wait_recv()
        small_y(layer).wait_send()
        lane = lax.broadcasted_iota(jnp.int32, (D, 128), 1)
        col = lax.broadcasted_iota(jnp.int32, (D, 128), 0)
        narrow = lane < d_rows
        pick = jnp.where((col == d_rows * d + lane) & narrow, 1.0, 0.0)
        both = S.sga[layer, 2 * x] + S.sga[layer, 2 * x + 1]
        found = dot_exact(both, pick)[:, 0:d_rows]
        g_biases[1, layer : layer + 1, :] = found[0:1]
        g_biases[2, layer : layer + 1, :] = found[1:2]
        g_gains[layer] = found[2:4]
        g_shifts[layer] = found[4:6]
        dim, is_query, is_value = packed_lanes((D, 128), 0)
        hit = (dim == d_rows * (d - 8 * z) + lane) & narrow
        attn = S.sga[layer, z]
        found = dot_exact(attn, jnp.where(hit & is_query, 1.0, 0.0))
        g_biases[0, layer : layer + 1, :] = found[7:8, 0:d_rows]
        found = dot_exact(attn, jnp.where(hit & is_value, 1.0, 0.0))
        g_value[layer : layer + 1, :] = found[7:8, 0:d_rows]
        pick = jnp.where((col == f_rows * (2 * z + y) + lane) & (lane < f_rows), 1.0, 0.0)
        found = dot_exact(S.sga[layer, m], pick)
        g_raise[layer : layer + 1, :] = found[6:7, 0:f_rows]

    def hand_wait(layer, kind):
        for r in range(3):
            hand_copy(layer, kind, r).wait_recv()

    def unpack_heads(layer):
        hand_wait(layer, 0)
        for pair in range(2):
            even = [S.oq[layer, 2 * pair, :, 128 * t : 128 * t + 128] for t in range(5)]
            odd = [S.oq[layer, 2 * pair + 1, :, 128 * t : 128 * t + 128] for t in range(5)]
            thirds = (
                (even[3], turn(odd[3])),
                (turn(even[3]), odd[3]),
                (even[4], turn(odd[4])),
            )
            for kind in range(3):
                turned = turn(odd[kind])
                tiles = [
                    even[kind],
                    jnp.where(lane_low, thirds[kind][0], turned),
                    jnp.where(lane_low, turned, thirds[kind][1]),
                ]
                base = 384 * pair
                g_qkv[layer, kind, :, base : base + 384] = jnp.concatenate(tiles, axis=1)

    def unpack_raise(layer):
        hand_wait(layer, 1)
        wide = [S.ou[layer, member] for member in range(MEMBERS)]
        parts = []
        for z_at in range(nz):
            for x_at in range(2):
                for y_at in range(2):
                    for c_at in range(2):
                        at = (2 * z_at + y_at) * f_rows
                        parts.append(wide[2 * x_at + c_at][:, at : at + f_rows])
        g_up[layer] = jnp.concatenate(parts, axis=1)

    S.sg[...] = jnp.zeros_like(S.sg)

    def turn_back(i):
        after_lower(1, i)
        lower_back(1, i, S.ct[piece_rows(i), :].astype(F32))

    pipeline(
        (turn_back, lambda i: raise_back(1, i), lambda i: part_pass(0, i)),
        {4: [lambda: lower_grad(1)]},
    )
    part_drain(1)
    raise_grad(1)
    scatter_out(0, S.back.at[0])
    pipeline((lambda i: branch_back(1, i), lambda i: attend_back(1, i)))
    part_drain(0)
    attend_back_end(1)
    pipeline((lambda i: project_back(1, i), lambda i: part_pass(1, i)))
    small_one(1)
    project_grad(1)
    out_grad(1)
    reduce_first(1, 1)
    pipeline(
        (
            lambda i: next_back(1, i),
            lambda i: raise_back(0, i),
            lambda i: part_pass(0, i),
        ),
        {1: [lambda: reduce_relay(1, 2)], 4: [lambda: lower_grad(0)]},
    )
    part_drain(1)
    reduce_first(1, 0)
    raise_grad(0)
    pipeline(
        (lambda i: branch_back(0, i), lambda i: attend_back(0, i)),
        {1: [lambda: reduce_relay(1, 1)], 3: [lambda: reduce_first(1, 3)]},
    )
    part_drain(0)
    attend_back_end(0)
    reduce_cross(1)
    small_one(0)
    pipeline((lambda i: project_back(0, i), lambda i: part_pass(1, i)))
    project_grad(0)
    out_grad(0)
    reduce_relay(1, 0)
    small_two(1)
    pipeline((lambda i: next_back(0, i),), {1: [lambda: reduce_relay(1, 3)]})
    part_drain(1)
    scatter_out(1, S.back.at[1])
    reduce_first(0, 2)
    small_three(1)
    reduce_last(1, 1)
    reduce_last(1, 0)
    reduce_first(0, 1)
    reduce_relay(0, 2)
    reduce_last(1, 3)
    small_two(0)
    reduce_last_d(1)
    small_four(1)
    reduce_first(0, 0)
    reduce_relay(0, 1)
    small_three(0)
    reduce_first(0, 3)
    reduce_last(0, 2)
    reduce_relay(0, 0)
    reduce_last(0, 1)
    reduce_relay(0, 3)
    small_four(0)
    unpack_heads(1)
    unpack_raise(1)
    reduce_last(0, 0)
    reduce_last(0, 3)

    for kind in range(3):
        for r in range(3):
            stage_copy(kind, r).wait_send()
    scatter_in_drain(0, inp, first)
    scatter_in_drain(1, cot, S.ct)

    @pl.when(jnp.logical_not(perm_stays))
    def _():
        perm_copy.wait_send()

    spot = first.at[pl.ds(mine, half)]
    rcopy(spot, spot, S.ins_s.at[0], S.ins_r.at[0], sibling).wait_send()
    for cls in range(9):
        gather_drain(cls)
    scatter_out_wait(0, S.back.at[0], out)
    scatter_out_wait(1, S.back.at[1], gin)
    for layer in range(LAYERS):
        for kind in range(4):
            reduce_drain(layer, kind)
    unpack_raise(0)
    unpack_heads(0)
    o_out[...] = S.oo[...]


def hand_over(*refs):
    for n in range(11):
        refs[n + 11][...] = refs[n][...]


def grouped(nz, ny):
    def run(inputs, w_qkv, w_out, w_up, w_down, biases, value_bias, up_bias, gains, shifts, cotangent):
        block = inputs.shape[1]
        d_rows = w_out.shape[1]
        f_rows = w_down.shape[1]
        rows = 2 * nz * block
        half = rows // 2
        layout = scratch_layout(nz, ny, rows, half, d_rows, f_rows)
        vmem = pl.BlockSpec(memory_space=pltpu.VMEM)
        weights = (w_qkv, w_out, w_up, w_down, biases.transpose(1, 0, 2), value_bias, up_bias, gains, shifts)
        shapes = [jax.ShapeDtypeStruct(inputs.shape, BF)] * 2
        shapes += [jax.ShapeDtypeStruct(array.shape, F32) for array in weights]
        results = pl.pallas_call(
            functools.partial(group_kernel, layout, nz),
            out_shape=tuple(shapes),
            in_specs=[vmem] * 11,
            out_specs=[vmem] * 11,
            scratch_shapes=list(layout.values()),
            compiler_params=pltpu.CompilerParams(
                collective_id=0, has_side_effects=True, vmem_limit_bytes=KERNEL_VMEM
            ),
        )(inputs, *weights, cotangent)
        handed = pl.pallas_call(
            hand_over,
            out_shape=tuple(shapes),
            in_specs=[vmem] * 11,
            out_specs=[vmem] * 11,
        )(*results)
        return (*handed[:6], handed[6].transpose(1, 0, 2), *handed[7:])

    return run


def part_count(row_count):
    count = 1
    while row_count % count != 0 or row_count // count > 2048:
        count = count + 1
    return count


def exact_gelu(values):
    return jax.nn.gelu(values, approximate=False)


def normalize(values, gain, shift):
    centred = values - jnp.mean(values, axis=1, keepdims=True)
    inv_std = lax.rsqrt(jnp.mean(centred * centred, axis=1, keepdims=True) + 1e-12)
    scaled = centred * inv_std
    return (scaled * gain + shift, scaled, inv_std)


def norm_back(grad, scaled, inv_std, gain):
    weighted = grad * gain
    return (
        weighted
        - jnp.mean(weighted, axis=1, keepdims=True)
        - scaled * jnp.mean(weighted * scaled, axis=1, keepdims=True)
    ) * inv_std


def split_heads(seq_array, count):
    seq_count, width, unused = seq_array.shape
    return seq_array.reshape(seq_count, count, width // count, HEADS, HEAD_DIM).transpose(
        1, 0, 2, 3, 4
    )


def merge_heads(head_array):
    seq_count, unused, row_count, unused_dim = head_array.shape
    return head_array.transpose(0, 2, 1, 3).reshape(seq_count * row_count, HEADS * HEAD_DIM)


def attend_forward(queries, keys, values):
    seq_count, row_count, unused = queries.shape
    factor = HEAD_DIM ** (-0.5)
    query_heads = queries.reshape(seq_count, row_count, HEADS, HEAD_DIM)
    start_state = (
        jnp.full((seq_count, HEADS, row_count), -1e30, jnp.float32),
        jnp.zeros((seq_count, HEADS, row_count), jnp.float32),
        jnp.zeros((seq_count, HEADS, row_count, HEAD_DIM), jnp.float32),
    )
    piece = (
        lax.all_gather(keys, "ctx", axis=1, tiled=True),
        lax.all_gather(values, "ctx", axis=1, tiled=True),
    )
    count = part_count(piece[0].shape[1])

    def attend_advance(inner, parts):
        peak, totals, accum = inner
        key_part, value_part = parts
        scores = (
            jnp.einsum("sthd,skhd->shtk", query_heads, key_part, preferred_element_type=jnp.float32)
            * factor
        )
        new_peak = jnp.maximum(peak, jnp.max(scores, axis=3))
        decay = jnp.exp(peak - new_peak)
        weights = jnp.exp(scores - new_peak[..., None])
        totals = totals * decay + jnp.sum(weights, axis=3)
        accum = accum * decay[..., None] + jnp.einsum(
            "shtk,skhd->shtd",
            weights.astype(jnp.bfloat16),
            value_part,
            preferred_element_type=jnp.float32,
        )
        return ((new_peak, totals, accum), None)

    result, _ = lax.scan(
        attend_advance, start_state, (split_heads(piece[0], count), split_heads(piece[1], count))
    )
    peak, totals, accum = result
    mixed = merge_heads(accum / totals[..., None])
    return (mixed, peak + jnp.log(totals))


def query_fold(queries, grad_mixed, logsum, row_delta, keys, values):
    seq_count, row_count, unused = queries.shape
    factor = HEAD_DIM ** (-0.5)
    query_heads = queries.reshape(seq_count, row_count, HEADS, HEAD_DIM)
    grad_heads = grad_mixed.reshape(seq_count, row_count, HEADS, HEAD_DIM)
    start_state = jnp.zeros((seq_count, HEADS, row_count, HEAD_DIM), jnp.float32)
    piece = (
        lax.all_gather(keys, "ctx", axis=1, tiled=True),
        lax.all_gather(values, "ctx", axis=1, tiled=True),
    )
    count = part_count(piece[0].shape[1])

    def query_advance(totals, parts):
        key_part, value_part = parts
        scores = (
            jnp.einsum("sthd,skhd->shtk", query_heads, key_part, preferred_element_type=jnp.float32)
            * factor
        )
        weights = jnp.exp(scores - logsum[..., None])
        grad_weights = jnp.einsum(
            "sthd,skhd->shtk", grad_heads, value_part, preferred_element_type=jnp.float32
        )
        grad_scores = (weights * (grad_weights - row_delta[..., None])).astype(jnp.bfloat16)
        return (
            totals
            + jnp.einsum(
                "shtk,skhd->shtd", grad_scores, key_part, preferred_element_type=jnp.float32
            )
            * factor,
            None,
        )

    result, _ = lax.scan(
        query_advance, start_state, (split_heads(piece[0], count), split_heads(piece[1], count))
    )
    return result


def key_fold(queries, grad_mixed, keys, values, all_logsum, all_delta):
    seq_count, row_count, unused = keys.shape
    factor = HEAD_DIM ** (-0.5)
    key_heads = keys.reshape(seq_count, row_count, HEADS, HEAD_DIM)
    value_heads = values.reshape(seq_count, row_count, HEADS, HEAD_DIM)
    start_state = (
        jnp.zeros((seq_count, HEADS, row_count, HEAD_DIM), jnp.float32),
        jnp.zeros((seq_count, HEADS, row_count, HEAD_DIM), jnp.float32),
    )
    piece = (
        lax.all_gather(queries, "ctx", axis=1, tiled=True),
        lax.all_gather(grad_mixed, "ctx", axis=1, tiled=True),
    )
    width = piece[0].shape[1]
    count = part_count(width)
    block = width // count
    log_parts = all_logsum.reshape(seq_count, HEADS, count, block).transpose(2, 0, 1, 3)
    delta_parts = all_delta.reshape(seq_count, HEADS, count, block).transpose(2, 0, 1, 3)

    def key_advance(inner, parts):
        grad_keys, grad_values = inner
        query_part, grad_part, log_part, delta_part = parts
        scores = (
            jnp.einsum("sqhd,skhd->shqk", query_part, key_heads, preferred_element_type=jnp.float32)
            * factor
        )
        weights = jnp.exp(scores - log_part[..., None])
        grad_values = grad_values + jnp.einsum(
            "shqk,sqhd->shkd",
            weights.astype(jnp.bfloat16),
            grad_part,
            preferred_element_type=jnp.float32,
        )
        grad_weights = jnp.einsum(
            "sqhd,skhd->shqk", grad_part, value_heads, preferred_element_type=jnp.float32
        )
        grad_scores = (weights * (grad_weights - delta_part[..., None])).astype(jnp.bfloat16)
        grad_keys = (
            grad_keys
            + jnp.einsum(
                "shqk,sqhd->shkd", grad_scores, query_part, preferred_element_type=jnp.float32
            )
            * factor
        )
        return ((grad_keys, grad_values), None)

    result, _ = lax.scan(
        key_advance,
        start_state,
        (split_heads(piece[0], count), split_heads(piece[1], count), log_parts, delta_parts),
    )
    return result


def forward_layer(stream, full, seq_count):
    w_attn, w_mix, w_raise, w_lower, bias_rows, bias_value, bias_raise, gain_rows, shift_rows = full
    total_rows = stream.shape[0]
    rounded = stream.astype(jnp.bfloat16)
    projected = jnp.einsum("td,cde->cte", rounded, w_attn, preferred_element_type=jnp.float32)
    queries = (projected[0] + bias_rows[0].astype(jnp.float32)).astype(jnp.bfloat16)
    keys = projected[1].astype(jnp.bfloat16)
    values = (projected[2] + bias_value.astype(jnp.float32)).astype(jnp.bfloat16)
    seq_shape = (seq_count, total_rows // seq_count, D)
    mixed, logsum = attend_forward(
        queries.reshape(seq_shape), keys.reshape(seq_shape), values.reshape(seq_shape)
    )
    mixed_low = mixed.astype(jnp.bfloat16)
    branch = jnp.dot(mixed_low, w_mix, preferred_element_type=jnp.float32) + bias_rows[1].astype(
        jnp.float32
    )
    normed, scaled_one, inv_one = normalize(
        stream + branch, gain_rows[0].astype(jnp.float32), shift_rows[0].astype(jnp.float32)
    )
    normed_low = normed.astype(jnp.bfloat16)
    upward = jnp.dot(normed_low, w_raise, preferred_element_type=jnp.float32) + bias_raise.astype(
        jnp.float32
    )
    active = exact_gelu(upward).astype(jnp.bfloat16)
    lowered = jnp.dot(active, w_lower, preferred_element_type=jnp.float32) + bias_rows[2].astype(
        jnp.float32
    )
    result, scaled_two, inv_two = normalize(
        normed + lowered, gain_rows[1].astype(jnp.float32), shift_rows[1].astype(jnp.float32)
    )
    states = (
        rounded,
        queries,
        keys,
        values,
        mixed,
        mixed_low,
        logsum,
        scaled_one,
        inv_one,
        normed_low,
        upward,
        active,
        scaled_two,
        inv_two,
    )
    return (result, states)


def backward_layer(grad, full, states, seq_count):
    w_attn, w_mix, w_raise, w_lower, bias_rows, bias_value, bias_raise, gain_rows, shift_rows = full
    (
        rounded,
        queries,
        keys,
        values,
        mixed,
        mixed_low,
        logsum,
        scaled_one,
        inv_one,
        normed_low,
        upward,
        active,
        scaled_two,
        inv_two,
    ) = states
    total_rows = grad.shape[0]
    row_count = total_rows // seq_count
    seq_shape = (seq_count, row_count, D)
    grad_gain_two = jnp.sum(grad * scaled_two, axis=0)
    grad_shift_two = jnp.sum(grad, axis=0)
    grad_resid = norm_back(grad, scaled_two, inv_two, gain_rows[1].astype(jnp.float32))
    grad_lowered = grad_resid.astype(jnp.bfloat16)
    grad_w_lower = jnp.einsum("tf,td->fd", active, grad_lowered, preferred_element_type=jnp.float32)
    grad_active = jnp.einsum("td,fd->tf", grad_lowered, w_lower, preferred_element_type=jnp.float32)
    unused, gelu_back = jax.vjp(exact_gelu, upward)
    grad_upward = gelu_back(grad_active)[0].astype(jnp.bfloat16)
    grad_w_raise = jnp.einsum(
        "td,tf->df", normed_low, grad_upward, preferred_element_type=jnp.float32
    )
    grad_normed = (
        jnp.einsum("tf,df->td", grad_upward, w_raise, preferred_element_type=jnp.float32)
        + grad_resid
    )
    grad_gain_one = jnp.sum(grad_normed * scaled_one, axis=0)
    grad_shift_one = jnp.sum(grad_normed, axis=0)
    grad_inner = norm_back(grad_normed, scaled_one, inv_one, gain_rows[0].astype(jnp.float32))
    grad_branch = grad_inner.astype(jnp.bfloat16)
    grad_w_mix = jnp.einsum("td,te->de", mixed_low, grad_branch, preferred_element_type=jnp.float32)
    grad_mixed = jnp.einsum(
        "te,de->td", grad_branch, w_mix, preferred_element_type=jnp.float32
    ).astype(jnp.bfloat16)
    row_delta = jnp.sum(
        (grad_mixed.astype(jnp.float32) * mixed).reshape(seq_count, row_count, HEADS, HEAD_DIM),
        axis=3,
    ).transpose(0, 2, 1)
    seq_queries = queries.reshape(seq_shape)
    seq_keys = keys.reshape(seq_shape)
    seq_values = values.reshape(seq_shape)
    seq_grad_mixed = grad_mixed.reshape(seq_shape)
    grad_queries = query_fold(seq_queries, seq_grad_mixed, logsum, row_delta, seq_keys, seq_values)
    grad_queries = merge_heads(grad_queries).astype(jnp.bfloat16)
    all_logsum, all_delta = (
        lax.all_gather(logsum, "ctx", axis=2, tiled=True),
        lax.all_gather(row_delta, "ctx", axis=2, tiled=True),
    )
    grad_keys, grad_values = key_fold(
        seq_queries, seq_grad_mixed, seq_keys, seq_values, all_logsum, all_delta
    )
    grad_keys = merge_heads(grad_keys).astype(jnp.bfloat16)
    grad_values = merge_heads(grad_values).astype(jnp.bfloat16)
    grad_project = jnp.stack([grad_queries, grad_keys, grad_values])
    grad_w_attn = jnp.einsum(
        "td,cte->dce", rounded, grad_project, preferred_element_type=jnp.float32
    )
    grad_stream = (
        jnp.einsum("cte,cde->td", grad_project, w_attn, preferred_element_type=jnp.float32)
        + grad_inner
    )
    grad_bias_rows = jnp.stack(
        [
            jnp.sum(grad_queries.astype(jnp.float32), axis=0),
            jnp.sum(grad_branch.astype(jnp.float32), axis=0),
            jnp.sum(grad_lowered.astype(jnp.float32), axis=0),
        ],
        axis=1,
    )
    grad_bias_value = jnp.sum(grad_values.astype(jnp.float32), axis=0)
    grad_bias_raise = jnp.sum(grad_upward.astype(jnp.float32), axis=0)
    local_sums = (
        grad_w_attn,
        grad_w_mix,
        grad_w_raise,
        grad_w_lower,
        grad_bias_rows,
        grad_bias_value,
        grad_bias_raise,
        jnp.stack([grad_gain_one, grad_gain_two], axis=1),
        jnp.stack([grad_shift_one, grad_shift_two], axis=1),
    )
    return (grad_stream, local_sums)


def body(inputs, w_qkv, w_out, w_up, w_down, biases, value_bias, up_bias, gains, shifts, cotangent):
    stacked = (w_qkv, w_out, w_up, w_down, biases, value_bias, up_bias, gains, shifts)
    seq_count = inputs.shape[0]
    stream = inputs.reshape(-1, D).astype(jnp.float32)
    kept_states = []
    for layer in range(LAYERS):
        shards = tuple((array[layer] for array in stacked))
        full = (
            lax.all_gather(shards[0], ("ctx", "fsdp"), axis=1, tiled=True),
            lax.all_gather(shards[1], ("ctx", "fsdp"), axis=0, tiled=True),
            lax.all_gather(shards[2], ("ctx", "fsdp"), axis=0, tiled=True),
            lax.all_gather(shards[3], ("ctx", "fsdp"), axis=0, tiled=True),
            lax.all_gather(shards[4], ("ctx", "fsdp"), axis=1, tiled=True),
            lax.all_gather(shards[5], ("ctx", "fsdp"), axis=0, tiled=True),
            lax.all_gather(shards[6], ("ctx", "fsdp"), axis=0, tiled=True),
            lax.all_gather(shards[7], ("ctx", "fsdp"), axis=1, tiled=True),
            lax.all_gather(shards[8], ("ctx", "fsdp"), axis=1, tiled=True),
        )
        stream, states = forward_layer(stream, full, seq_count)
        kept_states.append(states)
    output = stream.astype(jnp.bfloat16).reshape(inputs.shape)
    grad = cotangent.reshape(-1, D).astype(jnp.float32)
    layer_grads = [None] * LAYERS
    for layer in reversed(range(LAYERS)):
        shards = tuple((array[layer] for array in stacked))
        full = (
            lax.all_gather(shards[0], ("ctx", "fsdp"), axis=1, tiled=True),
            lax.all_gather(shards[1], ("ctx", "fsdp"), axis=0, tiled=True),
            lax.all_gather(shards[2], ("ctx", "fsdp"), axis=0, tiled=True),
            lax.all_gather(shards[3], ("ctx", "fsdp"), axis=0, tiled=True),
            lax.all_gather(shards[4], ("ctx", "fsdp"), axis=1, tiled=True),
            lax.all_gather(shards[5], ("ctx", "fsdp"), axis=0, tiled=True),
            lax.all_gather(shards[6], ("ctx", "fsdp"), axis=0, tiled=True),
            lax.all_gather(shards[7], ("ctx", "fsdp"), axis=1, tiled=True),
            lax.all_gather(shards[8], ("ctx", "fsdp"), axis=1, tiled=True),
        )
        grad, local_sums = backward_layer(grad, full, kept_states[layer], seq_count)
        partial_sums = (
            lax.psum_scatter(local_sums[0], "ctx", scatter_dimension=0, tiled=True),
            lax.psum_scatter(local_sums[1], "ctx", scatter_dimension=0, tiled=True),
            lax.psum_scatter(local_sums[2], "ctx", scatter_dimension=0, tiled=True),
            lax.psum_scatter(local_sums[3], "ctx", scatter_dimension=0, tiled=True),
            lax.psum_scatter(local_sums[4], "ctx", scatter_dimension=0, tiled=True),
            lax.psum_scatter(local_sums[5], "ctx", scatter_dimension=0, tiled=True),
            lax.psum_scatter(local_sums[6], "ctx", scatter_dimension=0, tiled=True),
            lax.psum_scatter(local_sums[7], "ctx", scatter_dimension=0, tiled=True),
            lax.psum_scatter(local_sums[8], "ctx", scatter_dimension=0, tiled=True),
        )
        reduced = (
            lax.psum_scatter(
                partial_sums[0].astype(jnp.bfloat16), "fsdp", scatter_dimension=0, tiled=True
            ).astype(jnp.float32),
            lax.psum_scatter(
                partial_sums[1].astype(jnp.bfloat16), "fsdp", scatter_dimension=0, tiled=True
            ).astype(jnp.float32),
            lax.psum_scatter(
                partial_sums[2].astype(jnp.bfloat16), "fsdp", scatter_dimension=0, tiled=True
            ).astype(jnp.float32),
            lax.psum_scatter(
                partial_sums[3].astype(jnp.bfloat16), "fsdp", scatter_dimension=0, tiled=True
            ).astype(jnp.float32),
            lax.psum_scatter(
                partial_sums[4].astype(jnp.bfloat16), "fsdp", scatter_dimension=0, tiled=True
            ).astype(jnp.float32),
            lax.psum_scatter(
                partial_sums[5].astype(jnp.bfloat16), "fsdp", scatter_dimension=0, tiled=True
            ).astype(jnp.float32),
            lax.psum_scatter(
                partial_sums[6].astype(jnp.bfloat16), "fsdp", scatter_dimension=0, tiled=True
            ).astype(jnp.float32),
            lax.psum_scatter(
                partial_sums[7].astype(jnp.bfloat16), "fsdp", scatter_dimension=0, tiled=True
            ).astype(jnp.float32),
            lax.psum_scatter(
                partial_sums[8].astype(jnp.bfloat16), "fsdp", scatter_dimension=0, tiled=True
            ).astype(jnp.float32),
        )
        layer_grads[layer] = (
            reduced[0].transpose(1, 0, 2),
            reduced[1],
            reduced[2],
            reduced[3],
            reduced[4].T,
            reduced[5],
            reduced[6],
            reduced[7].T,
            reduced[8].T,
        )
    grad_inputs = grad.astype(jnp.bfloat16).reshape(inputs.shape)
    return (
        output,
        grad_inputs,
        jnp.stack([member[0] for member in layer_grads]),
        jnp.stack([member[1] for member in layer_grads]),
        jnp.stack([member[2] for member in layer_grads]),
        jnp.stack([member[3] for member in layer_grads]),
        jnp.stack([member[4] for member in layer_grads]),
        jnp.stack([member[5] for member in layer_grads]),
        jnp.stack([member[6] for member in layer_grads]),
        jnp.stack([member[7] for member in layer_grads]),
        jnp.stack([member[8] for member in layer_grads]),
    )


def one_group_per_sequence(mesh, seqs):
    return mesh.shape["fsdp"] == 4 and mesh.shape["ctx"] == seqs


def solution(mesh):
    def run(*arrays):
        seqs = arrays[0].shape[0]
        chosen = grouped(mesh.shape["ctx"] // 2, 2) if one_group_per_sequence(mesh, seqs) else body
        return on_devices(mesh, chosen)(*arrays)

    return run


def on_devices(mesh, chosen):
    return jax.shard_map(
        chosen,
        mesh=mesh,
        in_specs=(
            P("fsdp", "ctx", None),
            P(None, None, ("ctx", "fsdp"), None),
            P(None, ("ctx", "fsdp"), None),
            P(None, ("ctx", "fsdp"), None),
            P(None, ("ctx", "fsdp"), None),
            P(None, None, ("ctx", "fsdp")),
            P(None, ("ctx", "fsdp")),
            P(None, ("ctx", "fsdp")),
            P(None, None, ("ctx", "fsdp")),
            P(None, None, ("ctx", "fsdp")),
            P("fsdp", "ctx", None),
        ),
        out_specs=(
            P("fsdp", "ctx", None),
            P("fsdp", "ctx", None),
            P(None, None, ("ctx", "fsdp"), None),
            P(None, ("ctx", "fsdp"), None),
            P(None, ("ctx", "fsdp"), None),
            P(None, ("ctx", "fsdp"), None),
            P(None, None, ("ctx", "fsdp")),
            P(None, ("ctx", "fsdp")),
            P(None, ("ctx", "fsdp")),
            P(None, None, ("ctx", "fsdp")),
            P(None, None, ("ctx", "fsdp")),
        ),
        check_vma=False,
    )
```
